32 devices in a mesh: mp: 2 (over x), vocab: 8 (over z, core), rows: 2 (over y).
Axes of the slice: x: 2, y: 2, z: 4, core: 2. Of those that a mesh axis runs over, the one named last changes fastest.
Arguments:
- hidden: bfloat16 [2, 512, 4096], P('mp', None, 'rows')
- norm_gain: bfloat16 [2, 4096], P('mp', 'rows'), may hold values from 0.5 to 1.5
- head_weights: bfloat16 [2, 4096, 12288], P('mp', 'rows', 'vocab')
- pair_source: int32 [32], P('vocab'), may hold values from 0 to 23, as said below
- pair_target: int32 [32], P('vocab'), may hold values from 0 to 23, as said below
- pair_count: int32 [8], P('vocab'), may hold values from 2 to 4, as said below
- pair_weight: bfloat16 [32, 512, 512], P('vocab'), may hold values from 0.00019454956 to 0.00390625
- next_token: int32 [512], P(('mp', 'rows')), may hold values from 0 to 12287
Outputs:
- ensemble_logp: float32 [512, 12288], P(('mp', 'rows'), 'vocab')
- target_nll: float32 [512], P(('mp', 'rows'))
The draws below stay inside these ranges and needn't reach their ends.
Inputs may be any that keep to these rules, and one draw needn't show every extreme that they name: `pair_target`: slot p targets one of the blocks of its own shard, (p // 4) * 3 to (p // 4) * 3 + 2. `pair_source`: slot p's source block lies from (p // 4) * 3 - 3 to (p // 4) * 3 + 2 * 3 - 1; slot 0 of every shard but the first and the last takes the block just below the shard's own, slot 1 of every shard but the last the block just above. The live slots of a shard are its first pair_count ones.
All inputs are finite; a program needn't handle non-finite values.
Results may differ from the reference program's by a relative error of at most 0.0003.
Values may be sent and summed in bfloat16 or wider, within the bound.
No kernel may reach another device: no remote copies, remote signals or barrier semaphores. Data moves between devices by JAX's collectives and lax.ppermute only.
A program may use at most 128 MiB of HBM per device.

```python
import math
import jax
import jax.numpy as jnp
from jax import lax

D = 4096
BLOCK = 512
BLK_DEV = 3
SLOTS = 4
ROWS = 512
SHARDS = 8
VOCAB = 12288
NBLOCKS = 24
PAIRS = 32


def drawn_columns(key):
    aligned = min(8, ROWS)
    return jax.random.randint(jax.random.fold_in(key, 57), (2, aligned, 2), 0, VOCAB)


def raw_column(key, model_index, column):
    column_key = jax.random.fold_in(jax.random.fold_in(key, 31 + model_index), column)
    return jnp.clip(jax.random.normal(column_key, (D,), jnp.float32), -6.0, 6.0)


def head_column(key, model_index, column):
    chosen = drawn_columns(key)[model_index].reshape(-1)
    boost = jnp.where(jnp.any(chosen == column), max(1.5, 80.0 / math.sqrt(D)), 1.0)
    return raw_column(key, model_index, column) * (3.5 / math.sqrt(D)) * boost


def draw_head_weights(key, part):
    columns = jnp.arange(VOCAB, dtype=jnp.int32)
    llama_head = jax.vmap(lambda column: head_column(key, 0, column))(columns).T
    qwen_head = jax.vmap(lambda column: head_column(key, 1, column))(columns).T
    return jnp.stack([llama_head, qwen_head]).astype(jnp.bfloat16)


def draw_hidden(key, part):
    base_key = key
    key = jax.random.fold_in(key, 7)
    samples = jnp.clip(jax.random.normal(key, (2, ROWS, D), jnp.float32), -6.0, 6.0)
    aligned = min(8, ROWS)
    chosen = drawn_columns(base_key)
    strength = 1.0 - 0.05 * jnp.arange(aligned, dtype=jnp.float32)
    second = jnp.where(jnp.arange(aligned) % 2 == 0, 0.0, 1.0)
    for model_index in range(2):
        first_dir = jax.vmap(lambda column: raw_column(base_key, model_index, column))(chosen[model_index, :, 0])
        second_dir = jax.vmap(lambda column: raw_column(base_key, model_index, column))(chosen[model_index, :, 1])
        direction = first_dir + second[:, None] * second_dir
        rows_scale = jnp.sqrt(jnp.mean(samples[model_index, :aligned] ** 2, axis=1, keepdims=True))
        rows_new = strength[:, None] * direction * rows_scale + (1.0 - strength[:, None]) * samples[model_index, :aligned]
        samples = samples.at[model_index, :aligned].set(rows_new)
    return samples.astype(jnp.bfloat16)


def pair_lists(key):
    key = jax.random.fold_in(key, 101)
    sub_keys = jax.random.split(key, 5)
    device_index = jnp.arange(PAIRS, dtype=jnp.int32) // SLOTS
    slot_index = jnp.arange(PAIRS, dtype=jnp.int32) % SLOTS
    target = device_index * BLK_DEV + jax.random.randint(sub_keys[0], (PAIRS,), 0, BLK_DEV)
    lower_bound = jnp.maximum(device_index * BLK_DEV - BLK_DEV, 0)
    upper_bound = jnp.minimum(device_index * BLK_DEV + 2 * BLK_DEV, NBLOCKS)
    source = jax.random.randint(sub_keys[1], (PAIRS,), lower_bound, upper_bound)
    below = jnp.maximum(device_index * BLK_DEV - 1, 0)
    above = jnp.minimum(device_index * BLK_DEV + BLK_DEV, NBLOCKS - 1)
    source = jnp.where(slot_index == 0, below, jnp.where(slot_index == 1, above, source))
    first_slot = (device_index == 0) & (slot_index == 0)
    last_slot = (device_index == SHARDS - 1) & (slot_index == 0)
    source = jnp.where(first_slot, 0, jnp.where(last_slot, NBLOCKS - 1, source))
    target = jnp.where(first_slot, 0, jnp.where(last_slot, NBLOCKS - 1, target))
    counts = jax.random.randint(sub_keys[2], (SHARDS,), 2, SLOTS + 1)
    busiest = jax.random.randint(sub_keys[3], (), 0, SHARDS)
    lightest = (busiest + 1 + jax.random.randint(sub_keys[4], (), 0, SHARDS - 1)) % SHARDS
    shard_index = jnp.arange(SHARDS, dtype=jnp.int32)
    counts = jnp.where(shard_index == busiest, SLOTS, jnp.where(shard_index == lightest, 2, counts))
    return (source.astype(jnp.int32), target.astype(jnp.int32), counts.astype(jnp.int32))


def draw_pair_source(key, part):
    return pair_lists(key)[0]


def draw_pair_target(key, part):
    return pair_lists(key)[1]


def draw_pair_count(key, part):
    return pair_lists(key)[2]


def place_ends(values, stream_key, least, top_value):
    dims = values.shape
    spot = [jax.random.randint(jax.random.fold_in(stream_key, axis), (), 0, dims[axis]) for axis in range(len(dims))]
    values = values.at[tuple(spot)].set(least)
    longest = dims.index(max(dims))
    spot[longest] = (spot[longest] + 1) % dims[longest]
    return values.at[tuple(spot)].set(top_value)


def level_of(rng, dims, cuts, least, top_value):
    gain, own = 1.0, jax.random.fold_in(rng, 6)
    for axis_at, blocks in cuts:
        steps = jnp.exp(jax.random.uniform(jax.random.fold_in(own, axis_at), (blocks,), jnp.float32, least / len(cuts), top_value / len(cuts)))
        gain = gain * jnp.repeat(steps, dims[axis_at] // blocks).reshape([-1 if axis == axis_at else 1 for axis in range(len(dims))])
    return gain


def setup_inputs(seed: int = 0) -> dict:
    arg_keys = jax.random.split(jax.random.key(seed), 9)
    return {
        "hidden": draw_hidden(jax.random.fold_in(arg_keys[8], 71), 0),
        "norm_gain": jnp.clip(1.0 + 0.1 * jax.random.normal(arg_keys[1], (2, D), jnp.float32), 0.5, 1.5).astype(jnp.bfloat16),
        "head_weights": draw_head_weights(jax.random.fold_in(arg_keys[8], 71), 0),
        "pair_source": draw_pair_source(jax.random.fold_in(arg_keys[8], 71), 0),
        "pair_target": draw_pair_target(jax.random.fold_in(arg_keys[8], 71), 0),
        "pair_count": draw_pair_count(jax.random.fold_in(arg_keys[8], 71), 0),
        "pair_weight": jnp.clip(0.00019454956 + 0.0037117004 * jax.random.uniform(arg_keys[6], (PAIRS, BLOCK, BLOCK), jnp.float32) ** level_of(arg_keys[6], (PAIRS, BLOCK, BLOCK), ((0, 8),), -0.2, 0.2), 0.00019454956, 0.00390625).astype(jnp.bfloat16),
        "next_token": place_ends(jax.random.randint(arg_keys[7], (ROWS,), 0, VOCAB), jax.random.fold_in(arg_keys[7], 1), 0, VOCAB - 1).astype(jnp.int32),
    }


def reference(hidden, norm_gain, head_weights, pair_source, pair_target, pair_count, pair_weight, next_token):
    values = hidden.astype(jnp.float32)
    scale = lax.rsqrt(lax.optimization_barrier(jnp.mean(values * values, axis=2, keepdims=True)) + 1e-05)
    normed = values * scale * norm_gain.astype(jnp.float32)[:, None, :]
    llama_logits = jnp.dot(normed[0], head_weights[0].astype(jnp.float32), preferred_element_type=jnp.float32, precision=lax.Precision.HIGHEST)
    qwen_logits = jnp.dot(normed[1], head_weights[1].astype(jnp.float32), preferred_element_type=jnp.float32, precision=lax.Precision.HIGHEST)
    llama_peak = lax.optimization_barrier(jnp.max(llama_logits, axis=1, keepdims=True))
    llama_total = lax.optimization_barrier(jnp.sum(jnp.exp(llama_logits - llama_peak), axis=1, keepdims=True))
    llama_logp = llama_logits - llama_peak - jnp.log(llama_total)
    qwen_peak = lax.optimization_barrier(jnp.max(qwen_logits, axis=1, keepdims=True))
    qwen_total = lax.optimization_barrier(jnp.sum(jnp.exp(qwen_logits - qwen_peak), axis=1, keepdims=True))
    qwen_prob = (jnp.exp(qwen_logits - qwen_peak) / qwen_total).astype(jnp.bfloat16)
    blocks = qwen_prob.reshape(ROWS, NBLOCKS, BLOCK)
    picked_blocks = jnp.take(blocks, pair_source, axis=1).astype(jnp.float32)
    contribution = jnp.einsum('rpk,pkn->prn', picked_blocks, pair_weight.astype(jnp.float32), precision=lax.Precision.HIGHEST)
    slot_index = jnp.arange(PAIRS, dtype=jnp.int32) % SLOTS
    owner_index = jnp.arange(PAIRS, dtype=jnp.int32) // SLOTS
    live_slot = slot_index < pair_count[owner_index]
    selector = ((pair_target[:, None] == jnp.arange(NBLOCKS, dtype=jnp.int32)[None, :]) & live_slot[:, None]).astype(jnp.float32)
    mapped = jnp.einsum('prn,pb->rbn', contribution, selector, precision=lax.Precision.HIGHEST).reshape(ROWS, VOCAB)
    mixed = jnp.logaddexp(jnp.maximum(llama_logp, -50.0), jnp.log(mapped))
    log_norm = jnp.log1p(lax.optimization_barrier(jnp.sum(mapped, axis=1)))
    ensemble = mixed - log_norm[:, None]
    picked = jnp.take_along_axis(mixed, next_token[:, None], axis=1)[:, 0]
    return (ensemble, log_norm - picked)
```

```python
import functools

import jax
import jax.numpy as jnp
from jax import lax
from jax.experimental import pallas as pl
from jax.experimental.pallas import tpu as pltpu
from jax.sharding import PartitionSpec as P

LANES = 128
EXTRA = 16
CODE = 512
HEAD_COPIES = 4
TOP = 32767.0
LEAST = 1e-30
FLOOR = 1.9287498479639178e-22
VMEM = 16 * 1024 * 1024

f32, bf16, i32, i16 = jnp.float32, jnp.bfloat16, jnp.int32, jnp.int16


def params():
    return pltpu.CompilerParams(vmem_limit_bytes=VMEM)


def exponent(value):
    return jnp.ceil(jnp.log2(jnp.maximum(value, LEAST)))


def columns_to_lanes(values, rows):
    lanes = lax.broadcasted_iota(i32, (rows, LANES), 1)
    out = jnp.zeros((rows, LANES), f32)
    for place, value in enumerate(values):
        out = jnp.where(lanes == place, value, out)
    return out


def split_exact(gained):
    high = gained.astype(bf16)
    return high, (gained - high.astype(f32)).astype(bf16)


def encode(values, power):
    size = jnp.sqrt(jnp.abs(values) * jnp.exp2(-power)) * TOP
    code = jnp.minimum(size + 0.5, TOP).astype(i32)
    return jnp.where(values < 0, -code, code).astype(i16)


def decode(codes, power):
    wide = codes.astype(i32).astype(f32)
    return wide * jnp.abs(wide) * (jnp.exp2(power) * (1.0 / (TOP * TOP)))


def encode_scalar(value):
    power = exponent(value)
    mantissa = jnp.maximum(value, LEAST) * jnp.exp2(-power) * 16384.0
    first = jnp.floor(mantissa)
    return power, first, jnp.floor((mantissa - first) * 16384.0)


def decode_scalar(power, first, second):
    return (first + second * (1.0 / 16384.0)) * (1.0 / 16384.0) * jnp.exp2(power)


def prepare(hidden, gain, left_ref, at):
    rows = hidden.shape[0]
    values = hidden.astype(f32)
    high, low = split_exact(values * gain)
    left_ref[pl.ds(at, rows), :] = high
    left_ref[pl.ds(at + rows, rows), :] = low
    return jnp.sum(values * values, axis=1, keepdims=True)


def put_codes(out_ref, both, first):
    rows = both.shape[0] // 2
    part = both[:rows] + both[rows:]
    power = exponent(jnp.max(jnp.abs(part), axis=1, keepdims=True))
    codes = encode(part, power)
    for k in range(part.shape[1] // LANES):
        out_ref[pl.ds((first // LANES + k) * rows, rows), :] = codes[:, k * LANES : (k + 1) * LANES]
    return power


def put_extra(out_ref, powers, squares):
    rows = squares.shape[0]
    extra = columns_to_lanes(powers + list(encode_scalar(squares)), rows)
    body = out_ref.shape[0] - EXTRA
    out_ref[pl.ds(body, EXTRA), :] = jnp.transpose(extra)[:EXTRA].astype(i32).astype(i16)


def first_kernel(kinds, rows, quarter_ref, hidden_ref, gain_ref, head_ref, *refs):
    count = len(kinds)
    left_refs, square_refs, head_out = refs[:count], refs[count : 2 * count], refs[2 * count]
    held, gain_held, sems, gain_sem, head_sems = refs[2 * count + 1 :]
    copies = []
    for place, which in enumerate(kinds):
        at = pl.ds(pl.multiple_of(quarter_ref[which] * rows, rows), rows)
        copies.append(pltpu.make_async_copy(hidden_ref.at[at, :], held.at[place], sems.at[place]))
    gain_copy = pltpu.make_async_copy(gain_ref, gain_held, gain_sem)
    deep = head_ref.shape[0] // HEAD_COPIES
    spans = [pl.ds(k * deep, deep) for k in range(HEAD_COPIES)]
    head_copies = [
        pltpu.make_async_copy(head_ref.at[at, :], head_out.at[at, :], head_sems.at[k])
        for k, at in enumerate(spans)
    ]
    gain_copy.start()
    for copy in copies + head_copies:
        copy.start()
    gain_copy.wait()
    gain = gain_held[...].astype(f32)
    for place, copy in enumerate(copies):
        copy.wait()
        squares = prepare(held[place], gain, left_refs[place], 0)
        square_refs[place][...] = jnp.broadcast_to(squares, (rows, LANES))
    for copy in head_copies:
        copy.wait()


def first_prep(quarters, hidden, gain, head, kinds):
    rows, feats, count = hidden.shape[0] // 4, hidden.shape[1], len(kinds)
    hbm = pl.BlockSpec(memory_space=pltpu.HBM)
    outs = pl.pallas_call(
        functools.partial(first_kernel, kinds, rows),
        in_specs=[pl.BlockSpec(memory_space=pltpu.SMEM), hbm, hbm, hbm],
        out_shape=[jax.ShapeDtypeStruct((2 * rows, feats), bf16)] * count
        + [jax.ShapeDtypeStruct((rows, LANES), f32)] * count
        + [jax.ShapeDtypeStruct(head.shape, head.dtype)],
        scratch_shapes=[
            pltpu.VMEM((count, rows, feats), bf16),
            pltpu.VMEM(gain.shape, bf16),
            pltpu.SemaphoreType.DMA((count,)),
            pltpu.SemaphoreType.DMA,
            pltpu.SemaphoreType.DMA((HEAD_COPIES,)),
        ],
        compiler_params=params(),
        cost_estimate=pl.CostEstimate(
            flops=8 * count * rows * feats, bytes_accessed=2 * head.size, transcendentals=0
        ),
        name="first_prep",
    )(quarters, hidden, gain, head)
    return outs[:count], outs[count : 2 * count], outs[2 * count]


def encode_kernel(count, both_ref, *refs):
    square_refs, outs = refs[:count], refs[count:]
    rows, cols = both_ref.shape[0] // count // 2, both_ref.shape[1]
    for place, out_ref in enumerate(outs):
        powers = []
        for first in range(0, cols, CODE):
            both = both_ref[pl.ds(2 * place * rows, 2 * rows), pl.ds(first, CODE)]
            powers.append(put_codes(out_ref, both, first))
        put_extra(out_ref, powers, square_refs[place][:, :1])


def encode_parts(both, squares):
    count = len(squares)
    rows, cols = both.shape[0] // count // 2, both.shape[1]
    return pl.pallas_call(
        functools.partial(encode_kernel, count),
        out_shape=[jax.ShapeDtypeStruct((cols // LANES * rows + EXTRA, LANES), i16)] * count,
        compiler_params=params(),
        cost_estimate=pl.CostEstimate(
            flops=20 * count * rows * cols, bytes_accessed=10 * count * rows * cols, transcendentals=count * rows * cols
        ),
        name="encode_parts",
    )(both, *squares)


def product(left, head):
    return jnp.dot(left, head, preferred_element_type=f32)


def side_kernel(width, blocks, own_which, meta_ref, quarter_ref, token_ref, hidden_ref, gain_ref, w_ref, near_ref, own_ref, far_ref, left_ref, squares_ref, held, gain_held, w_held, sum_ref, sem, gain_sem, w_sems):
    rows = token_ref.shape[1]
    slots = w_ref.shape[0]
    at = pl.ds(pl.multiple_of(quarter_ref[own_which] * rows, rows), rows)
    hidden_copy = pltpu.make_async_copy(hidden_ref.at[at, :], held, sem)
    gain_copy = pltpu.make_async_copy(gain_ref, gain_held, gain_sem)
    w_copies = [pltpu.make_async_copy(w_ref.at[k], w_held.at[k], w_sems.at[k]) for k in range(slots)]
    gain_copy.start()
    hidden_copy.start()
    for copy in w_copies:
        copy.start()
    shard = meta_ref[1]
    near_at = jnp.where(shard % 2 == 0, 2, 0)
    token = jnp.transpose(jnp.broadcast_to(token_ref[...].astype(f32), (8, rows)))[:, :1].astype(i32)
    place = lax.broadcasted_iota(i32, (rows, width), 1)
    sum_ref[...] = jnp.zeros_like(sum_ref)
    gain_copy.wait()
    hidden_copy.wait()
    squares = prepare(held[...], gain_held[...].astype(f32), left_ref, 0)
    squares_ref[...] = jnp.broadcast_to(squares, (rows, LANES))
    for slot in range(slots):
        w_copies[slot].wait()

        @pl.when(slot < meta_ref[2 + 2 * slots])
        def _():
            source = jnp.clip(meta_ref[2 + slot] - (shard - 1) * blocks, 0, 3 * blocks - 1)
            hits = (token - meta_ref[2 + slots + slot] * width == place).astype(bf16)
            left = jnp.concatenate([hits, jnp.ones((EXTRA, width), bf16)], axis=0)
            found = lax.dot_general(
                left, w_held[slot], (((1,), (1,)), ((), ())), preferred_element_type=f32
            )
            at = pl.ds(pl.multiple_of(source % blocks * width, width), width)
            sum_ref[source // blocks, :, at] += found

    order = lax.broadcasted_iota(i32, (EXTRA, 1), 0)
    for out_ref, k in ((near_ref, near_at), (own_ref, 1), (far_ref, 2 - near_at)):
        out_ref[pl.ds(0, rows), :] = sum_ref[k, pl.ds(0, rows), :].astype(bf16)
        sums = sum_ref[k, pl.ds(rows, EXTRA), :]
        first = sums.astype(bf16).astype(f32)
        second = (sums - first).astype(bf16).astype(f32)
        third = sums - first - second
        parts = jnp.where(order == 0, first, jnp.where(order == 1, second, jnp.where(order == 2, third, 0.0)))
        out_ref[pl.ds(rows, EXTRA), :] = parts.astype(bf16)


def side_parts(meta, quarters, token, hidden, gain, weights, width, cols):
    rows, feats = token.shape[1], hidden.shape[1]
    smem = pl.BlockSpec(memory_space=pltpu.SMEM)
    hbm = pl.BlockSpec(memory_space=pltpu.HBM)
    outs = pl.pallas_call(
        functools.partial(side_kernel, width, cols // width, 0),
        in_specs=[smem, smem, pl.BlockSpec(memory_space=pltpu.VMEM), hbm, hbm, hbm],
        out_shape=[jax.ShapeDtypeStruct((rows + EXTRA, cols), bf16)] * 3
        + [jax.ShapeDtypeStruct((2 * rows, feats), bf16), jax.ShapeDtypeStruct((rows, LANES), f32)],
        scratch_shapes=[
            pltpu.VMEM((rows, feats), bf16),
            pltpu.VMEM(gain.shape, bf16),
            pltpu.VMEM(weights.shape, bf16),
            pltpu.VMEM((3, rows + EXTRA, cols), f32),
            pltpu.SemaphoreType.DMA,
            pltpu.SemaphoreType.DMA,
            pltpu.SemaphoreType.DMA((weights.shape[0],)),
        ],
        compiler_params=params(),
        cost_estimate=pl.CostEstimate(flops=1, bytes_accessed=1, transcendentals=0),
        name="side_parts",
    )(meta, quarters, token, hidden, gain, weights)
    return outs[:3], outs[3], outs[4]


def extras(ref, rows):
    tile = ref[pl.ds(ref.shape[0] - EXTRA, EXTRA), :].astype(i32).astype(f32)
    wide = jnp.transpose(tile)
    groups = (ref.shape[0] - EXTRA) // rows * LANES // CODE
    at = [wide[:, j : j + 1] for j in range(groups + 3)]
    return at[:groups], decode_scalar(*at[groups:])


def model_logits(mine, features, own_ref, squares_ref, cy_ref, cx_ref, cd_ref, out_ref):
    rows = squares_ref.shape[0]
    cols = own_ref.shape[1]

    def run(scale, at_slab):
        for slab in range(cols // LANES):
            out_ref[:, pl.ds(slab * LANES, LANES)] = at_slab(slab) * scale

    @pl.when(mine)
    def _():
        power_y, squares_y = extras(cy_ref, rows)

        def at_slab(slab):
            at = pl.ds(slab * LANES, LANES)
            own = own_ref[pl.ds(0, rows), at] + own_ref[pl.ds(rows, rows), at]
            return own + decode(cy_ref[pl.ds(slab * rows, rows), :], power_y[slab * LANES // CODE])

        run(lax.rsqrt((squares_ref[:, :1] + squares_y) / features + 1e-05), at_slab)

    @pl.when(jnp.logical_not(mine))
    def _():
        power_x, squares_x = extras(cx_ref, rows)
        power_d, squares_d = extras(cd_ref, rows)

        def at_slab(slab):
            part, group = pl.ds(slab * rows, rows), slab * LANES // CODE
            return decode(cx_ref[part, :], power_x[group]) + decode(cd_ref[part, :], power_d[group])

        run(lax.rsqrt((squares_x + squares_d) / features + 1e-05), at_slab)

    peak = jnp.full((rows, LANES), -jnp.inf, f32)
    for slab in range(cols // LANES):
        peak = jnp.maximum(peak, out_ref[:, pl.ds(slab * LANES, LANES)])
    return jnp.max(peak, axis=1, keepdims=True)


def qwen_kernel(width, blocks, features, meta_ref, own_ref, squares_ref, cy_ref, cx_ref, cd_ref, u_ref, stats_ref, q_ref):
    rows = squares_ref.shape[0]
    body = blocks * width
    peak = model_logits(meta_ref[0] == 1, features, own_ref, squares_ref, cy_ref, cx_ref, cd_ref, q_ref)
    total = jnp.zeros((rows, 1), f32)
    for j in range(blocks):
        at = pl.ds(j * width, width)
        qwen = jnp.exp(q_ref[:, at] - peak)
        u_ref[:, at] = qwen.astype(bf16)
        total += jnp.sum(qwen, axis=1, keepdims=True)
    first = peak.astype(bf16).astype(f32)
    second = (peak - first).astype(bf16).astype(f32)
    third = peak - first - second
    u_ref[:, body:] = columns_to_lanes([first, second, third], rows).astype(bf16)
    stats_ref[...] = columns_to_lanes([peak, total], rows)


def join_qwen(meta, own, squares, codes, width, features):
    rows, cols = own.shape[0] // 2, own.shape[1]
    whole = pl.BlockSpec(memory_space=pltpu.VMEM)
    return pl.pallas_call(
        functools.partial(qwen_kernel, width, cols // width, features),
        in_specs=[pl.BlockSpec(memory_space=pltpu.SMEM)] + [whole] * 5,
        out_shape=[
            jax.ShapeDtypeStruct((rows, cols + LANES), bf16),
            jax.ShapeDtypeStruct((rows, LANES), f32),
        ],
        scratch_shapes=[pltpu.VMEM((rows, cols), f32)],
        compiler_params=params(),
        cost_estimate=pl.CostEstimate(flops=1, bytes_accessed=8 * 1024 * 1024, transcendentals=0),
        name="join_qwen",
    )(meta, own, squares, *codes)


def llama_kernel(width, blocks, features, meta_ref, own_ref, squares_ref, cy_ref, cx_ref, cd_ref, token_ref, u_ref, near_ref, mine_ref, far_ref, before_ref, e_ref, stats_ref):
    rows = squares_ref.shape[0]
    body = blocks * width
    columns_refs = (near_ref, mine_ref, far_ref)
    peak = model_logits(meta_ref[0] == 0, features, own_ref, squares_ref, cy_ref, cx_ref, cd_ref, e_ref)
    total = jnp.zeros((rows, 1), f32)
    mass = jnp.zeros((rows, 1), f32)
    pick_e = jnp.zeros((rows, 1), f32)
    pick_m = jnp.zeros((rows, 1), f32)
    token = jnp.transpose(jnp.broadcast_to(token_ref[...].astype(f32), (8, rows)))
    token = token[:, :1].astype(i32) - meta_ref[1] * body
    for j in range(blocks):
        at = pl.ds(j * width, width)
        llama = jnp.exp(e_ref[:, at] - peak)
        e_ref[:, at] = llama
        total += jnp.sum(llama, axis=1, keepdims=True)
        hit = lax.broadcasted_iota(i32, (rows, width), 1) + j * width == token
        pick_e += jnp.sum(jnp.where(hit, llama, 0.0), axis=1, keepdims=True)
        held = u_ref[:, at].astype(f32)
        columns = functools.reduce(jnp.add, [ref[pl.ds(0, rows), at].astype(f32) for ref in columns_refs])
        pick_m += jnp.sum(held * columns, axis=1, keepdims=True)
        sums = functools.reduce(jnp.add, [ref[pl.ds(rows, EXTRA), at].astype(f32) for ref in columns_refs])
        mass += jnp.sum(held * jnp.sum(sums, axis=0, keepdims=True), axis=1, keepdims=True)
    before = before_ref[...]
    stats = columns_to_lanes([peak, total, before[:, 0:1], before[:, 1:2], mass, pick_e, pick_m], rows)
    stats_ref[...] = jnp.transpose(stats)[:8]


def join_llama(meta, own, squares, codes, token, u, columns, stats, width, features):
    rows, cols = own.shape[0] // 2, own.shape[1]
    whole = pl.BlockSpec(memory_space=pltpu.VMEM)
    return pl.pallas_call(
        functools.partial(llama_kernel, width, cols // width, features),
        in_specs=[pl.BlockSpec(memory_space=pltpu.SMEM)] + [whole] * 11,
        out_shape=[jax.ShapeDtypeStruct((rows, cols), f32), jax.ShapeDtypeStruct((8, rows), f32)],
        compiler_params=params(),
        cost_estimate=pl.CostEstimate(flops=1, bytes_accessed=8 * 1024 * 1024, transcendentals=0),
        name="join_llama",
    )(meta, own, squares, *codes, token, u, *columns, stats)


def map_kernel(width, blocks, shards, meta_ref, u_ref, near_ref, far_ref, w_ref, m_ref, top_ref, all_ref, scale_ref):
    rows = u_ref.shape[0]
    body = blocks * width
    shard = meta_ref[1]
    slots = w_ref.shape[0]
    near_at = jnp.where(shard % 2 == 0, 2, 0)

    def peak_of(ref):
        lanes = ref[:, body:].astype(f32)
        return lanes[:, 0:1] + lanes[:, 1:2] + lanes[:, 2:3]

    own_peak = peak_of(u_ref)
    near_peak = peak_of(near_ref)
    far_peak = jnp.where((shard > 0) & (shard < shards - 1), peak_of(far_ref), own_peak)
    top = jnp.maximum(jnp.maximum(near_peak, far_peak), own_peak)
    for k, ref, peak in ((near_at, near_ref, near_peak), (1, u_ref, own_peak), (2 - near_at, far_ref, far_peak)):
        all_ref[k] = ref[:, :body]
        scale_ref[k] = jnp.broadcast_to(jnp.exp(peak - top), (rows, LANES))
    m_ref[...] = jnp.zeros_like(m_ref)
    for slot in range(slots):

        @pl.when(slot < meta_ref[2 + 2 * slots])
        def _():
            source = jnp.clip(meta_ref[2 + slot] - (shard - 1) * blocks, 0, 3 * blocks - 1)
            target = jnp.clip(meta_ref[2 + slots + slot] - shard * blocks, 0, blocks - 1)
            inside = pl.multiple_of(source % blocks * width, width)
            picked = all_ref[source // blocks, :, pl.ds(inside, width)]
            term = jnp.dot(picked, w_ref[slot], preferred_element_type=f32)
            at = pl.ds(pl.multiple_of(target * width, width), width)
            m_ref[:, at] += term * scale_ref[source // blocks][:, :1]

    top_ref[...] = jnp.broadcast_to(top, (rows, LANES))


def map_parts(meta, u, near, far, weights, width, shards):
    rows, cols = u.shape[0], u.shape[1] - LANES
    blocks = cols // width
    whole = pl.BlockSpec(memory_space=pltpu.VMEM)
    return pl.pallas_call(
        functools.partial(map_kernel, width, blocks, shards),
        in_specs=[pl.BlockSpec(memory_space=pltpu.SMEM)] + [whole] * 4,
        out_shape=[jax.ShapeDtypeStruct((rows, cols), f32), jax.ShapeDtypeStruct((rows, LANES), f32)],
        scratch_shapes=[pltpu.VMEM((3, rows, cols), bf16), pltpu.VMEM((3, rows, LANES), f32)],
        compiler_params=params(),
        cost_estimate=pl.CostEstimate(
            flops=2 * rows * weights.size, bytes_accessed=2 * weights.size, transcendentals=0
        ),
        name="map_parts",
    )(meta, u, near, far, weights)


def finish_kernel(pieces, *refs):
    stats_refs, (e_ref, m_ref, m_top_ref, out_ref, nll_ref) = refs[:pieces], refs[pieces:]
    stats = [ref[k : k + 8, :] for ref in stats_refs for k in range(0, ref.shape[0], 8)]
    shards = range(len(stats))
    row = lambda s, k: stats[s][k : k + 1, :]
    top_l = functools.reduce(jnp.maximum, [row(s, 0) for s in shards])
    top_q = functools.reduce(jnp.maximum, [row(s, 2) for s in shards])
    sum_l = functools.reduce(jnp.add, [row(s, 1) * jnp.exp(row(s, 0) - top_l) for s in shards])
    sum_q = functools.reduce(jnp.add, [row(s, 3) * jnp.exp(row(s, 2) - top_q) for s in shards])
    part_l = [jnp.exp(row(s, 0) - top_l) / sum_l for s in shards]
    part_q = [jnp.exp(row(s, 2) - top_q) / sum_q for s in shards]
    mass = functools.reduce(jnp.add, [row(s, 4) * part_q[s] for s in shards])
    pick_e = functools.reduce(jnp.add, [row(s, 5) * part_l[s] for s in shards])
    pick_m = functools.reduce(jnp.add, [row(s, 6) * part_q[s] for s in shards])
    log_norm = jnp.log1p(mass)
    nll_ref[...] = log_norm - jnp.log(jnp.maximum(pick_e, FLOOR) + pick_m)
    tile = jnp.concatenate([part_l[0], top_q, 1.0 / sum_q, log_norm, jnp.zeros((4, log_norm.shape[1]), f32)], axis=0)
    turned = jnp.transpose(tile)
    a, top, share, c = (turned[:, i : i + 1] for i in range(4))
    b = jnp.exp(m_top_ref[:, :1] - top) * share
    out_ref[...] = jnp.log(jnp.maximum(e_ref[...] * a, FLOOR) + m_ref[...] * b) - c


def finish(pieces, e, m, m_top):
    rows, cols = e.shape
    return pl.pallas_call(
        functools.partial(finish_kernel, len(pieces)),
        out_shape=[
            jax.ShapeDtypeStruct((rows, cols), f32),
            jax.ShapeDtypeStruct((1, rows), f32),
        ],
        compiler_params=params(),
        cost_estimate=pl.CostEstimate(
            flops=20 * rows * cols, bytes_accessed=12 * rows * cols, transcendentals=2 * rows * cols
        ),
        name="finish",
    )(*pieces, e, m, m_top)


def gather_pieces(own, shards):
    pieces, step = [own], 1
    while step < shards:
        radix = 4 if step > 1 and 4 * step <= shards else 2
        sent = pieces[0] if len(pieces) == 1 else jnp.concatenate(pieces, axis=0)
        for turn in range(1, radix):
            pieces.append(lax.ppermute(sent, "vocab", [(i, i ^ (turn * step)) for i in range(shards)]))
        step *= radix
    return pieces


def on_device(
    hidden, norm_gain, head_weights, pair_source, pair_target, pair_count, pair_weight, next_token
):
    shards = lax.axis_size("vocab")
    row_groups = lax.axis_size("rows")
    hidden, head = hidden[0], head_weights[0]
    token = next_token[None, :]
    held_hidden = pltpu.with_memory_space_constraint(hidden, pltpu.HBM)
    held_weight = pltpu.with_memory_space_constraint(pair_weight, pltpu.HBM)
    held_gain = pltpu.with_memory_space_constraint(norm_gain, pltpu.HBM)
    head = pltpu.with_memory_space_constraint(head, pltpu.HBM)
    width = pair_weight.shape[1]
    features = hidden.shape[1] * row_groups
    model, shard, side = (lax.axis_index(name).astype(i32) for name in ("mp", "vocab", "rows"))
    mine = 2 * model + side
    quarters = jnp.stack([mine, mine ^ 1, mine ^ 2, mine ^ 3])
    meta = jnp.concatenate([jnp.stack([model, shard]), pair_source, pair_target, pair_count])

    inside = [(i, i ^ 1) for i in range(shards)]
    across = [(i, i + 1 if i % 2 else i - 1) for i in range(1, shards - 1)]
    lefts, squares, head = first_prep(quarters, held_hidden, held_gain, head, (3, 1, 2))
    (to_d,) = encode_parts(product(lefts[0], head), squares[:1])
    from_d = lax.ppermute(to_d, ("mp", "rows"), [(0, 3), (1, 2), (2, 1), (3, 0)])
    left_y, _ = lax.optimization_barrier((lefts[1], to_d))
    (to_y,) = encode_parts(product(left_y, head), squares[1:2])
    from_y = lax.ppermute(to_y, "rows", [(0, 1), (1, 0)])
    left_x, _ = lax.optimization_barrier((lefts[2], to_y))
    (to_x,) = encode_parts(product(left_x, head), squares[2:])
    from_x = lax.ppermute(to_x, "mp", [(0, 1), (1, 0)])
    early, _ = lax.optimization_barrier((meta, to_x))
    (to_near, columns, to_far), left_own, squares_own = side_parts(
        early, quarters, token, held_hidden, held_gain, held_weight, width, head.shape[1]
    )
    far_columns = lax.ppermute(to_far, "vocab", across)
    near_columns = lax.ppermute(to_near, "vocab", inside)
    own = product(left_own, head)

    codes = (from_y, from_x, from_d)
    u, stats = join_qwen(meta, own, squares_own, codes, width, features)
    far = lax.ppermute(u, "vocab", across)
    near = lax.ppermute(u, "vocab", inside)
    e, stats = join_llama(
        meta, own, squares_own, codes, token, u, (near_columns, columns, far_columns), stats, width, features
    )
    m, m_top = map_parts(meta, u, near, far, pair_weight, width, shards)
    out, nll = finish(gather_pieces(stats, shards), e, m, m_top)
    return out, nll[0]


def solution(mesh):
    in_specs = (
        P("mp", None, "rows"),
        P("mp", "rows"),
        P("mp", "rows", "vocab"),
        P("vocab"),
        P("vocab"),
        P("vocab"),
        P("vocab", None, None),
        P(("mp", "rows")),
    )
    out_specs = (P(("mp", "rows"), "vocab"), P(("mp", "rows")))
    return jax.shard_map(
        on_device, mesh=mesh, in_specs=in_specs, out_specs=out_specs, check_vma=False
    )
```

```python
import functools

import jax
import jax.numpy as jnp
from jax import lax
from jax.experimental import pallas as pl
from jax.experimental.pallas import tpu as pltpu
from jax.sharding import PartitionSpec as P

LANES = 128
EXTRA = 16
CODE = 512
HEAD_COPIES = 1
TOP = 32767.0
LEAST = 1e-30
FLOOR = 1.9287498479639178e-22
VMEM = 16 * 1024 * 1024

f32, bf16, i32, i16 = jnp.float32, jnp.bfloat16, jnp.int32, jnp.int16


def params():
    return pltpu.CompilerParams(vmem_limit_bytes=VMEM)


def exponent(value):
    return jnp.ceil(jnp.log2(jnp.maximum(value, LEAST)))


def columns_to_lanes(values, rows):
    lanes = lax.broadcasted_iota(i32, (rows, LANES), 1)
    out = jnp.zeros((rows, LANES), f32)
    for place, value in enumerate(values):
        out = jnp.where(lanes == place, value, out)
    return out


def split_exact(gained):
    high = gained.astype(bf16)
    return high, (gained - high.astype(f32)).astype(bf16)


def encode(values, power):
    size = jnp.sqrt(jnp.abs(values) * jnp.exp2(-power)) * TOP
    code = jnp.minimum(size + 0.5, TOP).astype(i32)
    return jnp.where(values < 0, -code, code).astype(i16)


def decode(codes, power):
    wide = codes.astype(i32).astype(f32)
    return wide * jnp.abs(wide) * (jnp.exp2(power) * (1.0 / (TOP * TOP)))


def encode_scalar(value):
    power = exponent(value)
    mantissa = jnp.maximum(value, LEAST) * jnp.exp2(-power) * 16384.0
    first = jnp.floor(mantissa)
    return power, first, jnp.floor((mantissa - first) * 16384.0)


def decode_scalar(power, first, second):
    return (first + second * (1.0 / 16384.0)) * (1.0 / 16384.0) * jnp.exp2(power)


def prepare(hidden, gain, left_ref, at):
    rows = hidden.shape[0]
    values = hidden.astype(f32)
    high, low = split_exact(values * gain)
    left_ref[pl.ds(at, rows), :] = high
    left_ref[pl.ds(at + rows, rows), :] = low
    return jnp.sum(values * values, axis=1, keepdims=True)


def put_codes(out_ref, both, first):
    rows = both.shape[0] // 2
    part = both[:rows] + both[rows:]
    power = exponent(jnp.max(jnp.abs(part), axis=1, keepdims=True))
    codes = encode(part, power)
    for k in range(part.shape[1] // LANES):
        out_ref[pl.ds((first // LANES + k) * rows, rows), :] = codes[:, k * LANES : (k + 1) * LANES]
    return power


def put_extra(out_ref, powers, squares):
    rows = squares.shape[0]
    extra = columns_to_lanes(powers + list(encode_scalar(squares)), rows)
    body = out_ref.shape[0] - EXTRA
    out_ref[pl.ds(body, EXTRA), :] = jnp.transpose(extra)[:EXTRA].astype(i32).astype(i16)


def first_kernel(kinds, rows, quarter_ref, hidden_ref, gain_ref, head_ref, *refs):
    count = len(kinds)
    left_refs, square_refs, head_out = refs[:count], refs[count : 2 * count], refs[2 * count]
    held, gain_held, sems, gain_sem, head_sems = refs[2 * count + 1 :]
    copies = []
    for place, which in enumerate(kinds):
        at = pl.ds(pl.multiple_of(quarter_ref[which] * rows, rows), rows)
        copies.append(pltpu.make_async_copy(hidden_ref.at[at, :], held.at[place], sems.at[place]))
    gain_copy = pltpu.make_async_copy(gain_ref, gain_held, gain_sem)
    deep = head_ref.shape[0] // HEAD_COPIES
    spans = [pl.ds(k * deep, deep) for k in range(HEAD_COPIES)]
    head_copies = [
        pltpu.make_async_copy(head_ref.at[at, :], head_out.at[at, :], head_sems.at[k])
        for k, at in enumerate(spans)
    ]
    gain_copy.start()
    for copy in copies + head_copies:
        copy.start()
    gain_copy.wait()
    gain = gain_held[...].astype(f32)
    for place, copy in enumerate(copies):
        copy.wait()
        squares = prepare(held[place], gain, left_refs[place], 0)
        square_refs[place][...] = jnp.broadcast_to(squares, (rows, LANES))
    for copy in head_copies:
        copy.wait()


def first_prep(quarters, hidden, gain, head, kinds):
    rows, feats, count = hidden.shape[0] // 4, hidden.shape[1], len(kinds)
    hbm = pl.BlockSpec(memory_space=pltpu.HBM)
    outs = pl.pallas_call(
        functools.partial(first_kernel, kinds, rows),
        in_specs=[pl.BlockSpec(memory_space=pltpu.SMEM), hbm, hbm, hbm],
        out_shape=[jax.ShapeDtypeStruct((2 * rows, feats), bf16)] * count
        + [jax.ShapeDtypeStruct((rows, LANES), f32)] * count
        + [jax.ShapeDtypeStruct(head.shape, head.dtype)],
        scratch_shapes=[
            pltpu.VMEM((count, rows, feats), bf16),
            pltpu.VMEM(gain.shape, bf16),
            pltpu.SemaphoreType.DMA((count,)),
            pltpu.SemaphoreType.DMA,
            pltpu.SemaphoreType.DMA((HEAD_COPIES,)),
        ],
        compiler_params=params(),
        cost_estimate=pl.CostEstimate(
            flops=8 * count * rows * feats, bytes_accessed=2 * head.size, transcendentals=0
        ),
        name="first_prep",
    )(quarters, hidden, gain, head)
    return outs[:count], outs[count : 2 * count], outs[2 * count]


def encode_kernel(count, both_ref, *refs):
    square_refs, outs = refs[:count], refs[count:]
    rows, cols = both_ref.shape[0] // count // 2, both_ref.shape[1]
    for place, out_ref in enumerate(outs):
        powers = []
        for first in range(0, cols, CODE):
            both = both_ref[pl.ds(2 * place * rows, 2 * rows), pl.ds(first, CODE)]
            powers.append(put_codes(out_ref, both, first))
        put_extra(out_ref, powers, square_refs[place][:, :1])


def encode_parts(both, squares):
    count = len(squares)
    rows, cols = both.shape[0] // count // 2, both.shape[1]
    return pl.pallas_call(
        functools.partial(encode_kernel, count),
        out_shape=[jax.ShapeDtypeStruct((cols // LANES * rows + EXTRA, LANES), i16)] * count,
        compiler_params=params(),
        cost_estimate=pl.CostEstimate(
            flops=20 * count * rows * cols, bytes_accessed=10 * count * rows * cols, transcendentals=count * rows * cols
        ),
        name="encode_parts",
    )(both, *squares)


def product(left, head):
    return jnp.dot(left, head, preferred_element_type=f32)


def side_kernel(width, blocks, own_which, meta_ref, quarter_ref, token_ref, hidden_ref, gain_ref, w_ref, near_ref, own_ref, far_ref, left_ref, squares_ref, held, gain_held, w_held, sum_ref, sem, gain_sem, w_sems):
    rows = token_ref.shape[1]
    slots = w_ref.shape[0]
    at = pl.ds(pl.multiple_of(quarter_ref[own_which] * rows, rows), rows)
    hidden_copy = pltpu.make_async_copy(hidden_ref.at[at, :], held, sem)
    gain_copy = pltpu.make_async_copy(gain_ref, gain_held, gain_sem)
    w_copies = [pltpu.make_async_copy(w_ref.at[k], w_held.at[k], w_sems.at[k]) for k in range(slots)]
    gain_copy.start()
    hidden_copy.start()
    for copy in w_copies:
        copy.start()
    shard = meta_ref[1]
    near_at = jnp.where(shard % 2 == 0, 2, 0)
    token = jnp.transpose(jnp.broadcast_to(token_ref[...].astype(f32), (8, rows)))[:, :1].astype(i32)
    place = lax.broadcasted_iota(i32, (rows, width), 1)
    sum_ref[...] = jnp.zeros_like(sum_ref)
    gain_copy.wait()
    hidden_copy.wait()
    squares = prepare(held[...], gain_held[...].astype(f32), left_ref, 0)
    squares_ref[...] = jnp.broadcast_to(squares, (rows, LANES))
    for slot in range(slots):
        w_copies[slot].wait()

        @pl.when(slot < meta_ref[2 + 2 * slots])
        def _():
            source = jnp.clip(meta_ref[2 + slot] - (shard - 1) * blocks, 0, 3 * blocks - 1)
            hits = (token - meta_ref[2 + slots + slot] * width == place).astype(bf16)
            left = jnp.concatenate([hits, jnp.ones((EXTRA, width), bf16)], axis=0)
            found = lax.dot_general(
                left, w_held[slot], (((1,), (1,)), ((), ())), preferred_element_type=f32
            )
            at = pl.ds(pl.multiple_of(source % blocks * width, width), width)
            sum_ref[source // blocks, :, at] += found

    order = lax.broadcasted_iota(i32, (EXTRA, 1), 0)
    for out_ref, k in ((near_ref, near_at), (own_ref, 1), (far_ref, 2 - near_at)):
        out_ref[pl.ds(0, rows), :] = sum_ref[k, pl.ds(0, rows), :].astype(bf16)
        sums = sum_ref[k, pl.ds(rows, EXTRA), :]
        first = sums.astype(bf16).astype(f32)
        second = (sums - first).astype(bf16).astype(f32)
        third = sums - first - second
        parts = jnp.where(order == 0, first, jnp.where(order == 1, second, jnp.where(order == 2, third, 0.0)))
        out_ref[pl.ds(rows, EXTRA), :] = parts.astype(bf16)


def side_parts(meta, quarters, token, hidden, gain, weights, width, cols):
    rows, feats = token.shape[1], hidden.shape[1]
    smem = pl.BlockSpec(memory_space=pltpu.SMEM)
    hbm = pl.BlockSpec(memory_space=pltpu.HBM)
    outs = pl.pallas_call(
        functools.partial(side_kernel, width, cols // width, 0),
        in_specs=[smem, smem, pl.BlockSpec(memory_space=pltpu.VMEM), hbm, hbm, hbm],
        out_shape=[jax.ShapeDtypeStruct((rows + EXTRA, cols), bf16)] * 3
        + [jax.ShapeDtypeStruct((2 * rows, feats), bf16), jax.ShapeDtypeStruct((rows, LANES), f32)],
        scratch_shapes=[
            pltpu.VMEM((rows, feats), bf16),
            pltpu.VMEM(gain.shape, bf16),
            pltpu.VMEM(weights.shape, bf16),
            pltpu.VMEM((3, rows + EXTRA, cols), f32),
            pltpu.SemaphoreType.DMA,
            pltpu.SemaphoreType.DMA,
            pltpu.SemaphoreType.DMA((weights.shape[0],)),
        ],
        compiler_params=params(),
        cost_estimate=pl.CostEstimate(flops=1, bytes_accessed=1, transcendentals=0),
        name="side_parts",
    )(meta, quarters, token, hidden, gain, weights)
    return outs[:3], outs[3], outs[4]


def extras(ref, rows):
    tile = ref[pl.ds(ref.shape[0] - EXTRA, EXTRA), :].astype(i32).astype(f32)
    wide = jnp.transpose(tile)
    groups = (ref.shape[0] - EXTRA) // rows * LANES // CODE
    at = [wide[:, j : j + 1] for j in range(groups + 3)]
    return at[:groups], decode_scalar(*at[groups:])


def model_logits(mine, features, own_ref, squares_ref, cy_ref, cx_ref, cd_ref, out_ref):
    rows = squares_ref.shape[0]
    cols = own_ref.shape[1]

    def run(scale, at_slab):
        for slab in range(cols // LANES):
            out_ref[:, pl.ds(slab * LANES, LANES)] = at_slab(slab) * scale

    @pl.when(mine)
    def _():
        power_y, squares_y = extras(cy_ref, rows)

        def at_slab(slab):
            at = pl.ds(slab * LANES, LANES)
            own = own_ref[pl.ds(0, rows), at] + own_ref[pl.ds(rows, rows), at]
            return own + decode(cy_ref[pl.ds(slab * rows, rows), :], power_y[slab * LANES // CODE])

        run(lax.rsqrt((squares_ref[:, :1] + squares_y) / features + 1e-05), at_slab)

    @pl.when(jnp.logical_not(mine))
    def _():
        power_x, squares_x = extras(cx_ref, rows)
        power_d, squares_d = extras(cd_ref, rows)

        def at_slab(slab):
            part, group = pl.ds(slab * rows, rows), slab * LANES // CODE
            return decode(cx_ref[part, :], power_x[group]) + decode(cd_ref[part, :], power_d[group])

        run(lax.rsqrt((squares_x + squares_d) / features + 1e-05), at_slab)

    peak = jnp.full((rows, LANES), -jnp.inf, f32)
    for slab in range(cols // LANES):
        peak = jnp.maximum(peak, out_ref[:, pl.ds(slab * LANES, LANES)])
    return jnp.max(peak, axis=1, keepdims=True)


def qwen_kernel(width, blocks, features, meta_ref, own_ref, squares_ref, cy_ref, cx_ref, cd_ref, u_ref, stats_ref, q_ref):
    rows = squares_ref.shape[0]
    body = blocks * width
    peak = model_logits(meta_ref[0] == 1, features, own_ref, squares_ref, cy_ref, cx_ref, cd_ref, q_ref)
    total = jnp.zeros((rows, 1), f32)
    for j in range(blocks):
        at = pl.ds(j * width, width)
        qwen = jnp.exp(q_ref[:, at] - peak)
        u_ref[:, at] = qwen.astype(bf16)
        total += jnp.sum(qwen, axis=1, keepdims=True)
    first = peak.astype(bf16).astype(f32)
    second = (peak - first).astype(bf16).astype(f32)
    third = peak - first - second
    u_ref[:, body:] = columns_to_lanes([first, second, third], rows).astype(bf16)
    stats_ref[...] = columns_to_lanes([peak, total], rows)


def join_qwen(meta, own, squares, codes, width, features):
    rows, cols = own.shape[0] // 2, own.shape[1]
    whole = pl.BlockSpec(memory_space=pltpu.VMEM)
    return pl.pallas_call(
        functools.partial(qwen_kernel, width, cols // width, features),
        in_specs=[pl.BlockSpec(memory_space=pltpu.SMEM)] + [whole] * 5,
        out_shape=[
            jax.ShapeDtypeStruct((rows, cols + LANES), bf16),
            jax.ShapeDtypeStruct((rows, LANES), f32),
        ],
        scratch_shapes=[pltpu.VMEM((rows, cols), f32)],
        compiler_params=params(),
        cost_estimate=pl.CostEstimate(flops=20000000000, bytes_accessed=8 * 1024 * 1024, transcendentals=0),
        name="join_qwen",
    )(meta, own, squares, *codes)


def llama_kernel(width, blocks, features, meta_ref, own_ref, squares_ref, cy_ref, cx_ref, cd_ref, token_ref, u_ref, near_ref, mine_ref, far_ref, before_ref, e_ref, stats_ref):
    rows = squares_ref.shape[0]
    body = blocks * width
    columns_refs = (near_ref, mine_ref, far_ref)
    peak = model_logits(meta_ref[0] == 0, features, own_ref, squares_ref, cy_ref, cx_ref, cd_ref, e_ref)
    total = jnp.zeros((rows, 1), f32)
    mass = jnp.zeros((rows, 1), f32)
    pick_e = jnp.zeros((rows, 1), f32)
    pick_m = jnp.zeros((rows, 1), f32)
    token = jnp.transpose(jnp.broadcast_to(token_ref[...].astype(f32), (8, rows)))
    token = token[:, :1].astype(i32) - meta_ref[1] * body
    for j in range(blocks):
        at = pl.ds(j * width, width)
        llama = jnp.exp(e_ref[:, at] - peak)
        e_ref[:, at] = llama
        total += jnp.sum(llama, axis=1, keepdims=True)
        hit = lax.broadcasted_iota(i32, (rows, width), 1) + j * width == token
        pick_e += jnp.sum(jnp.where(hit, llama, 0.0), axis=1, keepdims=True)
        held = u_ref[:, at].astype(f32)
        columns = functools.reduce(jnp.add, [ref[pl.ds(0, rows), at].astype(f32) for ref in columns_refs])
        pick_m += jnp.sum(held * columns, axis=1, keepdims=True)
        sums = functools.reduce(jnp.add, [ref[pl.ds(rows, EXTRA), at].astype(f32) for ref in columns_refs])
        mass += jnp.sum(held * jnp.sum(sums, axis=0, keepdims=True), axis=1, keepdims=True)
    before = before_ref[...]
    stats = columns_to_lanes([peak, total, before[:, 0:1], before[:, 1:2], mass, pick_e, pick_m], rows)
    stats_ref[...] = jnp.transpose(stats)[:8]


def join_llama(meta, own, squares, codes, token, u, columns, stats, width, features):
    rows, cols = own.shape[0] // 2, own.shape[1]
    whole = pl.BlockSpec(memory_space=pltpu.VMEM)
    return pl.pallas_call(
        functools.partial(llama_kernel, width, cols // width, features),
        in_specs=[pl.BlockSpec(memory_space=pltpu.SMEM)] + [whole] * 11,
        out_shape=[jax.ShapeDtypeStruct((rows, cols), f32), jax.ShapeDtypeStruct((8, rows), f32)],
        compiler_params=params(),
        cost_estimate=pl.CostEstimate(flops=20000000000, bytes_accessed=8 * 1024 * 1024, transcendentals=0),
        name="join_llama",
    )(meta, own, squares, *codes, token, u, *columns, stats)


def map_kernel(width, blocks, shards, meta_ref, u_ref, near_ref, far_ref, w_ref, m_ref, top_ref, all_ref, scale_ref):
    rows = u_ref.shape[0]
    body = blocks * width
    shard = meta_ref[1]
    slots = w_ref.shape[0]
    near_at = jnp.where(shard % 2 == 0, 2, 0)

    def peak_of(ref):
        lanes = ref[:, body:].astype(f32)
        return lanes[:, 0:1] + lanes[:, 1:2] + lanes[:, 2:3]

    own_peak = peak_of(u_ref)
    near_peak = peak_of(near_ref)
    far_peak = jnp.where((shard > 0) & (shard < shards - 1), peak_of(far_ref), own_peak)
    top = jnp.maximum(jnp.maximum(near_peak, far_peak), own_peak)
    for k, ref, peak in ((near_at, near_ref, near_peak), (1, u_ref, own_peak), (2 - near_at, far_ref, far_peak)):
        all_ref[k] = ref[:, :body]
        scale_ref[k] = jnp.broadcast_to(jnp.exp(peak - top), (rows, LANES))
    m_ref[...] = jnp.zeros_like(m_ref)
    for slot in range(slots):

        @pl.when(slot < meta_ref[2 + 2 * slots])
        def _():
            source = jnp.clip(meta_ref[2 + slot] - (shard - 1) * blocks, 0, 3 * blocks - 1)
            target = jnp.clip(meta_ref[2 + slots + slot] - shard * blocks, 0, blocks - 1)
            inside = pl.multiple_of(source % blocks * width, width)
            picked = all_ref[source // blocks, :, pl.ds(inside, width)]
            term = jnp.dot(picked, w_ref[slot], preferred_element_type=f32)
            at = pl.ds(pl.multiple_of(target * width, width), width)
            m_ref[:, at] += term * scale_ref[source // blocks][:, :1]

    top_ref[...] = jnp.broadcast_to(top, (rows, LANES))


def map_parts(meta, u, near, far, weights, width, shards):
    rows, cols = u.shape[0], u.shape[1] - LANES
    blocks = cols // width
    whole = pl.BlockSpec(memory_space=pltpu.VMEM)
    return pl.pallas_call(
        functools.partial(map_kernel, width, blocks, shards),
        in_specs=[pl.BlockSpec(memory_space=pltpu.SMEM)] + [whole] * 4,
        out_shape=[jax.ShapeDtypeStruct((rows, cols), f32), jax.ShapeDtypeStruct((rows, LANES), f32)],
        scratch_shapes=[pltpu.VMEM((3, rows, cols), bf16), pltpu.VMEM((3, rows, LANES), f32)],
        compiler_params=params(),
        cost_estimate=pl.CostEstimate(
            flops=2 * rows * weights.size, bytes_accessed=2 * weights.size, transcendentals=0
        ),
        name="map_parts",
    )(meta, u, near, far, weights)


def finish_kernel(pieces, *refs):
    stats_refs, (e_ref, m_ref, m_top_ref, out_ref, nll_ref) = refs[:pieces], refs[pieces:]
    stats = [ref[k : k + 8, :] for ref in stats_refs for k in range(0, ref.shape[0], 8)]
    shards = range(len(stats))
    row = lambda s, k: stats[s][k : k + 1, :]
    top_l = functools.reduce(jnp.maximum, [row(s, 0) for s in shards])
    top_q = functools.reduce(jnp.maximum, [row(s, 2) for s in shards])
    sum_l = functools.reduce(jnp.add, [row(s, 1) * jnp.exp(row(s, 0) - top_l) for s in shards])
    sum_q = functools.reduce(jnp.add, [row(s, 3) * jnp.exp(row(s, 2) - top_q) for s in shards])
    part_l = [jnp.exp(row(s, 0) - top_l) / sum_l for s in shards]
    part_q = [jnp.exp(row(s, 2) - top_q) / sum_q for s in shards]
    mass = functools.reduce(jnp.add, [row(s, 4) * part_q[s] for s in shards])
    pick_e = functools.reduce(jnp.add, [row(s, 5) * part_l[s] for s in shards])
    pick_m = functools.reduce(jnp.add, [row(s, 6) * part_q[s] for s in shards])
    log_norm = jnp.log1p(mass)
    nll_ref[...] = log_norm - jnp.log(jnp.maximum(pick_e, FLOOR) + pick_m)
    tile = jnp.concatenate([part_l[0], top_q, 1.0 / sum_q, log_norm, jnp.zeros((4, log_norm.shape[1]), f32)], axis=0)
    turned = jnp.transpose(tile)
    a, top, share, c = (turned[:, i : i + 1] for i in range(4))
    b = jnp.exp(m_top_ref[:, :1] - top) * share
    out_ref[...] = jnp.log(jnp.maximum(e_ref[...] * a, FLOOR) + m_ref[...] * b) - c


def finish(pieces, e, m, m_top):
    rows, cols = e.shape
    return pl.pallas_call(
        functools.partial(finish_kernel, len(pieces)),
        out_shape=[
            jax.ShapeDtypeStruct((rows, cols), f32),
            jax.ShapeDtypeStruct((1, rows), f32),
        ],
        compiler_params=params(),
        cost_estimate=pl.CostEstimate(
            flops=20 * rows * cols, bytes_accessed=12 * rows * cols, transcendentals=2 * rows * cols
        ),
        name="finish",
    )(*pieces, e, m, m_top)


def gather_pieces(own, shards):
    pieces, step = [own], 1
    while step < shards:
        radix = 4 if step > 1 and 4 * step <= shards else 2
        sent = pieces[0] if len(pieces) == 1 else jnp.concatenate(pieces, axis=0)
        for turn in range(1, radix):
            pieces.append(lax.ppermute(sent, "vocab", [(i, i ^ (turn * step)) for i in range(shards)]))
        step *= radix
    return pieces, sent


def on_device(
    hidden, norm_gain, head_weights, pair_source, pair_target, pair_count, pair_weight, next_token
):
    shards = lax.axis_size("vocab")
    row_groups = lax.axis_size("rows")
    hidden, head = hidden[0], head_weights[0]
    token = next_token[None, :]
    held_hidden = pltpu.with_memory_space_constraint(hidden, pltpu.HBM)
    held_weight = pltpu.with_memory_space_constraint(pair_weight, pltpu.HBM)
    held_gain = pltpu.with_memory_space_constraint(norm_gain, pltpu.HBM)
    head = pltpu.with_memory_space_constraint(head, pltpu.HBM)
    width = pair_weight.shape[1]
    features = hidden.shape[1] * row_groups
    model, shard, side = (lax.axis_index(name).astype(i32) for name in ("mp", "vocab", "rows"))
    mine = 2 * model + side
    quarters = jnp.stack([mine, mine ^ 1, mine ^ 2, mine ^ 3])
    meta = jnp.concatenate([jnp.stack([model, shard]), pair_source, pair_target, pair_count])

    inside = [(i, i ^ 1) for i in range(shards)]
    across = [(i, i + 1 if i % 2 else i - 1) for i in range(1, shards - 1)]
    lefts, squares, head = first_prep(quarters, held_hidden, held_gain, head, (3, 1, 2))
    (to_d,) = encode_parts(product(lefts[0], head), squares[:1])
    from_d = lax.ppermute(to_d, ("mp", "rows"), [(0, 3), (1, 2), (2, 1), (3, 0)])
    left_y, _ = lax.optimization_barrier((lefts[1], to_d))
    (to_y,) = encode_parts(product(left_y, head), squares[1:2])
    from_y = lax.ppermute(to_y, "rows", [(0, 1), (1, 0)])
    left_x, _ = lax.optimization_barrier((lefts[2], to_y))
    (to_x,) = encode_parts(product(left_x, head), squares[2:])
    from_x = lax.ppermute(to_x, "mp", [(0, 1), (1, 0)])
    early, _ = lax.optimization_barrier((meta, to_x))
    (to_near, columns, to_far), left_own, squares_own = side_parts(
        early, quarters, token, held_hidden, held_gain, held_weight, width, head.shape[1]
    )
    far_columns = lax.ppermute(to_far, "vocab", across)
    near_columns = lax.ppermute(to_near, "vocab", inside)
    own = product(left_own, head)

    codes = (from_y, from_x, from_d)
    u, stats = join_qwen(meta, own, squares_own, codes, width, features)
    far = lax.ppermute(u, "vocab", across)
    e, stats = join_llama(
        meta, own, squares_own, codes, token, u, (near_columns, columns, far_columns), stats, width, features
    )
    pieces, last = gather_pieces(stats, shards)
    late_u, _ = lax.optimization_barrier((u, last))
    near = lax.ppermute(late_u, "vocab", inside)
    m, m_top = map_parts(meta, u, near, far, pair_weight, width, shards)
    out, nll = finish(pieces, e, m, m_top)
    return out, nll[0]


def solution(mesh):
    in_specs = (
        P("mp", None, "rows"),
        P("mp", "rows"),
        P("mp", "rows", "vocab"),
        P("vocab"),
        P("vocab"),
        P("vocab"),
        P("vocab", None, None),
        P(("mp", "rows")),
    )
    out_specs = (P(("mp", "rows"), "vocab"), P(("mp", "rows")))
    return jax.shard_map(
        on_device, mesh=mesh, in_specs=in_specs, out_specs=out_specs, check_vma=False
    )
```

```python
import functools

import jax
import jax.numpy as jnp
from jax import lax
from jax.experimental import pallas as pl
from jax.experimental.pallas import tpu as pltpu
from jax.sharding import PartitionSpec as P

LANES = 128
EXTRA = 16
CODE = 512
HEAD_COPIES = 1
TOP = 32767.0
LEAST = 1e-30
FLOOR = 1.9287498479639178e-22
VMEM = 16 * 1024 * 1024

f32, bf16, i32, i16 = jnp.float32, jnp.bfloat16, jnp.int32, jnp.int16


def params():
    return pltpu.CompilerParams(vmem_limit_bytes=VMEM)


def exponent(value):
    return jnp.ceil(jnp.log2(jnp.maximum(value, LEAST)))


def columns_to_lanes(values, rows):
    lanes = lax.broadcasted_iota(i32, (rows, LANES), 1)
    out = jnp.zeros((rows, LANES), f32)
    for place, value in enumerate(values):
        out = jnp.where(lanes == place, value, out)
    return out


def split_exact(gained):
    high = gained.astype(bf16)
    return high, (gained - high.astype(f32)).astype(bf16)


def encode(values, power):
    size = jnp.sqrt(jnp.abs(values) * jnp.exp2(-power)) * TOP
    code = jnp.minimum(size + 0.5, TOP).astype(i32)
    return jnp.where(values < 0, -code, code).astype(i16)


def decode(codes, power):
    wide = codes.astype(i32).astype(f32)
    return wide * jnp.abs(wide) * (jnp.exp2(power) * (1.0 / (TOP * TOP)))


def encode_scalar(value):
    power = exponent(value)
    mantissa = jnp.maximum(value, LEAST) * jnp.exp2(-power) * 16384.0
    first = jnp.floor(mantissa)
    return power, first, jnp.floor((mantissa - first) * 16384.0)


def decode_scalar(power, first, second):
    return (first + second * (1.0 / 16384.0)) * (1.0 / 16384.0) * jnp.exp2(power)


def prepare(hidden, gain, left_ref, at):
    rows = hidden.shape[0]
    values = hidden.astype(f32)
    high, low = split_exact(values * gain)
    left_ref[pl.ds(at, rows), :] = high
    left_ref[pl.ds(at + rows, rows), :] = low
    return jnp.sum(values * values, axis=1, keepdims=True)


def put_codes(out_ref, both, first):
    rows = both.shape[0] // 2
    part = both[:rows] + both[rows:]
    power = exponent(jnp.max(jnp.abs(part), axis=1, keepdims=True))
    codes = encode(part, power)
    for k in range(part.shape[1] // LANES):
        out_ref[pl.ds((first // LANES + k) * rows, rows), :] = codes[:, k * LANES : (k + 1) * LANES]
    return power


def put_extra(out_ref, powers, squares):
    rows = squares.shape[0]
    extra = columns_to_lanes(powers + list(encode_scalar(squares)), rows)
    body = out_ref.shape[0] - EXTRA
    out_ref[pl.ds(body, EXTRA), :] = jnp.transpose(extra)[:EXTRA].astype(i32).astype(i16)


def first_kernel(kinds, rows, quarter_ref, hidden_ref, gain_ref, head_ref, *refs):
    count = len(kinds)
    left_refs, square_refs, head_out = refs[:count], refs[count : 2 * count], refs[2 * count]
    held, gain_held, sems, gain_sem, head_sems = refs[2 * count + 1 :]
    copies = []
    for place, which in enumerate(kinds):
        at = pl.ds(pl.multiple_of(quarter_ref[which] * rows, rows), rows)
        copies.append(pltpu.make_async_copy(hidden_ref.at[at, :], held.at[place], sems.at[place]))
    gain_copy = pltpu.make_async_copy(gain_ref, gain_held, gain_sem)
    deep = head_ref.shape[0] // HEAD_COPIES
    spans = [pl.ds(k * deep, deep) for k in range(HEAD_COPIES)]
    head_copies = [
        pltpu.make_async_copy(head_ref.at[at, :], head_out.at[at, :], head_sems.at[k])
        for k, at in enumerate(spans)
    ]
    gain_copy.start()
    for copy in copies + head_copies:
        copy.start()
    gain_copy.wait()
    gain = gain_held[...].astype(f32)
    for place, copy in enumerate(copies):
        copy.wait()
        squares = prepare(held[place], gain, left_refs[place], 0)
        square_refs[place][...] = jnp.broadcast_to(squares, (rows, LANES))
    for copy in head_copies:
        copy.wait()


def first_prep(quarters, hidden, gain, head, kinds):
    rows, feats, count = hidden.shape[0] // 4, hidden.shape[1], len(kinds)
    hbm = pl.BlockSpec(memory_space=pltpu.HBM)
    outs = pl.pallas_call(
        functools.partial(first_kernel, kinds, rows),
        in_specs=[pl.BlockSpec(memory_space=pltpu.SMEM), hbm, hbm, hbm],
        out_shape=[jax.ShapeDtypeStruct((2 * rows, feats), bf16)] * count
        + [jax.ShapeDtypeStruct((rows, LANES), f32)] * count
        + [jax.ShapeDtypeStruct(head.shape, head.dtype)],
        scratch_shapes=[
            pltpu.VMEM((count, rows, feats), bf16),
            pltpu.VMEM(gain.shape, bf16),
            pltpu.SemaphoreType.DMA((count,)),
            pltpu.SemaphoreType.DMA,
            pltpu.SemaphoreType.DMA((HEAD_COPIES,)),
        ],
        compiler_params=params(),
        cost_estimate=pl.CostEstimate(
            flops=8 * count * rows * feats, bytes_accessed=2 * head.size, transcendentals=0
        ),
        name="first_prep",
    )(quarters, hidden, gain, head)
    return outs[:count], outs[count : 2 * count], outs[2 * count]


def encode_kernel(count, both_ref, *refs):
    square_refs, outs = refs[:count], refs[count:]
    rows, cols = both_ref.shape[0] // count // 2, both_ref.shape[1]
    for place, out_ref in enumerate(outs):
        powers = []
        for first in range(0, cols, CODE):
            both = both_ref[pl.ds(2 * place * rows, 2 * rows), pl.ds(first, CODE)]
            powers.append(put_codes(out_ref, both, first))
        put_extra(out_ref, powers, square_refs[place][:, :1])


def encode_parts(both, squares):
    count = len(squares)
    rows, cols = both.shape[0] // count // 2, both.shape[1]
    return pl.pallas_call(
        functools.partial(encode_kernel, count),
        out_shape=[jax.ShapeDtypeStruct((cols // LANES * rows + EXTRA, LANES), i16)] * count,
        compiler_params=params(),
        cost_estimate=pl.CostEstimate(
            flops=20 * count * rows * cols, bytes_accessed=10 * count * rows * cols, transcendentals=count * rows * cols
        ),
        name="encode_parts",
    )(both, *squares)


def product(left, head):
    return jnp.dot(left, head, preferred_element_type=f32)


def side_kernel(width, blocks, own_which, meta_ref, quarter_ref, token_ref, hidden_ref, gain_ref, w_ref, head_ref, near_ref, own_ref, far_ref, left_ref, squares_ref, head_out, held, gain_held, w_held, sum_ref, sem, gain_sem, w_sems, head_sem):
    rows = token_ref.shape[1]
    slots = w_ref.shape[0]
    at = pl.ds(pl.multiple_of(quarter_ref[own_which] * rows, rows), rows)
    hidden_copy = pltpu.make_async_copy(hidden_ref.at[at, :], held, sem)
    gain_copy = pltpu.make_async_copy(gain_ref, gain_held, gain_sem)
    w_copies = [pltpu.make_async_copy(w_ref.at[k], w_held.at[k], w_sems.at[k]) for k in range(slots)]
    gain_copy.start()
    hidden_copy.start()
    for copy in w_copies:
        copy.start()
    head_copy = pltpu.make_async_copy(head_ref, head_out, head_sem)
    head_copy.start()
    shard = meta_ref[1]
    near_at = jnp.where(shard % 2 == 0, 2, 0)
    token = jnp.transpose(jnp.broadcast_to(token_ref[...].astype(f32), (8, rows)))[:, :1].astype(i32)
    place = lax.broadcasted_iota(i32, (rows, width), 1)
    sum_ref[...] = jnp.zeros_like(sum_ref)
    gain_copy.wait()
    hidden_copy.wait()
    squares = prepare(held[...], gain_held[...].astype(f32), left_ref, 0)
    squares_ref[...] = jnp.broadcast_to(squares, (rows, LANES))
    for slot in range(slots):
        w_copies[slot].wait()

        @pl.when(slot < meta_ref[2 + 2 * slots])
        def _():
            source = jnp.clip(meta_ref[2 + slot] - (shard - 1) * blocks, 0, 3 * blocks - 1)
            hits = (token - meta_ref[2 + slots + slot] * width == place).astype(bf16)
            left = jnp.concatenate([hits, jnp.ones((EXTRA, width), bf16)], axis=0)
            found = lax.dot_general(
                left, w_held[slot], (((1,), (1,)), ((), ())), preferred_element_type=f32
            )
            at = pl.ds(pl.multiple_of(source % blocks * width, width), width)
            sum_ref[source // blocks, :, at] += found

    order = lax.broadcasted_iota(i32, (EXTRA, 1), 0)
    for out_ref, k in ((near_ref, near_at), (own_ref, 1), (far_ref, 2 - near_at)):
        out_ref[pl.ds(0, rows), :] = sum_ref[k, pl.ds(0, rows), :].astype(bf16)
        sums = sum_ref[k, pl.ds(rows, EXTRA), :]
        first = sums.astype(bf16).astype(f32)
        second = (sums - first).astype(bf16).astype(f32)
        third = sums - first - second
        parts = jnp.where(order == 0, first, jnp.where(order == 1, second, jnp.where(order == 2, third, 0.0)))
        out_ref[pl.ds(rows, EXTRA), :] = parts.astype(bf16)
    near_ref[pl.ds(rows + EXTRA, EXTRA), :] = jnp.zeros((EXTRA, near_ref.shape[1]), bf16)
    head_copy.wait()


def side_parts(meta, quarters, token, hidden, gain, weights, head, width):
    rows, feats, cols = token.shape[1], hidden.shape[1], head.shape[1]
    smem = pl.BlockSpec(memory_space=pltpu.SMEM)
    hbm = pl.BlockSpec(memory_space=pltpu.HBM)
    outs = pl.pallas_call(
        functools.partial(side_kernel, width, cols // width, 0),
        in_specs=[smem, smem, pl.BlockSpec(memory_space=pltpu.VMEM), hbm, hbm, hbm, hbm],
        out_shape=[jax.ShapeDtypeStruct((rows + many * EXTRA, cols), bf16) for many in (2, 1, 1)]
        + [jax.ShapeDtypeStruct((2 * rows, feats), bf16), jax.ShapeDtypeStruct((rows, LANES), f32)]
        + [jax.ShapeDtypeStruct(head.shape, head.dtype)],
        scratch_shapes=[
            pltpu.VMEM((rows, feats), bf16),
            pltpu.VMEM(gain.shape, bf16),
            pltpu.VMEM(weights.shape, bf16),
            pltpu.VMEM((3, rows + EXTRA, cols), f32),
            pltpu.SemaphoreType.DMA,
            pltpu.SemaphoreType.DMA,
            pltpu.SemaphoreType.DMA((weights.shape[0],)),
            pltpu.SemaphoreType.DMA,
        ],
        compiler_params=params(),
        cost_estimate=pl.CostEstimate(flops=1, bytes_accessed=1, transcendentals=0),
        name="side_parts",
    )(meta, quarters, token, hidden, gain, weights, head)
    return outs[:3], outs[3], outs[4], outs[5]


def extras(ref, rows):
    tile = ref[pl.ds(ref.shape[0] - EXTRA, EXTRA), :].astype(i32).astype(f32)
    wide = jnp.transpose(tile)
    groups = (ref.shape[0] - EXTRA) // rows * LANES // CODE
    at = [wide[:, j : j + 1] for j in range(groups + 3)]
    return at[:groups], decode_scalar(*at[groups:])


def model_logits(mine, features, own_ref, squares_ref, cy_ref, cx_ref, cd_ref, out_ref):
    rows = squares_ref.shape[0]
    cols = own_ref.shape[1]

    def run(scale, at_slab):
        for slab in range(cols // LANES):
            out_ref[:, pl.ds(slab * LANES, LANES)] = at_slab(slab) * scale

    @pl.when(mine)
    def _():
        power_y, squares_y = extras(cy_ref, rows)

        def at_slab(slab):
            at = pl.ds(slab * LANES, LANES)
            own = own_ref[pl.ds(0, rows), at] + own_ref[pl.ds(rows, rows), at]
            return own + decode(cy_ref[pl.ds(slab * rows, rows), :], power_y[slab * LANES // CODE])

        run(lax.rsqrt((squares_ref[:, :1] + squares_y) / features + 1e-05), at_slab)

    @pl.when(jnp.logical_not(mine))
    def _():
        power_x, squares_x = extras(cx_ref, rows)
        power_d, squares_d = extras(cd_ref, rows)

        def at_slab(slab):
            part, group = pl.ds(slab * rows, rows), slab * LANES // CODE
            return decode(cx_ref[part, :], power_x[group]) + decode(cd_ref[part, :], power_d[group])

        run(lax.rsqrt((squares_x + squares_d) / features + 1e-05), at_slab)

    peak = jnp.full((rows, LANES), -jnp.inf, f32)
    for slab in range(cols // LANES):
        peak = jnp.maximum(peak, out_ref[:, pl.ds(slab * LANES, LANES)])
    return jnp.max(peak, axis=1, keepdims=True)


def qwen_kernel(width, blocks, features, meta_ref, own_ref, squares_ref, cy_ref, cx_ref, cd_ref, u_ref, stats_ref, q_ref):
    rows = squares_ref.shape[0]
    body = blocks * width
    peak = model_logits(meta_ref[0] == 1, features, own_ref, squares_ref, cy_ref, cx_ref, cd_ref, q_ref)
    total = jnp.zeros((rows, 1), f32)
    for j in range(blocks):
        at = pl.ds(j * width, width)
        qwen = jnp.exp(q_ref[:, at] - peak)
        u_ref[:, at] = qwen.astype(bf16)
        total += jnp.sum(qwen, axis=1, keepdims=True)
    first = peak.astype(bf16).astype(f32)
    second = (peak - first).astype(bf16).astype(f32)
    third = peak - first - second
    u_ref[:, body:] = columns_to_lanes([first, second, third], rows).astype(bf16)
    stats_ref[...] = columns_to_lanes([peak, total], rows)


def join_qwen(meta, own, squares, codes, width, features):
    rows, cols = own.shape[0] // 2, own.shape[1]
    whole = pl.BlockSpec(memory_space=pltpu.VMEM)
    return pl.pallas_call(
        functools.partial(qwen_kernel, width, cols // width, features),
        in_specs=[pl.BlockSpec(memory_space=pltpu.SMEM)] + [whole] * 5,
        out_shape=[
            jax.ShapeDtypeStruct((rows, cols + LANES), bf16),
            jax.ShapeDtypeStruct((rows, LANES), f32),
        ],
        scratch_shapes=[pltpu.VMEM((rows, cols), f32)],
        compiler_params=params(),
        cost_estimate=pl.CostEstimate(flops=20000000000, bytes_accessed=8 * 1024 * 1024, transcendentals=0),
        name="join_qwen",
    )(meta, own, squares, *codes)


def llama_kernel(width, blocks, features, meta_ref, own_ref, squares_ref, cy_ref, cx_ref, cd_ref, token_ref, u_ref, near_ref, mine_ref, far_ref, before_ref, e_ref, stats_ref):
    rows = squares_ref.shape[0]
    body = blocks * width
    columns_refs = (near_ref, mine_ref, far_ref)
    peak = model_logits(meta_ref[0] == 0, features, own_ref, squares_ref, cy_ref, cx_ref, cd_ref, e_ref)
    total = jnp.zeros((rows, 1), f32)
    mass = jnp.zeros((rows, 1), f32)
    pick_e = jnp.zeros((rows, 1), f32)
    pick_m = jnp.zeros((rows, 1), f32)
    token = jnp.transpose(jnp.broadcast_to(token_ref[...].astype(f32), (8, rows)))
    token = token[:, :1].astype(i32) - meta_ref[1] * body
    for j in range(blocks):
        at = pl.ds(j * width, width)
        llama = jnp.exp(e_ref[:, at] - peak)
        e_ref[:, at] = llama
        total += jnp.sum(llama, axis=1, keepdims=True)
        hit = lax.broadcasted_iota(i32, (rows, width), 1) + j * width == token
        pick_e += jnp.sum(jnp.where(hit, llama, 0.0), axis=1, keepdims=True)
        held = u_ref[:, at].astype(f32)
        columns = functools.reduce(jnp.add, [ref[pl.ds(0, rows), at].astype(f32) for ref in columns_refs])
        pick_m += jnp.sum(held * columns, axis=1, keepdims=True)
        sums = functools.reduce(jnp.add, [ref[pl.ds(rows, EXTRA), at].astype(f32) for ref in columns_refs])
        mass += jnp.sum(held * jnp.sum(sums, axis=0, keepdims=True), axis=1, keepdims=True)
    before = before_ref[...]
    stats = columns_to_lanes([peak, total, before[:, 0:1], before[:, 1:2], mass, pick_e, pick_m], rows)
    stats_ref[...] = jnp.transpose(stats)[:8]


def join_llama(meta, own, squares, codes, token, u, columns, stats, width, features):
    rows, cols = own.shape[0] // 2, own.shape[1]
    whole = pl.BlockSpec(memory_space=pltpu.VMEM)
    return pl.pallas_call(
        functools.partial(llama_kernel, width, cols // width, features),
        in_specs=[pl.BlockSpec(memory_space=pltpu.SMEM)] + [whole] * 11,
        out_shape=[jax.ShapeDtypeStruct((rows, cols), f32), jax.ShapeDtypeStruct((8, rows), f32)],
        compiler_params=params(),
        cost_estimate=pl.CostEstimate(flops=20000000000, bytes_accessed=8 * 1024 * 1024, transcendentals=0),
        name="join_llama",
    )(meta, own, squares, *codes, token, u, *columns, stats)


def map_kernel(width, blocks, shards, meta_ref, u_ref, near_ref, far_ref, w_ref, m_ref, top_ref, all_ref, scale_ref):
    rows = u_ref.shape[0]
    body = blocks * width
    shard = meta_ref[1]
    slots = w_ref.shape[0]
    near_at = jnp.where(shard % 2 == 0, 2, 0)

    def peak_of(ref):
        lanes = ref[:, body:].astype(f32)
        return lanes[:, 0:1] + lanes[:, 1:2] + lanes[:, 2:3]

    own_peak = peak_of(u_ref)
    near_peak = peak_of(near_ref)
    far_peak = jnp.where((shard > 0) & (shard < shards - 1), peak_of(far_ref), own_peak)
    top = jnp.maximum(jnp.maximum(near_peak, far_peak), own_peak)
    for k, ref, peak in ((near_at, near_ref, near_peak), (1, u_ref, own_peak), (2 - near_at, far_ref, far_peak)):
        all_ref[k] = ref[:, :body]
        scale_ref[k] = jnp.broadcast_to(jnp.exp(peak - top), (rows, LANES))
    m_ref[...] = jnp.zeros_like(m_ref)
    for slot in range(slots):

        @pl.when(slot < meta_ref[2 + 2 * slots])
        def _():
            source = jnp.clip(meta_ref[2 + slot] - (shard - 1) * blocks, 0, 3 * blocks - 1)
            target = jnp.clip(meta_ref[2 + slots + slot] - shard * blocks, 0, blocks - 1)
            inside = pl.multiple_of(source % blocks * width, width)
            picked = all_ref[source // blocks, :, pl.ds(inside, width)]
            term = jnp.dot(picked, w_ref[slot], preferred_element_type=f32)
            at = pl.ds(pl.multiple_of(target * width, width), width)
            m_ref[:, at] += term * scale_ref[source // blocks][:, :1]

    top_ref[...] = jnp.broadcast_to(top, (rows, LANES))


def map_parts(meta, u, near, far, weights, width, shards):
    rows, cols = u.shape[0], u.shape[1] - LANES
    blocks = cols // width
    whole = pl.BlockSpec(memory_space=pltpu.VMEM)
    return pl.pallas_call(
        functools.partial(map_kernel, width, blocks, shards),
        in_specs=[pl.BlockSpec(memory_space=pltpu.SMEM)] + [whole] * 4,
        out_shape=[jax.ShapeDtypeStruct((rows, cols), f32), jax.ShapeDtypeStruct((rows, LANES), f32)],
        scratch_shapes=[pltpu.VMEM((3, rows, cols), bf16), pltpu.VMEM((3, rows, LANES), f32)],
        compiler_params=params(),
        cost_estimate=pl.CostEstimate(
            flops=2 * rows * weights.size, bytes_accessed=2 * weights.size, transcendentals=0
        ),
        name="map_parts",
    )(meta, u, near, far, weights)


def finish_kernel(pieces, *refs):
    stats_refs, (e_ref, m_ref, m_top_ref, out_ref, nll_ref) = refs[:pieces], refs[pieces:]
    stats = [ref[k : k + 8, :] for ref in stats_refs for k in range(0, ref.shape[0], 8)]
    shards = range(len(stats))
    row = lambda s, k: stats[s][k : k + 1, :]
    top_l = functools.reduce(jnp.maximum, [row(s, 0) for s in shards])
    top_q = functools.reduce(jnp.maximum, [row(s, 2) for s in shards])
    sum_l = functools.reduce(jnp.add, [row(s, 1) * jnp.exp(row(s, 0) - top_l) for s in shards])
    sum_q = functools.reduce(jnp.add, [row(s, 3) * jnp.exp(row(s, 2) - top_q) for s in shards])
    part_l = [jnp.exp(row(s, 0) - top_l) / sum_l for s in shards]
    part_q = [jnp.exp(row(s, 2) - top_q) / sum_q for s in shards]
    mass = functools.reduce(jnp.add, [row(s, 4) * part_q[s] for s in shards])
    pick_e = functools.reduce(jnp.add, [row(s, 5) * part_l[s] for s in shards])
    pick_m = functools.reduce(jnp.add, [row(s, 6) * part_q[s] for s in shards])
    log_norm = jnp.log1p(mass)
    nll_ref[...] = log_norm - jnp.log(jnp.maximum(pick_e, FLOOR) + pick_m)
    tile = jnp.concatenate([part_l[0], top_q, 1.0 / sum_q, log_norm, jnp.zeros((4, log_norm.shape[1]), f32)], axis=0)
    turned = jnp.transpose(tile)
    a, top, share, c = (turned[:, i : i + 1] for i in range(4))
    b = jnp.exp(m_top_ref[:, :1] - top) * share
    out_ref[...] = jnp.log(jnp.maximum(e_ref[...] * a, FLOOR) + m_ref[...] * b) - c


def finish(pieces, e, m, m_top):
    rows, cols = e.shape
    return pl.pallas_call(
        functools.partial(finish_kernel, len(pieces)),
        out_shape=[
            jax.ShapeDtypeStruct((rows, cols), f32),
            jax.ShapeDtypeStruct((1, rows), f32),
        ],
        compiler_params=params(),
        cost_estimate=pl.CostEstimate(
            flops=20 * rows * cols, bytes_accessed=12 * rows * cols, transcendentals=2 * rows * cols
        ),
        name="finish",
    )(*pieces, e, m, m_top)


def gather_pieces(own, shards):
    pieces, step = [own], 1
    while step < shards:
        radix = 4 if step > 1 and 4 * step <= shards else 2
        sent = pieces[0] if len(pieces) == 1 else jnp.concatenate(pieces, axis=0)
        for turn in range(1, radix):
            pieces.append(lax.ppermute(sent, "vocab", [(i, i ^ (turn * step)) for i in range(shards)]))
        step *= radix
    return pieces, sent


def on_device(
    hidden, norm_gain, head_weights, pair_source, pair_target, pair_count, pair_weight, next_token
):
    shards = lax.axis_size("vocab")
    row_groups = lax.axis_size("rows")
    hidden, head = hidden[0], head_weights[0]
    token = next_token[None, :]
    held_hidden = pltpu.with_memory_space_constraint(hidden, pltpu.HBM)
    held_weight = pltpu.with_memory_space_constraint(pair_weight, pltpu.HBM)
    held_gain = pltpu.with_memory_space_constraint(norm_gain, pltpu.HBM)
    held_head = pltpu.with_memory_space_constraint(head, pltpu.HBM)
    width = pair_weight.shape[1]
    features = hidden.shape[1] * row_groups
    model, shard, side = (lax.axis_index(name).astype(i32) for name in ("mp", "vocab", "rows"))
    mine = 2 * model + side
    quarters = jnp.stack([mine, mine ^ 1, mine ^ 2, mine ^ 3])
    meta = jnp.concatenate([jnp.stack([model, shard]), pair_source, pair_target, pair_count])

    inside = [(i, i ^ 1) for i in range(shards)]
    across = [(i, i + 1 if i % 2 else i - 1) for i in range(1, shards - 1)]
    lefts, squares, head = first_prep(quarters, held_hidden, held_gain, held_head, (3, 1, 2))
    (to_d,) = encode_parts(product(lefts[0], head), squares[:1])
    from_d = lax.ppermute(to_d, ("mp", "rows"), [(0, 3), (1, 2), (2, 1), (3, 0)])
    left_y, _ = lax.optimization_barrier((lefts[1], to_d))
    (to_y,) = encode_parts(product(left_y, head), squares[1:2])
    from_y = lax.ppermute(to_y, "rows", [(0, 1), (1, 0)])
    left_x, _ = lax.optimization_barrier((lefts[2], to_y))
    (to_x,) = encode_parts(product(left_x, head), squares[2:])
    from_x = lax.ppermute(to_x, "mp", [(0, 1), (1, 0)])
    early, _ = lax.optimization_barrier((meta, to_x))
    (to_near, columns, to_far), left_own, squares_own, head = side_parts(
        early, quarters, token, held_hidden, held_gain, held_weight, held_head, width
    )
    own = product(left_own, head)
    to_near, _ = lax.optimization_barrier((to_near, own))
    near_columns = lax.ppermute(to_near, "vocab", inside)
    far_columns = lax.ppermute(to_far, "vocab", across)

    codes = (from_y, from_x, from_d)
    u, stats = join_qwen(meta, own, squares_own, codes, width, features)
    far = lax.ppermute(u, "vocab", across)
    e, stats = join_llama(
        meta, own, squares_own, codes, token, u, (near_columns, columns, far_columns), stats, width, features
    )
    pieces, last = gather_pieces(stats, shards)
    late_u, _ = lax.optimization_barrier((u, last))
    near = lax.ppermute(late_u, "vocab", inside)
    m, m_top = map_parts(meta, u, near, far, pair_weight, width, shards)
    out, nll = finish(pieces, e, m, m_top)
    return out, nll[0]


def solution(mesh):
    in_specs = (
        P("mp", None, "rows"),
        P("mp", "rows"),
        P("mp", "rows", "vocab"),
        P("vocab"),
        P("vocab"),
        P("vocab"),
        P("vocab", None, None),
        P(("mp", "rows")),
    )
    out_specs = (P(("mp", "rows"), "vocab"), P(("mp", "rows")))
    return jax.shard_map(
        on_device, mesh=mesh, in_specs=in_specs, out_specs=out_specs, check_vma=False
    )
```

```python
import functools

import jax
import jax.numpy as jnp
from jax import lax
from jax.experimental import pallas as pl
from jax.experimental.pallas import tpu as pltpu
from jax.sharding import PartitionSpec as P

LANES = 128
EXTRA = 16
CODE = 512
HEAD_COPIES = 1
TOP = 32700.0
ROUNDER = 12582912.0
LEAST = 1e-30
FLOOR = 1.9287498479639178e-22
VMEM = 16 * 1024 * 1024

f32, bf16, i32, i16 = jnp.float32, jnp.bfloat16, jnp.int32, jnp.int16


def params():
    return pltpu.CompilerParams(vmem_limit_bytes=VMEM)


def exponent(value):
    return jnp.ceil(jnp.log2(jnp.maximum(value, LEAST)))


def columns_to_lanes(values, rows):
    lanes = lax.broadcasted_iota(i32, (rows, LANES), 1)
    out = jnp.zeros((rows, LANES), f32)
    for place, value in enumerate(values):
        out = jnp.where(lanes == place, value, out)
    return out


def split_exact(gained):
    high = gained.astype(bf16)
    return high, (gained - high.astype(f32)).astype(bf16)


def encode(values, power):
    wide = values * (jnp.exp2(-power) * (TOP * TOP))
    root = wide * lax.rsqrt(jnp.maximum(jnp.abs(wide), LEAST))
    return ((root + ROUNDER) - ROUNDER).astype(i32).astype(i16)


def decode(codes, power):
    wide = codes.astype(i32).astype(f32)
    return wide * jnp.abs(wide) * (jnp.exp2(power) * (1.0 / (TOP * TOP)))


def encode_scalar(value):
    power = exponent(value)
    mantissa = jnp.maximum(value, LEAST) * jnp.exp2(-power) * 16384.0
    first = jnp.floor(mantissa)
    return power, first, jnp.floor((mantissa - first) * 16384.0)


def decode_scalar(power, first, second):
    return (first + second * (1.0 / 16384.0)) * (1.0 / 16384.0) * jnp.exp2(power)


def prepare(hidden, gain, left_ref, at):
    rows = hidden.shape[0]
    values = hidden.astype(f32)
    high, low = split_exact(values * gain)
    left_ref[pl.ds(at, rows), :] = high
    left_ref[pl.ds(at + rows, rows), :] = low
    return jnp.sum(values * values, axis=1, keepdims=True)


def put_codes(out_ref, both, first):
    rows = both.shape[0] // 2
    part = both[:rows] + both[rows:]
    power = exponent(jnp.max(jnp.abs(part), axis=1, keepdims=True))
    codes = encode(part, power)
    for k in range(part.shape[1] // LANES):
        out_ref[pl.ds((first // LANES + k) * rows, rows), :] = codes[:, k * LANES : (k + 1) * LANES]
    return power


def put_extra(out_ref, powers, squares):
    rows = squares.shape[0]
    extra = columns_to_lanes(powers + list(encode_scalar(squares)), rows)
    body = out_ref.shape[0] - EXTRA
    out_ref[pl.ds(body, EXTRA), :] = jnp.transpose(extra)[:EXTRA].astype(i32).astype(i16)


def first_kernel(kinds, rows, quarter_ref, hidden_ref, gain_ref, head_ref, *refs):
    count = len(kinds)
    left_refs, square_refs, head_out = refs[:count], refs[count : 2 * count], refs[2 * count]
    held, gain_held, sems, gain_sem, head_sems = refs[2 * count + 1 :]
    copies = []
    for place, which in enumerate(kinds):
        at = pl.ds(pl.multiple_of(quarter_ref[which] * rows, rows), rows)
        copies.append(pltpu.make_async_copy(hidden_ref.at[at, :], held.at[place], sems.at[place]))
    gain_copy = pltpu.make_async_copy(gain_ref, gain_held, gain_sem)
    deep = head_ref.shape[0] // HEAD_COPIES
    spans = [pl.ds(k * deep, deep) for k in range(HEAD_COPIES)]
    head_copies = [
        pltpu.make_async_copy(head_ref.at[at, :], head_out.at[at, :], head_sems.at[k])
        for k, at in enumerate(spans)
    ]
    gain_copy.start()
    for copy in copies + head_copies:
        copy.start()
    gain_copy.wait()
    gain = gain_held[...].astype(f32)
    for place, copy in enumerate(copies):
        copy.wait()
        squares = prepare(held[place], gain, left_refs[place], 0)
        square_refs[place][...] = jnp.broadcast_to(squares, (rows, LANES))
    for copy in head_copies:
        copy.wait()


def first_prep(quarters, hidden, gain, head, kinds):
    rows, feats, count = hidden.shape[0] // 4, hidden.shape[1], len(kinds)
    hbm = pl.BlockSpec(memory_space=pltpu.HBM)
    outs = pl.pallas_call(
        functools.partial(first_kernel, kinds, rows),
        in_specs=[pl.BlockSpec(memory_space=pltpu.SMEM), hbm, hbm, hbm],
        out_shape=[jax.ShapeDtypeStruct((2 * rows, feats), bf16)] * count
        + [jax.ShapeDtypeStruct((rows, LANES), f32)] * count
        + [jax.ShapeDtypeStruct(head.shape, head.dtype)],
        scratch_shapes=[
            pltpu.VMEM((count, rows, feats), bf16),
            pltpu.VMEM(gain.shape, bf16),
            pltpu.SemaphoreType.DMA((count,)),
            pltpu.SemaphoreType.DMA,
            pltpu.SemaphoreType.DMA((HEAD_COPIES,)),
        ],
        compiler_params=params(),
        cost_estimate=pl.CostEstimate(
            flops=8 * count * rows * feats, bytes_accessed=2 * head.size, transcendentals=0
        ),
        name="first_prep",
    )(quarters, hidden, gain, head)
    return outs[:count], outs[count : 2 * count], outs[2 * count]


def encode_kernel(count, both_ref, *refs):
    square_refs, outs = refs[:count], refs[count:]
    rows, cols = both_ref.shape[0] // count // 2, both_ref.shape[1]
    for place, out_ref in enumerate(outs):
        powers = []
        for first in range(0, cols, CODE):
            both = both_ref[pl.ds(2 * place * rows, 2 * rows), pl.ds(first, CODE)]
            powers.append(put_codes(out_ref, both, first))
        put_extra(out_ref, powers, square_refs[place][:, :1])


def encode_parts(both, squares):
    count = len(squares)
    rows, cols = both.shape[0] // count // 2, both.shape[1]
    return pl.pallas_call(
        functools.partial(encode_kernel, count),
        out_shape=[jax.ShapeDtypeStruct((cols // LANES * rows + EXTRA, LANES), i16)] * count,
        compiler_params=params(),
        cost_estimate=pl.CostEstimate(
            flops=20 * count * rows * cols, bytes_accessed=10 * count * rows * cols, transcendentals=count * rows * cols
        ),
        name="encode_parts",
    )(both, *squares)


def product(left, head):
    return jnp.dot(left, head, preferred_element_type=f32)


def side_kernel(width, blocks, own_which, meta_ref, quarter_ref, token_ref, hidden_ref, gain_ref, w_ref, head_ref, near_ref, own_ref, far_ref, left_ref, squares_ref, head_out, held, gain_held, w_held, sum_ref, sem, gain_sem, w_sems, head_sem):
    rows = token_ref.shape[1]
    slots = w_ref.shape[0]
    at = pl.ds(pl.multiple_of(quarter_ref[own_which] * rows, rows), rows)
    hidden_copy = pltpu.make_async_copy(hidden_ref.at[at, :], held, sem)
    gain_copy = pltpu.make_async_copy(gain_ref, gain_held, gain_sem)
    w_copies = [pltpu.make_async_copy(w_ref.at[k], w_held.at[k], w_sems.at[k]) for k in range(slots)]
    gain_copy.start()
    hidden_copy.start()
    for copy in w_copies:
        copy.start()
    head_copy = pltpu.make_async_copy(head_ref, head_out, head_sem)
    head_copy.start()
    shard = meta_ref[1]
    near_at = jnp.where(shard % 2 == 0, 2, 0)
    token = jnp.transpose(jnp.broadcast_to(token_ref[...].astype(f32), (8, rows)))[:, :1].astype(i32)
    place = lax.broadcasted_iota(i32, (rows, width), 1)
    sum_ref[...] = jnp.zeros_like(sum_ref)
    gain_copy.wait()
    hidden_copy.wait()
    squares = prepare(held[...], gain_held[...].astype(f32), left_ref, 0)
    squares_ref[...] = jnp.broadcast_to(squares, (rows, LANES))
    for slot in range(slots):
        w_copies[slot].wait()

        @pl.when(slot < meta_ref[2 + 2 * slots])
        def _():
            source = jnp.clip(meta_ref[2 + slot] - (shard - 1) * blocks, 0, 3 * blocks - 1)
            hits = (token - meta_ref[2 + slots + slot] * width == place).astype(bf16)
            left = jnp.concatenate([hits, jnp.ones((EXTRA, width), bf16)], axis=0)
            found = lax.dot_general(
                left, w_held[slot], (((1,), (1,)), ((), ())), preferred_element_type=f32
            )
            at = pl.ds(pl.multiple_of(source % blocks * width, width), width)
            sum_ref[source // blocks, :, at] += found

    order = lax.broadcasted_iota(i32, (EXTRA, 1), 0)
    for out_ref, k in ((near_ref, near_at), (own_ref, 1), (far_ref, 2 - near_at)):
        out_ref[pl.ds(0, rows), :] = sum_ref[k, pl.ds(0, rows), :].astype(bf16)
        sums = sum_ref[k, pl.ds(rows, EXTRA), :]
        first = sums.astype(bf16).astype(f32)
        second = (sums - first).astype(bf16).astype(f32)
        third = sums - first - second
        parts = jnp.where(order == 0, first, jnp.where(order == 1, second, jnp.where(order == 2, third, 0.0)))
        out_ref[pl.ds(rows, EXTRA), :] = parts.astype(bf16)
    near_ref[pl.ds(rows + EXTRA, EXTRA), :] = jnp.zeros((EXTRA, near_ref.shape[1]), bf16)
    head_copy.wait()


def side_parts(meta, quarters, token, hidden, gain, weights, head, width):
    rows, feats, cols = token.shape[1], hidden.shape[1], head.shape[1]
    smem = pl.BlockSpec(memory_space=pltpu.SMEM)
    hbm = pl.BlockSpec(memory_space=pltpu.HBM)
    outs = pl.pallas_call(
        functools.partial(side_kernel, width, cols // width, 0),
        in_specs=[smem, smem, pl.BlockSpec(memory_space=pltpu.VMEM), hbm, hbm, hbm, hbm],
        out_shape=[jax.ShapeDtypeStruct((rows + many * EXTRA, cols), bf16) for many in (2, 1, 1)]
        + [jax.ShapeDtypeStruct((2 * rows, feats), bf16), jax.ShapeDtypeStruct((rows, LANES), f32)]
        + [jax.ShapeDtypeStruct(head.shape, head.dtype)],
        scratch_shapes=[
            pltpu.VMEM((rows, feats), bf16),
            pltpu.VMEM(gain.shape, bf16),
            pltpu.VMEM(weights.shape, bf16),
            pltpu.VMEM((3, rows + EXTRA, cols), f32),
            pltpu.SemaphoreType.DMA,
            pltpu.SemaphoreType.DMA,
            pltpu.SemaphoreType.DMA((weights.shape[0],)),
            pltpu.SemaphoreType.DMA,
        ],
        compiler_params=params(),
        cost_estimate=pl.CostEstimate(flops=1, bytes_accessed=1, transcendentals=0),
        name="side_parts",
    )(meta, quarters, token, hidden, gain, weights, head)
    return outs[:3], outs[3], outs[4], outs[5]


def extras(ref, rows):
    tile = ref[pl.ds(ref.shape[0] - EXTRA, EXTRA), :].astype(i32).astype(f32)
    wide = jnp.transpose(tile)
    groups = (ref.shape[0] - EXTRA) // rows * LANES // CODE
    at = [wide[:, j : j + 1] for j in range(groups + 3)]
    return at[:groups], decode_scalar(*at[groups:])


def model_logits(mine, features, own_ref, squares_ref, cy_ref, cx_ref, cd_ref, out_ref):
    rows = squares_ref.shape[0]
    cols = own_ref.shape[1]

    def run(scale, at_slab):
        for slab in range(cols // LANES):
            out_ref[:, pl.ds(slab * LANES, LANES)] = at_slab(slab) * scale

    @pl.when(mine)
    def _():
        power_y, squares_y = extras(cy_ref, rows)

        def at_slab(slab):
            at = pl.ds(slab * LANES, LANES)
            own = own_ref[pl.ds(0, rows), at] + own_ref[pl.ds(rows, rows), at]
            return own + decode(cy_ref[pl.ds(slab * rows, rows), :], power_y[slab * LANES // CODE])

        run(lax.rsqrt((squares_ref[:, :1] + squares_y) / features + 1e-05), at_slab)

    @pl.when(jnp.logical_not(mine))
    def _():
        power_x, squares_x = extras(cx_ref, rows)
        power_d, squares_d = extras(cd_ref, rows)

        def at_slab(slab):
            part, group = pl.ds(slab * rows, rows), slab * LANES // CODE
            return decode(cx_ref[part, :], power_x[group]) + decode(cd_ref[part, :], power_d[group])

        run(lax.rsqrt((squares_x + squares_d) / features + 1e-05), at_slab)

    peak = jnp.full((rows, LANES), -jnp.inf, f32)
    for slab in range(cols // LANES):
        peak = jnp.maximum(peak, out_ref[:, pl.ds(slab * LANES, LANES)])
    return jnp.max(peak, axis=1, keepdims=True)


def qwen_kernel(width, blocks, features, meta_ref, own_ref, squares_ref, cy_ref, cx_ref, cd_ref, u_ref, stats_ref, q_ref):
    rows = squares_ref.shape[0]
    body = blocks * width
    peak = model_logits(meta_ref[0] == 1, features, own_ref, squares_ref, cy_ref, cx_ref, cd_ref, q_ref)
    total = jnp.zeros((rows, 1), f32)
    for j in range(blocks):
        at = pl.ds(j * width, width)
        qwen = jnp.exp(q_ref[:, at] - peak)
        u_ref[:, at] = qwen.astype(bf16)
        total += jnp.sum(qwen, axis=1, keepdims=True)
    first = peak.astype(bf16).astype(f32)
    second = (peak - first).astype(bf16).astype(f32)
    third = peak - first - second
    u_ref[:, body:] = columns_to_lanes([first, second, third], rows).astype(bf16)
    stats_ref[...] = columns_to_lanes([peak, total], rows)


def join_qwen(meta, own, squares, codes, width, features):
    rows, cols = own.shape[0] // 2, own.shape[1]
    whole = pl.BlockSpec(memory_space=pltpu.VMEM)
    return pl.pallas_call(
        functools.partial(qwen_kernel, width, cols // width, features),
        in_specs=[pl.BlockSpec(memory_space=pltpu.SMEM)] + [whole] * 5,
        out_shape=[
            jax.ShapeDtypeStruct((rows, cols + LANES), bf16),
            jax.ShapeDtypeStruct((rows, LANES), f32),
        ],
        scratch_shapes=[pltpu.VMEM((rows, cols), f32)],
        compiler_params=params(),
        cost_estimate=pl.CostEstimate(flops=20000000000, bytes_accessed=8 * 1024 * 1024, transcendentals=0),
        name="join_qwen",
    )(meta, own, squares, *codes)


def llama_kernel(width, blocks, features, meta_ref, own_ref, squares_ref, cy_ref, cx_ref, cd_ref, token_ref, u_ref, near_ref, mine_ref, far_ref, before_ref, e_ref, stats_ref):
    rows = squares_ref.shape[0]
    body = blocks * width
    columns_refs = (near_ref, mine_ref, far_ref)
    peak = model_logits(meta_ref[0] == 0, features, own_ref, squares_ref, cy_ref, cx_ref, cd_ref, e_ref)
    total = jnp.zeros((rows, 1), f32)
    mass = jnp.zeros((rows, 1), f32)
    pick_e = jnp.zeros((rows, 1), f32)
    pick_m = jnp.zeros((rows, 1), f32)
    token = jnp.transpose(jnp.broadcast_to(token_ref[...].astype(f32), (8, rows)))
    token = token[:, :1].astype(i32) - meta_ref[1] * body
    for j in range(blocks):
        at = pl.ds(j * width, width)
        llama = jnp.exp(e_ref[:, at] - peak)
        e_ref[:, at] = llama
        total += jnp.sum(llama, axis=1, keepdims=True)
        hit = lax.broadcasted_iota(i32, (rows, width), 1) + j * width == token
        pick_e += jnp.sum(jnp.where(hit, llama, 0.0), axis=1, keepdims=True)
        held = u_ref[:, at].astype(f32)
        columns = functools.reduce(jnp.add, [ref[pl.ds(0, rows), at].astype(f32) for ref in columns_refs])
        pick_m += jnp.sum(held * columns, axis=1, keepdims=True)
        sums = functools.reduce(jnp.add, [ref[pl.ds(rows, EXTRA), at].astype(f32) for ref in columns_refs])
        mass += jnp.sum(held * jnp.sum(sums, axis=0, keepdims=True), axis=1, keepdims=True)
    before = before_ref[...]
    stats = columns_to_lanes([peak, total, before[:, 0:1], before[:, 1:2], mass, pick_e, pick_m], rows)
    stats_ref[...] = jnp.transpose(stats)[:8]


def join_llama(meta, own, squares, codes, token, u, columns, stats, width, features):
    rows, cols = own.shape[0] // 2, own.shape[1]
    whole = pl.BlockSpec(memory_space=pltpu.VMEM)
    return pl.pallas_call(
        functools.partial(llama_kernel, width, cols // width, features),
        in_specs=[pl.BlockSpec(memory_space=pltpu.SMEM)] + [whole] * 11,
        out_shape=[jax.ShapeDtypeStruct((rows, cols), f32), jax.ShapeDtypeStruct((8, rows), f32)],
        compiler_params=params(),
        cost_estimate=pl.CostEstimate(flops=20000000000, bytes_accessed=8 * 1024 * 1024, transcendentals=0),
        name="join_llama",
    )(meta, own, squares, *codes, token, u, *columns, stats)


def map_kernel(width, blocks, shards, meta_ref, u_ref, near_ref, far_ref, w_ref, m_ref, top_ref, all_ref, scale_ref):
    rows = u_ref.shape[0]
    body = blocks * width
    shard = meta_ref[1]
    slots = w_ref.shape[0]
    near_at = jnp.where(shard % 2 == 0, 2, 0)

    def peak_of(ref):
        lanes = ref[:, body:].astype(f32)
        return lanes[:, 0:1] + lanes[:, 1:2] + lanes[:, 2:3]

    own_peak = peak_of(u_ref)
    near_peak = peak_of(near_ref)
    far_peak = jnp.where((shard > 0) & (shard < shards - 1), peak_of(far_ref), own_peak)
    top = jnp.maximum(jnp.maximum(near_peak, far_peak), own_peak)
    for k, ref, peak in ((near_at, near_ref, near_peak), (1, u_ref, own_peak), (2 - near_at, far_ref, far_peak)):
        all_ref[k] = ref[:, :body]
        scale_ref[k] = jnp.broadcast_to(jnp.exp(peak - top), (rows, LANES))
    m_ref[...] = jnp.zeros_like(m_ref)
    for slot in range(slots):

        @pl.when(slot < meta_ref[2 + 2 * slots])
        def _():
            source = jnp.clip(meta_ref[2 + slot] - (shard - 1) * blocks, 0, 3 * blocks - 1)
            target = jnp.clip(meta_ref[2 + slots + slot] - shard * blocks, 0, blocks - 1)
            inside = pl.multiple_of(source % blocks * width, width)
            picked = all_ref[source // blocks, :, pl.ds(inside, width)]
            term = jnp.dot(picked, w_ref[slot], preferred_element_type=f32)
            at = pl.ds(pl.multiple_of(target * width, width), width)
            m_ref[:, at] += term * scale_ref[source // blocks][:, :1]

    top_ref[...] = jnp.broadcast_to(top, (rows, LANES))


def map_parts(meta, u, near, far, weights, width, shards):
    rows, cols = u.shape[0], u.shape[1] - LANES
    blocks = cols // width
    whole = pl.BlockSpec(memory_space=pltpu.VMEM)
    return pl.pallas_call(
        functools.partial(map_kernel, width, blocks, shards),
        in_specs=[pl.BlockSpec(memory_space=pltpu.SMEM)] + [whole] * 4,
        out_shape=[jax.ShapeDtypeStruct((rows, cols), f32), jax.ShapeDtypeStruct((rows, LANES), f32)],
        scratch_shapes=[pltpu.VMEM((3, rows, cols), bf16), pltpu.VMEM((3, rows, LANES), f32)],
        compiler_params=params(),
        cost_estimate=pl.CostEstimate(
            flops=2 * rows * weights.size, bytes_accessed=2 * weights.size, transcendentals=0
        ),
        name="map_parts",
    )(meta, u, near, far, weights)


def finish_kernel(pieces, *refs):
    stats_refs, (e_ref, m_ref, m_top_ref, out_ref, nll_ref) = refs[:pieces], refs[pieces:]
    stats = [ref[k : k + 8, :] for ref in stats_refs for k in range(0, ref.shape[0], 8)]
    shards = range(len(stats))
    row = lambda s, k: stats[s][k : k + 1, :]
    top_l = functools.reduce(jnp.maximum, [row(s, 0) for s in shards])
    top_q = functools.reduce(jnp.maximum, [row(s, 2) for s in shards])
    sum_l = functools.reduce(jnp.add, [row(s, 1) * jnp.exp(row(s, 0) - top_l) for s in shards])
    sum_q = functools.reduce(jnp.add, [row(s, 3) * jnp.exp(row(s, 2) - top_q) for s in shards])
    part_l = [jnp.exp(row(s, 0) - top_l) / sum_l for s in shards]
    part_q = [jnp.exp(row(s, 2) - top_q) / sum_q for s in shards]
    mass = functools.reduce(jnp.add, [row(s, 4) * part_q[s] for s in shards])
    pick_e = functools.reduce(jnp.add, [row(s, 5) * part_l[s] for s in shards])
    pick_m = functools.reduce(jnp.add, [row(s, 6) * part_q[s] for s in shards])
    log_norm = jnp.log1p(mass)
    nll_ref[...] = log_norm - jnp.log(jnp.maximum(pick_e, FLOOR) + pick_m)
    tile = jnp.concatenate([part_l[0], top_q, 1.0 / sum_q, log_norm, jnp.zeros((4, log_norm.shape[1]), f32)], axis=0)
    turned = jnp.transpose(tile)
    a, top, share, c = (turned[:, i : i + 1] for i in range(4))
    b = jnp.exp(m_top_ref[:, :1] - top) * share
    out_ref[...] = jnp.log(jnp.maximum(e_ref[...] * a, FLOOR) + m_ref[...] * b) - c


def finish(pieces, e, m, m_top):
    rows, cols = e.shape
    return pl.pallas_call(
        functools.partial(finish_kernel, len(pieces)),
        out_shape=[
            jax.ShapeDtypeStruct((rows, cols), f32),
            jax.ShapeDtypeStruct((1, rows), f32),
        ],
        compiler_params=params(),
        cost_estimate=pl.CostEstimate(
            flops=20 * rows * cols, bytes_accessed=12 * rows * cols, transcendentals=2 * rows * cols
        ),
        name="finish",
    )(*pieces, e, m, m_top)


def gather_pieces(own, shards):
    pieces, step = [own], 1
    while step < shards:
        radix = 4 if step > 1 and 4 * step <= shards else 2
        sent = pieces[0] if len(pieces) == 1 else jnp.concatenate(pieces, axis=0)
        for turn in range(1, radix):
            pieces.append(lax.ppermute(sent, "vocab", [(i, i ^ (turn * step)) for i in range(shards)]))
        step *= radix
    return pieces, sent


def on_device(
    hidden, norm_gain, head_weights, pair_source, pair_target, pair_count, pair_weight, next_token
):
    shards = lax.axis_size("vocab")
    row_groups = lax.axis_size("rows")
    hidden, head = hidden[0], head_weights[0]
    token = next_token[None, :]
    held_hidden = pltpu.with_memory_space_constraint(hidden, pltpu.HBM)
    held_weight = pltpu.with_memory_space_constraint(pair_weight, pltpu.HBM)
    held_gain = pltpu.with_memory_space_constraint(norm_gain, pltpu.HBM)
    held_head = pltpu.with_memory_space_constraint(head, pltpu.HBM)
    width = pair_weight.shape[1]
    features = hidden.shape[1] * row_groups
    model, shard, side = (lax.axis_index(name).astype(i32) for name in ("mp", "vocab", "rows"))
    mine = 2 * model + side
    quarters = jnp.stack([mine, mine ^ 1, mine ^ 2, mine ^ 3])
    meta = jnp.concatenate([jnp.stack([model, shard]), pair_source, pair_target, pair_count])

    inside = [(i, i ^ 1) for i in range(shards)]
    across = [(i, i + 1 if i % 2 else i - 1) for i in range(1, shards - 1)]
    lefts, squares, head = first_prep(quarters, held_hidden, held_gain, held_head, (3, 1, 2))
    (to_d,) = encode_parts(product(lefts[0], head), squares[:1])
    from_d = lax.ppermute(to_d, ("mp", "rows"), [(0, 3), (1, 2), (2, 1), (3, 0)])
    left_y, _ = lax.optimization_barrier((lefts[1], to_d))
    (to_y,) = encode_parts(product(left_y, head), squares[1:2])
    from_y = lax.ppermute(to_y, "rows", [(0, 1), (1, 0)])
    left_x, _ = lax.optimization_barrier((lefts[2], to_y))
    (to_x,) = encode_parts(product(left_x, head), squares[2:])
    from_x = lax.ppermute(to_x, "mp", [(0, 1), (1, 0)])
    early, _ = lax.optimization_barrier((meta, to_x))
    (to_near, columns, to_far), left_own, squares_own, head = side_parts(
        early, quarters, token, held_hidden, held_gain, held_weight, held_head, width
    )
    own = product(left_own, head)
    to_near, _ = lax.optimization_barrier((to_near, own))
    near_columns = lax.ppermute(to_near, "vocab", inside)
    far_columns = lax.ppermute(to_far, "vocab", across)

    codes = (from_y, from_x, from_d)
    u, stats = join_qwen(meta, own, squares_own, codes, width, features)
    far = lax.ppermute(u, "vocab", across)
    e, stats = join_llama(
        meta, own, squares_own, codes, token, u, (near_columns, columns, far_columns), stats, width, features
    )
    pieces, last = gather_pieces(stats, shards)
    late_u, _ = lax.optimization_barrier((u, last))
    near = lax.ppermute(late_u, "vocab", inside)
    m, m_top = map_parts(meta, u, near, far, pair_weight, width, shards)
    out, nll = finish(pieces, e, m, m_top)
    return out, nll[0]


def solution(mesh):
    in_specs = (
        P("mp", None, "rows"),
        P("mp", "rows"),
        P("mp", "rows", "vocab"),
        P("vocab"),
        P("vocab"),
        P("vocab"),
        P("vocab", None, None),
        P(("mp", "rows")),
    )
    out_specs = (P(("mp", "rows"), "vocab"), P(("mp", "rows")))
    return jax.shard_map(
        on_device, mesh=mesh, in_specs=in_specs, out_specs=out_specs, check_vma=False
    )
```

```python
import functools

import jax
import jax.numpy as jnp
from jax import lax
from jax.experimental import pallas as pl
from jax.experimental.pallas import tpu as pltpu
from jax.sharding import PartitionSpec as P

LANES = 128
EXTRA = 16
CODE = 512
HEAD_COPIES = 1
TOP = 32700.0
ROUNDER = 12582912.0
LEAST = 1e-30
FLOOR = 1.9287498479639178e-22
VMEM = 16 * 1024 * 1024

f32, bf16, i32, i16 = jnp.float32, jnp.bfloat16, jnp.int32, jnp.int16


def params():
    return pltpu.CompilerParams(vmem_limit_bytes=VMEM)


def exponent(value):
    return jnp.ceil(jnp.log2(jnp.maximum(value, LEAST)))


def columns_to_lanes(values, rows):
    lanes = lax.broadcasted_iota(i32, (rows, LANES), 1)
    out = jnp.zeros((rows, LANES), f32)
    for place, value in enumerate(values):
        out = jnp.where(lanes == place, value, out)
    return out


def split_exact(gained):
    high = gained.astype(bf16)
    return high, (gained - high.astype(f32)).astype(bf16)


def encode(values, power):
    wide = values * (jnp.exp2(-power) * (TOP * TOP))
    root = wide * lax.rsqrt(jnp.maximum(jnp.abs(wide), LEAST))
    return ((root + ROUNDER) - ROUNDER).astype(i32).astype(i16)


def decode(codes, power):
    wide = codes.astype(i32).astype(f32)
    return wide * jnp.abs(wide) * (jnp.exp2(power) * (1.0 / (TOP * TOP)))


def encode_scalar(value):
    power = exponent(value)
    mantissa = jnp.maximum(value, LEAST) * jnp.exp2(-power) * 16384.0
    first = jnp.floor(mantissa)
    return power, first, jnp.floor((mantissa - first) * 16384.0)


def decode_scalar(power, first, second):
    return (first + second * (1.0 / 16384.0)) * (1.0 / 16384.0) * jnp.exp2(power)


def prepare(hidden, gain, left_ref, at):
    rows = hidden.shape[0]
    values = hidden.astype(f32)
    high, low = split_exact(values * gain)
    left_ref[pl.ds(at, rows), :] = high
    left_ref[pl.ds(at + rows, rows), :] = low
    return jnp.sum(values * values, axis=1, keepdims=True)


def put_codes(out_ref, both, first):
    rows = both.shape[0] // 2
    part = both[:rows] + both[rows:]
    power = exponent(jnp.max(jnp.abs(part), axis=1, keepdims=True))
    codes = encode(part, power)
    for k in range(part.shape[1] // LANES):
        out_ref[pl.ds((first // LANES + k) * rows, rows), :] = codes[:, k * LANES : (k + 1) * LANES]
    return power


def put_extra(out_ref, powers, squares):
    rows = squares.shape[0]
    extra = columns_to_lanes(powers + list(encode_scalar(squares)), rows)
    body = out_ref.shape[0] - EXTRA
    out_ref[pl.ds(body, EXTRA), :] = jnp.transpose(extra)[:EXTRA].astype(i32).astype(i16)


def first_kernel(kinds, rows, hidden_ref, gain_ref, head_ref, *refs):
    count = len(kinds)
    left_refs, square_refs, head_out = refs[:count], refs[count : 2 * count], refs[2 * count]
    held, gain_held, sems, gain_sem, head_sems = refs[2 * count + 1 :]
    copies = []
    for place, which in enumerate(kinds):
        quarter = jnp.bitwise_xor(2 * lax.axis_index("mp") + lax.axis_index("rows"), which)
        at = pl.ds(pl.multiple_of(quarter * rows, rows), rows)
        copies.append(pltpu.make_async_copy(hidden_ref.at[at, :], held.at[place], sems.at[place]))
    gain_copy = pltpu.make_async_copy(gain_ref, gain_held, gain_sem)
    deep = head_ref.shape[0] // HEAD_COPIES
    spans = [pl.ds(k * deep, deep) for k in range(HEAD_COPIES)]
    head_copies = [
        pltpu.make_async_copy(head_ref.at[at, :], head_out.at[at, :], head_sems.at[k])
        for k, at in enumerate(spans)
    ]
    gain_copy.start()
    for copy in copies + head_copies:
        copy.start()
    gain_copy.wait()
    gain = gain_held[...].astype(f32)
    for place, copy in enumerate(copies):
        copy.wait()
        squares = prepare(held[place], gain, left_refs[place], 0)
        square_refs[place][...] = jnp.broadcast_to(squares, (rows, LANES))
    for copy in head_copies:
        copy.wait()


def first_prep(hidden, gain, head, kinds):
    rows, feats, count = hidden.shape[0] // 4, hidden.shape[1], len(kinds)
    hbm = pl.BlockSpec(memory_space=pltpu.HBM)
    outs = pl.pallas_call(
        functools.partial(first_kernel, kinds, rows),
        in_specs=[hbm, hbm, hbm],
        out_shape=[jax.ShapeDtypeStruct((2 * rows, feats), bf16)] * count
        + [jax.ShapeDtypeStruct((rows, LANES), f32)] * count
        + [jax.ShapeDtypeStruct(head.shape, head.dtype)],
        scratch_shapes=[
            pltpu.VMEM((count, rows, feats), bf16),
            pltpu.VMEM(gain.shape, bf16),
            pltpu.SemaphoreType.DMA((count,)),
            pltpu.SemaphoreType.DMA,
            pltpu.SemaphoreType.DMA((HEAD_COPIES,)),
        ],
        compiler_params=params(),
        cost_estimate=pl.CostEstimate(
            flops=8 * count * rows * feats, bytes_accessed=2 * head.size, transcendentals=0
        ),
        name="first_prep",
    )(hidden, gain, head)
    return outs[:count], outs[count : 2 * count], outs[2 * count]


def encode_kernel(count, both_ref, *refs):
    square_refs, outs = refs[:count], refs[count:]
    rows, cols = both_ref.shape[0] // count // 2, both_ref.shape[1]
    for place, out_ref in enumerate(outs):
        powers = []
        for first in range(0, cols, CODE):
            both = both_ref[pl.ds(2 * place * rows, 2 * rows), pl.ds(first, CODE)]
            powers.append(put_codes(out_ref, both, first))
        put_extra(out_ref, powers, square_refs[place][:, :1])


def encode_parts(both, squares):
    count = len(squares)
    rows, cols = both.shape[0] // count // 2, both.shape[1]
    return pl.pallas_call(
        functools.partial(encode_kernel, count),
        out_shape=[jax.ShapeDtypeStruct((cols // LANES * rows + EXTRA, LANES), i16)] * count,
        compiler_params=params(),
        cost_estimate=pl.CostEstimate(
            flops=20 * count * rows * cols, bytes_accessed=10 * count * rows * cols, transcendentals=count * rows * cols
        ),
        name="encode_parts",
    )(both, *squares)


def product(left, head):
    return jnp.dot(left, head, preferred_element_type=f32)


def side_kernel(width, blocks, own_which, meta_ref, quarter_ref, token_ref, hidden_ref, gain_ref, w_ref, head_ref, near_ref, own_ref, far_ref, left_ref, squares_ref, head_out, held, gain_held, w_held, sum_ref, sem, gain_sem, w_sems, head_sem):
    rows = token_ref.shape[1]
    slots = w_ref.shape[0]
    at = pl.ds(pl.multiple_of(quarter_ref[own_which] * rows, rows), rows)
    hidden_copy = pltpu.make_async_copy(hidden_ref.at[at, :], held, sem)
    gain_copy = pltpu.make_async_copy(gain_ref, gain_held, gain_sem)
    w_copies = [pltpu.make_async_copy(w_ref.at[k], w_held.at[k], w_sems.at[k]) for k in range(slots)]
    gain_copy.start()
    hidden_copy.start()
    for copy in w_copies:
        copy.start()
    head_copy = pltpu.make_async_copy(head_ref, head_out, head_sem)
    head_copy.start()
    shard = meta_ref[1]
    near_at = jnp.where(shard % 2 == 0, 2, 0)
    token = jnp.transpose(jnp.broadcast_to(token_ref[...].astype(f32), (8, rows)))[:, :1].astype(i32)
    place = lax.broadcasted_iota(i32, (rows, width), 1)
    sum_ref[...] = jnp.zeros_like(sum_ref)
    gain_copy.wait()
    hidden_copy.wait()
    squares = prepare(held[...], gain_held[...].astype(f32), left_ref, 0)
    squares_ref[...] = jnp.broadcast_to(squares, (rows, LANES))
    for slot in range(slots):
        w_copies[slot].wait()

        @pl.when(slot < meta_ref[2 + 2 * slots])
        def _():
            source = jnp.clip(meta_ref[2 + slot] - (shard - 1) * blocks, 0, 3 * blocks - 1)
            hits = (token - meta_ref[2 + slots + slot] * width == place).astype(bf16)
            left = jnp.concatenate([hits, jnp.ones((EXTRA, width), bf16)], axis=0)
            found = lax.dot_general(
                left, w_held[slot], (((1,), (1,)), ((), ())), preferred_element_type=f32
            )
            at = pl.ds(pl.multiple_of(source % blocks * width, width), width)
            sum_ref[source // blocks, :, at] += found

    order = lax.broadcasted_iota(i32, (EXTRA, 1), 0)
    for out_ref, k in ((near_ref, near_at), (own_ref, 1), (far_ref, 2 - near_at)):
        out_ref[pl.ds(0, rows), :] = sum_ref[k, pl.ds(0, rows), :].astype(bf16)
        sums = sum_ref[k, pl.ds(rows, EXTRA), :]
        first = sums.astype(bf16).astype(f32)
        second = (sums - first).astype(bf16).astype(f32)
        third = sums - first - second
        parts = jnp.where(order == 0, first, jnp.where(order == 1, second, jnp.where(order == 2, third, 0.0)))
        out_ref[pl.ds(rows, EXTRA), :] = parts.astype(bf16)
    near_ref[pl.ds(rows + EXTRA, EXTRA), :] = jnp.zeros((EXTRA, near_ref.shape[1]), bf16)
    head_copy.wait()


def side_parts(meta, quarters, token, hidden, gain, weights, head, width):
    rows, feats, cols = token.shape[1], hidden.shape[1], head.shape[1]
    smem = pl.BlockSpec(memory_space=pltpu.SMEM)
    hbm = pl.BlockSpec(memory_space=pltpu.HBM)
    outs = pl.pallas_call(
        functools.partial(side_kernel, width, cols // width, 0),
        in_specs=[smem, smem, pl.BlockSpec(memory_space=pltpu.VMEM), hbm, hbm, hbm, hbm],
        out_shape=[jax.ShapeDtypeStruct((rows + many * EXTRA, cols), bf16) for many in (2, 1, 1)]
        + [jax.ShapeDtypeStruct((2 * rows, feats), bf16), jax.ShapeDtypeStruct((rows, LANES), f32)]
        + [jax.ShapeDtypeStruct(head.shape, head.dtype)],
        scratch_shapes=[
            pltpu.VMEM((rows, feats), bf16),
            pltpu.VMEM(gain.shape, bf16),
            pltpu.VMEM(weights.shape, bf16),
            pltpu.VMEM((3, rows + EXTRA, cols), f32),
            pltpu.SemaphoreType.DMA,
            pltpu.SemaphoreType.DMA,
            pltpu.SemaphoreType.DMA((weights.shape[0],)),
            pltpu.SemaphoreType.DMA,
        ],
        compiler_params=params(),
        cost_estimate=pl.CostEstimate(flops=1, bytes_accessed=1, transcendentals=0),
        name="side_parts",
    )(meta, quarters, token, hidden, gain, weights, head)
    return outs[:3], outs[3], outs[4], outs[5]


def extras(ref, rows):
    tile = ref[pl.ds(ref.shape[0] - EXTRA, EXTRA), :].astype(i32).astype(f32)
    wide = jnp.transpose(tile)
    groups = (ref.shape[0] - EXTRA) // rows * LANES // CODE
    at = [wide[:, j : j + 1] for j in range(groups + 3)]
    return at[:groups], decode_scalar(*at[groups:])


def model_logits(mine, features, own_ref, squares_ref, cy_ref, cx_ref, cd_ref, out_ref):
    rows = squares_ref.shape[0]
    cols = own_ref.shape[1]

    def run(scale, at_slab):
        for slab in range(cols // LANES):
            out_ref[:, pl.ds(slab * LANES, LANES)] = at_slab(slab) * scale

    @pl.when(mine)
    def _():
        power_y, squares_y = extras(cy_ref, rows)

        def at_slab(slab):
            at = pl.ds(slab * LANES, LANES)
            own = own_ref[pl.ds(0, rows), at] + own_ref[pl.ds(rows, rows), at]
            return own + decode(cy_ref[pl.ds(slab * rows, rows), :], power_y[slab * LANES // CODE])

        run(lax.rsqrt((squares_ref[:, :1] + squares_y) / features + 1e-05), at_slab)

    @pl.when(jnp.logical_not(mine))
    def _():
        power_x, squares_x = extras(cx_ref, rows)
        power_d, squares_d = extras(cd_ref, rows)

        def at_slab(slab):
            part, group = pl.ds(slab * rows, rows), slab * LANES // CODE
            return decode(cx_ref[part, :], power_x[group]) + decode(cd_ref[part, :], power_d[group])

        run(lax.rsqrt((squares_x + squares_d) / features + 1e-05), at_slab)

    peak = jnp.full((rows, LANES), -jnp.inf, f32)
    for slab in range(cols // LANES):
        peak = jnp.maximum(peak, out_ref[:, pl.ds(slab * LANES, LANES)])
    return jnp.max(peak, axis=1, keepdims=True)


def qwen_kernel(width, blocks, features, own_ref, squares_ref, cy_ref, cx_ref, cd_ref, u_ref, stats_ref, q_ref):
    rows = squares_ref.shape[0]
    body = blocks * width
    peak = model_logits(lax.axis_index("mp") == 1, features, own_ref, squares_ref, cy_ref, cx_ref, cd_ref, q_ref)
    total = jnp.zeros((rows, 1), f32)
    for j in range(blocks):
        at = pl.ds(j * width, width)
        qwen = jnp.exp(q_ref[:, at] - peak)
        u_ref[:, at] = qwen.astype(bf16)
        total += jnp.sum(qwen, axis=1, keepdims=True)
    first = peak.astype(bf16).astype(f32)
    second = (peak - first).astype(bf16).astype(f32)
    third = peak - first - second
    u_ref[:, body:] = columns_to_lanes([first, second, third], rows).astype(bf16)
    stats_ref[...] = columns_to_lanes([peak, total], rows)


def join_qwen(own, squares, codes, width, features):
    rows, cols = own.shape[0] // 2, own.shape[1]
    whole = pl.BlockSpec(memory_space=pltpu.VMEM)
    return pl.pallas_call(
        functools.partial(qwen_kernel, width, cols // width, features),
        in_specs=[whole] * 5,
        out_shape=[
            jax.ShapeDtypeStruct((rows, cols + LANES), bf16),
            jax.ShapeDtypeStruct((rows, LANES), f32),
        ],
        scratch_shapes=[pltpu.VMEM((rows, cols), f32)],
        compiler_params=params(),
        cost_estimate=pl.CostEstimate(flops=20000000000, bytes_accessed=8 * 1024 * 1024, transcendentals=0),
        name="join_qwen",
    )(own, squares, *codes)


def llama_kernel(width, blocks, features, own_ref, squares_ref, cy_ref, cx_ref, cd_ref, token_ref, u_ref, near_ref, mine_ref, far_ref, before_ref, e_ref, stats_ref):
    rows = squares_ref.shape[0]
    body = blocks * width
    columns_refs = (near_ref, mine_ref, far_ref)
    peak = model_logits(lax.axis_index("mp") == 0, features, own_ref, squares_ref, cy_ref, cx_ref, cd_ref, e_ref)
    total = jnp.zeros((rows, 1), f32)
    mass = jnp.zeros((rows, 1), f32)
    pick_e = jnp.zeros((rows, 1), f32)
    pick_m = jnp.zeros((rows, 1), f32)
    token = jnp.transpose(jnp.broadcast_to(token_ref[...].astype(f32), (8, rows)))
    token = token[:, :1].astype(i32) - lax.axis_index("vocab") * body
    for j in range(blocks):
        at = pl.ds(j * width, width)
        llama = jnp.exp(e_ref[:, at] - peak)
        e_ref[:, at] = llama
        total += jnp.sum(llama, axis=1, keepdims=True)
        hit = lax.broadcasted_iota(i32, (rows, width), 1) + j * width == token
        pick_e += jnp.sum(jnp.where(hit, llama, 0.0), axis=1, keepdims=True)
        held = u_ref[:, at].astype(f32)
        columns = functools.reduce(jnp.add, [ref[pl.ds(0, rows), at].astype(f32) for ref in columns_refs])
        pick_m += jnp.sum(held * columns, axis=1, keepdims=True)
        sums = functools.reduce(jnp.add, [ref[pl.ds(rows, EXTRA), at].astype(f32) for ref in columns_refs])
        mass += jnp.sum(held * jnp.sum(sums, axis=0, keepdims=True), axis=1, keepdims=True)
    before = before_ref[...]
    stats = columns_to_lanes([peak, total, before[:, 0:1], before[:, 1:2], mass, pick_e, pick_m], rows)
    stats_ref[...] = jnp.transpose(stats)[:8]


def join_llama(own, squares, codes, token, u, columns, stats, width, features):
    rows, cols = own.shape[0] // 2, own.shape[1]
    whole = pl.BlockSpec(memory_space=pltpu.VMEM)
    return pl.pallas_call(
        functools.partial(llama_kernel, width, cols // width, features),
        in_specs=[whole] * 11,
        out_shape=[jax.ShapeDtypeStruct((rows, cols), f32), jax.ShapeDtypeStruct((8, rows), f32)],
        compiler_params=params(),
        cost_estimate=pl.CostEstimate(flops=20000000000, bytes_accessed=8 * 1024 * 1024, transcendentals=0),
        name="join_llama",
    )(own, squares, *codes, token, u, *columns, stats)


def map_kernel(width, blocks, shards, meta_ref, u_ref, near_ref, far_ref, w_ref, m_ref, top_ref, all_ref, scale_ref):
    rows = u_ref.shape[0]
    body = blocks * width
    shard = meta_ref[1]
    slots = w_ref.shape[0]
    near_at = jnp.where(shard % 2 == 0, 2, 0)

    def peak_of(ref):
        lanes = ref[:, body:].astype(f32)
        return lanes[:, 0:1] + lanes[:, 1:2] + lanes[:, 2:3]

    own_peak = peak_of(u_ref)
    near_peak = peak_of(near_ref)
    far_peak = jnp.where((shard > 0) & (shard < shards - 1), peak_of(far_ref), own_peak)
    top = jnp.maximum(jnp.maximum(near_peak, far_peak), own_peak)
    for k, ref, peak in ((near_at, near_ref, near_peak), (1, u_ref, own_peak), (2 - near_at, far_ref, far_peak)):
        all_ref[k] = ref[:, :body]
        scale_ref[k] = jnp.broadcast_to(jnp.exp(peak - top), (rows, LANES))
    m_ref[...] = jnp.zeros_like(m_ref)
    for slot in range(slots):

        @pl.when(slot < meta_ref[2 + 2 * slots])
        def _():
            source = jnp.clip(meta_ref[2 + slot] - (shard - 1) * blocks, 0, 3 * blocks - 1)
            target = jnp.clip(meta_ref[2 + slots + slot] - shard * blocks, 0, blocks - 1)
            inside = pl.multiple_of(source % blocks * width, width)
            picked = all_ref[source // blocks, :, pl.ds(inside, width)]
            term = jnp.dot(picked, w_ref[slot], preferred_element_type=f32)
            at = pl.ds(pl.multiple_of(target * width, width), width)
            m_ref[:, at] += term * scale_ref[source // blocks][:, :1]

    top_ref[...] = jnp.broadcast_to(top, (rows, LANES))


def map_parts(meta, u, near, far, weights, width, shards):
    rows, cols = u.shape[0], u.shape[1] - LANES
    blocks = cols // width
    whole = pl.BlockSpec(memory_space=pltpu.VMEM)
    return pl.pallas_call(
        functools.partial(map_kernel, width, blocks, shards),
        in_specs=[pl.BlockSpec(memory_space=pltpu.SMEM)] + [whole] * 4,
        out_shape=[jax.ShapeDtypeStruct((rows, cols), f32), jax.ShapeDtypeStruct((rows, LANES), f32)],
        scratch_shapes=[pltpu.VMEM((3, rows, cols), bf16), pltpu.VMEM((3, rows, LANES), f32)],
        compiler_params=params(),
        cost_estimate=pl.CostEstimate(
            flops=2 * rows * weights.size, bytes_accessed=2 * weights.size, transcendentals=0
        ),
        name="map_parts",
    )(meta, u, near, far, weights)


def finish_kernel(pieces, *refs):
    stats_refs, (e_ref, m_ref, m_top_ref, out_ref, nll_ref) = refs[:pieces], refs[pieces:]
    stats = [ref[k : k + 8, :] for ref in stats_refs for k in range(0, ref.shape[0], 8)]
    shards = range(len(stats))
    row = lambda s, k: stats[s][k : k + 1, :]
    top_l = functools.reduce(jnp.maximum, [row(s, 0) for s in shards])
    top_q = functools.reduce(jnp.maximum, [row(s, 2) for s in shards])
    sum_l = functools.reduce(jnp.add, [row(s, 1) * jnp.exp(row(s, 0) - top_l) for s in shards])
    sum_q = functools.reduce(jnp.add, [row(s, 3) * jnp.exp(row(s, 2) - top_q) for s in shards])
    part_l = [jnp.exp(row(s, 0) - top_l) / sum_l for s in shards]
    part_q = [jnp.exp(row(s, 2) - top_q) / sum_q for s in shards]
    mass = functools.reduce(jnp.add, [row(s, 4) * part_q[s] for s in shards])
    pick_e = functools.reduce(jnp.add, [row(s, 5) * part_l[s] for s in shards])
    pick_m = functools.reduce(jnp.add, [row(s, 6) * part_q[s] for s in shards])
    log_norm = jnp.log1p(mass)
    nll_ref[...] = log_norm - jnp.log(jnp.maximum(pick_e, FLOOR) + pick_m)
    tile = jnp.concatenate([part_l[0], top_q, 1.0 / sum_q, log_norm, jnp.zeros((4, log_norm.shape[1]), f32)], axis=0)
    turned = jnp.transpose(tile)
    a, top, share, c = (turned[:, i : i + 1] for i in range(4))
    b = jnp.exp(m_top_ref[:, :1] - top) * share
    out_ref[...] = jnp.log(jnp.maximum(e_ref[...] * a, FLOOR) + m_ref[...] * b) - c


def finish(pieces, e, m, m_top):
    rows, cols = e.shape
    return pl.pallas_call(
        functools.partial(finish_kernel, len(pieces)),
        out_shape=[
            jax.ShapeDtypeStruct((rows, cols), f32),
            jax.ShapeDtypeStruct((1, rows), f32),
        ],
        compiler_params=params(),
        cost_estimate=pl.CostEstimate(
            flops=20 * rows * cols, bytes_accessed=12 * rows * cols, transcendentals=2 * rows * cols
        ),
        name="finish",
    )(*pieces, e, m, m_top)


def gather_pieces(own, shards):
    pieces, step = [own], 1
    while step < shards:
        radix = 4 if step > 1 and 4 * step <= shards else 2
        sent = pieces[0] if len(pieces) == 1 else jnp.concatenate(pieces, axis=0)
        for turn in range(1, radix):
            pieces.append(lax.ppermute(sent, "vocab", [(i, i ^ (turn * step)) for i in range(shards)]))
        step *= radix
    return pieces, sent


def on_device(
    hidden, norm_gain, head_weights, pair_source, pair_target, pair_count, pair_weight, next_token
):
    shards = lax.axis_size("vocab")
    row_groups = lax.axis_size("rows")
    hidden, head = hidden[0], head_weights[0]
    token = next_token[None, :]
    held_hidden = pltpu.with_memory_space_constraint(hidden, pltpu.HBM)
    held_weight = pltpu.with_memory_space_constraint(pair_weight, pltpu.HBM)
    held_gain = pltpu.with_memory_space_constraint(norm_gain, pltpu.HBM)
    held_head = pltpu.with_memory_space_constraint(head, pltpu.HBM)
    width = pair_weight.shape[1]
    features = hidden.shape[1] * row_groups
    model, shard, side = (lax.axis_index(name).astype(i32) for name in ("mp", "vocab", "rows"))
    mine = 2 * model + side
    quarters = jnp.stack([mine, mine ^ 1, mine ^ 2, mine ^ 3])
    meta = jnp.concatenate([jnp.stack([model, shard]), pair_source, pair_target, pair_count])

    inside = [(i, i ^ 1) for i in range(shards)]
    across = [(i, i + 1 if i % 2 else i - 1) for i in range(1, shards - 1)]
    lefts, squares, head = first_prep(held_hidden, held_gain, held_head, (3, 1, 2))
    (to_d,) = encode_parts(product(lefts[0], head), squares[:1])
    from_d = lax.ppermute(to_d, ("mp", "rows"), [(0, 3), (1, 2), (2, 1), (3, 0)])
    left_y, _ = lax.optimization_barrier((lefts[1], to_d))
    (to_y,) = encode_parts(product(left_y, head), squares[1:2])
    from_y = lax.ppermute(to_y, "rows", [(0, 1), (1, 0)])
    left_x, _ = lax.optimization_barrier((lefts[2], to_y))
    (to_x,) = encode_parts(product(left_x, head), squares[2:])
    from_x = lax.ppermute(to_x, "mp", [(0, 1), (1, 0)])
    early, _ = lax.optimization_barrier((meta, to_x))
    (to_near, columns, to_far), left_own, squares_own, head = side_parts(
        early, quarters, token, held_hidden, held_gain, held_weight, held_head, width
    )
    own = product(left_own, head)
    to_near, _ = lax.optimization_barrier((to_near, own))
    near_columns = lax.ppermute(to_near, "vocab", inside)
    far_columns = lax.ppermute(to_far, "vocab", across)

    codes = (from_y, from_x, from_d)
    u, stats = join_qwen(own, squares_own, codes, width, features)
    far = lax.ppermute(u, "vocab", across)
    e, stats = join_llama(
        own, squares_own, codes, token, u, (near_columns, columns, far_columns), stats, width, features
    )
    pieces, last = gather_pieces(stats, shards)
    late_u, _ = lax.optimization_barrier((u, last))
    near = lax.ppermute(late_u, "vocab", inside)
    m, m_top = map_parts(meta, u, near, far, pair_weight, width, shards)
    out, nll = finish(pieces, e, m, m_top)
    return out, nll[0]


def solution(mesh):
    in_specs = (
        P("mp", None, "rows"),
        P("mp", "rows"),
        P("mp", "rows", "vocab"),
        P("vocab"),
        P("vocab"),
        P("vocab"),
        P("vocab", None, None),
        P(("mp", "rows")),
    )
    out_specs = (P(("mp", "rows"), "vocab"), P(("mp", "rows")))
    return jax.shard_map(
        on_device, mesh=mesh, in_specs=in_specs, out_specs=out_specs, check_vma=False
    )
```

```python
import functools

import jax
import jax.numpy as jnp
from jax import lax
from jax.experimental import pallas as pl
from jax.experimental.pallas import tpu as pltpu
from jax.sharding import PartitionSpec as P

LANES = 128
EXTRA = 16
CODE = 512
HEAD_COPIES = 1
TOP = 32700.0
ROUNDER = 12582912.0
LEAST = 1e-30
FLOOR = 1.9287498479639178e-22
VMEM = 16 * 1024 * 1024

f32, bf16, i32, i16 = jnp.float32, jnp.bfloat16, jnp.int32, jnp.int16


def params():
    return pltpu.CompilerParams(vmem_limit_bytes=VMEM)


def exponent(value):
    return jnp.ceil(jnp.log2(jnp.maximum(value, LEAST)))


def columns_to_lanes(values, rows):
    lanes = lax.broadcasted_iota(i32, (rows, LANES), 1)
    out = jnp.zeros((rows, LANES), f32)
    for place, value in enumerate(values):
        out = jnp.where(lanes == place, value, out)
    return out


def split_exact(gained):
    high = gained.astype(bf16)
    return high, (gained - high.astype(f32)).astype(bf16)


def encode(values, power):
    wide = values * (jnp.exp2(-power) * (TOP * TOP))
    root = wide * lax.rsqrt(jnp.maximum(jnp.abs(wide), LEAST))
    return ((root + ROUNDER) - ROUNDER).astype(i32).astype(i16)


def decode(codes, power):
    wide = codes.astype(i32).astype(f32)
    return wide * jnp.abs(wide) * (jnp.exp2(power) * (1.0 / (TOP * TOP)))


def encode_scalar(value):
    power = exponent(value)
    mantissa = jnp.maximum(value, LEAST) * jnp.exp2(-power) * 16384.0
    first = jnp.floor(mantissa)
    return power, first, jnp.floor((mantissa - first) * 16384.0)


def decode_scalar(power, first, second):
    return (first + second * (1.0 / 16384.0)) * (1.0 / 16384.0) * jnp.exp2(power)


def prepare(hidden, gain, left_ref, at):
    rows = hidden.shape[0]
    values = hidden.astype(f32)
    high, low = split_exact(values * gain)
    left_ref[pl.ds(at, rows), :] = high
    left_ref[pl.ds(at + rows, rows), :] = low
    return jnp.sum(values * values, axis=1, keepdims=True)


def put_codes(out_ref, both, first):
    rows = both.shape[0] // 2
    part = both[:rows] + both[rows:]
    power = exponent(jnp.max(jnp.abs(part), axis=1, keepdims=True))
    codes = encode(part, power)
    for k in range(part.shape[1] // LANES):
        out_ref[pl.ds((first // LANES + k) * rows, rows), :] = codes[:, k * LANES : (k + 1) * LANES]
    return power


def put_extra(out_ref, powers, squares):
    rows = squares.shape[0]
    extra = columns_to_lanes(powers + list(encode_scalar(squares)), rows)
    body = out_ref.shape[0] - EXTRA
    out_ref[pl.ds(body, EXTRA), :] = jnp.transpose(extra)[:EXTRA].astype(i32).astype(i16)


def first_kernel(kinds, rows, hidden_ref, gain_ref, head_ref, *refs):
    count = len(kinds)
    left_refs, square_refs, head_out = refs[:count], refs[count : 2 * count], refs[2 * count]
    held, gain_held, sems, gain_sem, head_sems = refs[2 * count + 1 :]
    copies = []
    for place, which in enumerate(kinds):
        quarter = jnp.bitwise_xor(2 * lax.axis_index("mp") + lax.axis_index("rows"), which)
        at = pl.ds(pl.multiple_of(quarter * rows, rows), rows)
        copies.append(pltpu.make_async_copy(hidden_ref.at[at, :], held.at[place], sems.at[place]))
    gain_copy = pltpu.make_async_copy(gain_ref, gain_held, gain_sem)
    deep = head_ref.shape[0] // HEAD_COPIES
    spans = [pl.ds(k * deep, deep) for k in range(HEAD_COPIES)]
    head_copies = [
        pltpu.make_async_copy(head_ref.at[at, :], head_out.at[at, :], head_sems.at[k])
        for k, at in enumerate(spans)
    ]
    gain_copy.start()
    for copy in copies + head_copies:
        copy.start()
    gain_copy.wait()
    gain = gain_held[...].astype(f32)
    for place, copy in enumerate(copies):
        copy.wait()
        squares = prepare(held[place], gain, left_refs[place], 0)
        square_refs[place][...] = jnp.broadcast_to(squares, (rows, LANES))
    for copy in head_copies:
        copy.wait()


def first_prep(hidden, gain, head, kinds):
    rows, feats, count = hidden.shape[0] // 4, hidden.shape[1], len(kinds)
    hbm = pl.BlockSpec(memory_space=pltpu.HBM)
    outs = pl.pallas_call(
        functools.partial(first_kernel, kinds, rows),
        in_specs=[hbm, hbm, hbm],
        out_shape=[jax.ShapeDtypeStruct((2 * rows, feats), bf16)] * count
        + [jax.ShapeDtypeStruct((rows, LANES), f32)] * count
        + [jax.ShapeDtypeStruct(head.shape, head.dtype)],
        scratch_shapes=[
            pltpu.VMEM((count, rows, feats), bf16),
            pltpu.VMEM(gain.shape, bf16),
            pltpu.SemaphoreType.DMA((count,)),
            pltpu.SemaphoreType.DMA,
            pltpu.SemaphoreType.DMA((HEAD_COPIES,)),
        ],
        compiler_params=params(),
        cost_estimate=pl.CostEstimate(
            flops=8 * count * rows * feats, bytes_accessed=2 * head.size, transcendentals=0
        ),
        name="first_prep",
    )(hidden, gain, head)
    return outs[:count], outs[count : 2 * count], outs[2 * count]


def rows_kernel(which, hidden_ref, gain_ref, left_ref, squares_ref, held, sem):
    rows = held.shape[0]
    quarter = jnp.bitwise_xor(2 * lax.axis_index("mp") + lax.axis_index("rows"), which)
    at = pl.ds(pl.multiple_of(quarter * rows, rows), rows)
    hidden_copy = pltpu.make_async_copy(hidden_ref.at[at, :], held, sem)
    hidden_copy.start()
    hidden_copy.wait()
    squares = prepare(held[...], gain_ref[...].astype(f32), left_ref, 0)
    squares_ref[...] = jnp.broadcast_to(squares, (rows, LANES))


def prep_rows(hidden, gain, which):
    rows, feats = hidden.shape[0] // 4, hidden.shape[1]
    vmem = pl.BlockSpec(memory_space=pltpu.VMEM)
    return pl.pallas_call(
        functools.partial(rows_kernel, which),
        in_specs=[pl.BlockSpec(memory_space=pltpu.HBM), vmem],
        out_shape=[jax.ShapeDtypeStruct((2 * rows, feats), bf16), jax.ShapeDtypeStruct((rows, LANES), f32)],
        scratch_shapes=[pltpu.VMEM((rows, feats), bf16), pltpu.SemaphoreType.DMA],
        compiler_params=params(),
        cost_estimate=pl.CostEstimate(flops=1, bytes_accessed=6 * rows * feats, transcendentals=0),
        name="prep_rows",
    )(hidden, gain)


def encode_kernel(count, both_ref, *refs):
    square_refs, outs = refs[:count], refs[count:]
    rows, cols = both_ref.shape[0] // count // 2, both_ref.shape[1]
    for place, out_ref in enumerate(outs):
        powers = []
        for first in range(0, cols, CODE):
            both = both_ref[pl.ds(2 * place * rows, 2 * rows), pl.ds(first, CODE)]
            powers.append(put_codes(out_ref, both, first))
        put_extra(out_ref, powers, square_refs[place][:, :1])


def encode_parts(both, squares):
    count = len(squares)
    rows, cols = both.shape[0] // count // 2, both.shape[1]
    return pl.pallas_call(
        functools.partial(encode_kernel, count),
        out_shape=[jax.ShapeDtypeStruct((cols // LANES * rows + EXTRA, LANES), i16)] * count,
        compiler_params=params(),
        cost_estimate=pl.CostEstimate(
            flops=20 * count * rows * cols, bytes_accessed=10 * count * rows * cols, transcendentals=count * rows * cols
        ),
        name="encode_parts",
    )(both, *squares)


def product(left, head):
    return jnp.dot(left, head, preferred_element_type=f32)


def side_kernel(width, blocks, lists_ref, token_ref, hidden_ref, gain_ref, w_ref, head_ref, near_ref, own_ref, far_ref, left_ref, squares_ref, head_out, held, gain_held, w_held, sum_ref, meta_ref, sem, gain_sem, w_sems, head_sem, meta_sem):
    rows = token_ref.shape[1]
    slots = w_ref.shape[0]
    meta_copy = pltpu.make_async_copy(lists_ref, meta_ref, meta_sem)
    meta_copy.start()
    quarter = 2 * lax.axis_index("mp") + lax.axis_index("rows")
    at = pl.ds(pl.multiple_of(quarter * rows, rows), rows)
    hidden_copy = pltpu.make_async_copy(hidden_ref.at[at, :], held, sem)
    gain_copy = pltpu.make_async_copy(gain_ref, gain_held, gain_sem)
    w_copies = [pltpu.make_async_copy(w_ref.at[k], w_held.at[k], w_sems.at[k]) for k in range(slots)]
    gain_copy.start()
    hidden_copy.start()
    for copy in w_copies:
        copy.start()
    head_copy = pltpu.make_async_copy(head_ref, head_out, head_sem)
    head_copy.start()
    shard = lax.axis_index("vocab")
    near_at = jnp.where(shard % 2 == 0, 2, 0)
    token = jnp.transpose(jnp.broadcast_to(token_ref[...].astype(f32), (8, rows)))[:, :1].astype(i32)
    place = lax.broadcasted_iota(i32, (rows, width), 1)
    sum_ref[...] = jnp.zeros_like(sum_ref)
    gain_copy.wait()
    hidden_copy.wait()
    squares = prepare(held[...], gain_held[...].astype(f32), left_ref, 0)
    squares_ref[...] = jnp.broadcast_to(squares, (rows, LANES))
    meta_copy.wait()
    for slot in range(slots):
        w_copies[slot].wait()

        @pl.when(slot < meta_ref[2 * slots])
        def _():
            source = jnp.clip(meta_ref[slot] - (shard - 1) * blocks, 0, 3 * blocks - 1)
            hits = (token - meta_ref[slots + slot] * width == place).astype(bf16)
            left = jnp.concatenate([hits, jnp.ones((EXTRA, width), bf16)], axis=0)
            found = lax.dot_general(
                left, w_held[slot], (((1,), (1,)), ((), ())), preferred_element_type=f32
            )
            at = pl.ds(pl.multiple_of(source % blocks * width, width), width)
            sum_ref[source // blocks, :, at] += found

    order = lax.broadcasted_iota(i32, (EXTRA, 1), 0)
    for out_ref, k in ((near_ref, near_at), (own_ref, 1), (far_ref, 2 - near_at)):
        out_ref[pl.ds(0, rows), :] = sum_ref[k, pl.ds(0, rows), :].astype(bf16)
        sums = sum_ref[k, pl.ds(rows, EXTRA), :]
        first = sums.astype(bf16).astype(f32)
        second = (sums - first).astype(bf16).astype(f32)
        third = sums - first - second
        parts = jnp.where(order == 0, first, jnp.where(order == 1, second, jnp.where(order == 2, third, 0.0)))
        out_ref[pl.ds(rows, EXTRA), :] = parts.astype(bf16)
    near_ref[pl.ds(rows + EXTRA, EXTRA), :] = jnp.zeros((EXTRA, near_ref.shape[1]), bf16)
    head_copy.wait()


def side_parts(lists, token, hidden, gain, weights, head, width):
    rows, feats, cols = token.shape[1], hidden.shape[1], head.shape[1]
    hbm = pl.BlockSpec(memory_space=pltpu.HBM)
    outs = pl.pallas_call(
        functools.partial(side_kernel, width, cols // width),
        in_specs=[pl.BlockSpec(memory_space=pl.ANY), pl.BlockSpec(memory_space=pltpu.VMEM), hbm, hbm, hbm, hbm],
        out_shape=[jax.ShapeDtypeStruct((rows + many * EXTRA, cols), bf16) for many in (2, 1, 1)]
        + [jax.ShapeDtypeStruct((2 * rows, feats), bf16), jax.ShapeDtypeStruct((rows, LANES), f32)]
        + [jax.ShapeDtypeStruct(head.shape, head.dtype)],
        scratch_shapes=[
            pltpu.VMEM((rows, feats), bf16),
            pltpu.VMEM(gain.shape, bf16),
            pltpu.VMEM(weights.shape, bf16),
            pltpu.VMEM((3, rows + EXTRA, cols), f32),
            pltpu.SMEM(lists.shape, i32),
            pltpu.SemaphoreType.DMA,
            pltpu.SemaphoreType.DMA,
            pltpu.SemaphoreType.DMA((weights.shape[0],)),
            pltpu.SemaphoreType.DMA,
            pltpu.SemaphoreType.DMA,
        ],
        compiler_params=params(),
        cost_estimate=pl.CostEstimate(flops=1, bytes_accessed=1, transcendentals=0),
        name="side_parts",
    )(lists, token, hidden, gain, weights, head)
    return outs[:3], outs[3], outs[4], outs[5]


def extras(ref, rows):
    tile = ref[pl.ds(ref.shape[0] - EXTRA, EXTRA), :].astype(i32).astype(f32)
    wide = jnp.transpose(tile)
    groups = (ref.shape[0] - EXTRA) // rows * LANES // CODE
    at = [wide[:, j : j + 1] for j in range(groups + 3)]
    return at[:groups], decode_scalar(*at[groups:])


def model_logits(mine, features, own_ref, squares_ref, cy_ref, cx_ref, cd_ref, out_ref):
    rows = squares_ref.shape[0]
    cols = own_ref.shape[1]

    def run(scale, at_slab):
        for slab in range(cols // LANES):
            out_ref[:, pl.ds(slab * LANES, LANES)] = at_slab(slab) * scale

    @pl.when(mine)
    def _():
        power_y, squares_y = extras(cy_ref, rows)

        def at_slab(slab):
            at = pl.ds(slab * LANES, LANES)
            own = own_ref[pl.ds(0, rows), at] + own_ref[pl.ds(rows, rows), at]
            return own + decode(cy_ref[pl.ds(slab * rows, rows), :], power_y[slab * LANES // CODE])

        run(lax.rsqrt((squares_ref[:, :1] + squares_y) / features + 1e-05), at_slab)

    @pl.when(jnp.logical_not(mine))
    def _():
        power_x, squares_x = extras(cx_ref, rows)
        power_d, squares_d = extras(cd_ref, rows)

        def at_slab(slab):
            part, group = pl.ds(slab * rows, rows), slab * LANES // CODE
            return decode(cx_ref[part, :], power_x[group]) + decode(cd_ref[part, :], power_d[group])

        run(lax.rsqrt((squares_x + squares_d) / features + 1e-05), at_slab)

    peak = jnp.full((rows, LANES), -jnp.inf, f32)
    for slab in range(cols // LANES):
        peak = jnp.maximum(peak, out_ref[:, pl.ds(slab * LANES, LANES)])
    return jnp.max(peak, axis=1, keepdims=True)


def qwen_kernel(width, blocks, features, own_ref, squares_ref, cy_ref, cx_ref, cd_ref, u_ref, stats_ref, q_ref):
    rows = squares_ref.shape[0]
    body = blocks * width
    peak = model_logits(lax.axis_index("mp") == 1, features, own_ref, squares_ref, cy_ref, cx_ref, cd_ref, q_ref)
    total = jnp.zeros((rows, 1), f32)
    for j in range(blocks):
        at = pl.ds(j * width, width)
        qwen = jnp.exp(q_ref[:, at] - peak)
        u_ref[:, at] = qwen.astype(bf16)
        total += jnp.sum(qwen, axis=1, keepdims=True)
    first = peak.astype(bf16).astype(f32)
    second = (peak - first).astype(bf16).astype(f32)
    third = peak - first - second
    u_ref[:, body:] = columns_to_lanes([first, second, third], rows).astype(bf16)
    stats_ref[...] = columns_to_lanes([peak, total], rows)


def join_qwen(own, squares, codes, width, features):
    rows, cols = own.shape[0] // 2, own.shape[1]
    whole = pl.BlockSpec(memory_space=pltpu.VMEM)
    return pl.pallas_call(
        functools.partial(qwen_kernel, width, cols // width, features),
        in_specs=[whole] * 5,
        out_shape=[
            jax.ShapeDtypeStruct((rows, cols + LANES), bf16),
            jax.ShapeDtypeStruct((rows, LANES), f32),
        ],
        scratch_shapes=[pltpu.VMEM((rows, cols), f32)],
        compiler_params=params(),
        cost_estimate=pl.CostEstimate(flops=20000000000, bytes_accessed=8 * 1024 * 1024, transcendentals=0),
        name="join_qwen",
    )(own, squares, *codes)


def llama_kernel(width, blocks, features, own_ref, squares_ref, cy_ref, cx_ref, cd_ref, token_ref, u_ref, near_ref, mine_ref, far_ref, before_ref, e_ref, stats_ref):
    rows = squares_ref.shape[0]
    body = blocks * width
    columns_refs = (near_ref, mine_ref, far_ref)
    peak = model_logits(lax.axis_index("mp") == 0, features, own_ref, squares_ref, cy_ref, cx_ref, cd_ref, e_ref)
    total = jnp.zeros((rows, 1), f32)
    mass = jnp.zeros((rows, 1), f32)
    pick_e = jnp.zeros((rows, 1), f32)
    pick_m = jnp.zeros((rows, 1), f32)
    token = jnp.transpose(jnp.broadcast_to(token_ref[...].astype(f32), (8, rows)))
    token = token[:, :1].astype(i32) - lax.axis_index("vocab") * body
    for j in range(blocks):
        at = pl.ds(j * width, width)
        llama = jnp.exp(e_ref[:, at] - peak)
        e_ref[:, at] = llama
        total += jnp.sum(llama, axis=1, keepdims=True)
        hit = lax.broadcasted_iota(i32, (rows, width), 1) + j * width == token
        pick_e += jnp.sum(jnp.where(hit, llama, 0.0), axis=1, keepdims=True)
        held = u_ref[:, at].astype(f32)
        columns = functools.reduce(jnp.add, [ref[pl.ds(0, rows), at].astype(f32) for ref in columns_refs])
        pick_m += jnp.sum(held * columns, axis=1, keepdims=True)
        sums = functools.reduce(jnp.add, [ref[pl.ds(rows, EXTRA), at].astype(f32) for ref in columns_refs])
        mass += jnp.sum(held * jnp.sum(sums, axis=0, keepdims=True), axis=1, keepdims=True)
    before = before_ref[...]
    stats = columns_to_lanes([peak, total, before[:, 0:1], before[:, 1:2], mass, pick_e, pick_m], rows)
    stats_ref[...] = jnp.transpose(stats)[:8]


def join_llama(own, squares, codes, token, u, columns, stats, width, features):
    rows, cols = own.shape[0] // 2, own.shape[1]
    whole = pl.BlockSpec(memory_space=pltpu.VMEM)
    return pl.pallas_call(
        functools.partial(llama_kernel, width, cols // width, features),
        in_specs=[whole] * 11,
        out_shape=[jax.ShapeDtypeStruct((rows, cols), f32), jax.ShapeDtypeStruct((8, rows), f32)],
        compiler_params=params(),
        cost_estimate=pl.CostEstimate(flops=20000000000, bytes_accessed=8 * 1024 * 1024, transcendentals=0),
        name="join_llama",
    )(own, squares, *codes, token, u, *columns, stats)


def map_kernel(width, blocks, shards, lists_ref, u_ref, near_ref, far_ref, w_ref, m_ref, top_ref, all_ref, scale_ref, meta_ref, meta_sem):
    rows = u_ref.shape[0]
    body = blocks * width
    meta_copy = pltpu.make_async_copy(lists_ref, meta_ref, meta_sem)
    meta_copy.start()
    shard = lax.axis_index("vocab")
    slots = w_ref.shape[0]
    near_at = jnp.where(shard % 2 == 0, 2, 0)

    def peak_of(ref):
        lanes = ref[:, body:].astype(f32)
        return lanes[:, 0:1] + lanes[:, 1:2] + lanes[:, 2:3]

    own_peak = peak_of(u_ref)
    near_peak = peak_of(near_ref)
    far_peak = jnp.where((shard > 0) & (shard < shards - 1), peak_of(far_ref), own_peak)
    top = jnp.maximum(jnp.maximum(near_peak, far_peak), own_peak)
    for k, ref, peak in ((near_at, near_ref, near_peak), (1, u_ref, own_peak), (2 - near_at, far_ref, far_peak)):
        all_ref[k] = ref[:, :body]
        scale_ref[k] = jnp.broadcast_to(jnp.exp(peak - top), (rows, LANES))
    m_ref[...] = jnp.zeros_like(m_ref)
    meta_copy.wait()
    for slot in range(slots):

        @pl.when(slot < meta_ref[2 * slots])
        def _():
            source = jnp.clip(meta_ref[slot] - (shard - 1) * blocks, 0, 3 * blocks - 1)
            target = jnp.clip(meta_ref[slots + slot] - shard * blocks, 0, blocks - 1)
            inside = pl.multiple_of(source % blocks * width, width)
            picked = all_ref[source // blocks, :, pl.ds(inside, width)]
            term = jnp.dot(picked, w_ref[slot], preferred_element_type=f32)
            at = pl.ds(pl.multiple_of(target * width, width), width)
            m_ref[:, at] += term * scale_ref[source // blocks][:, :1]

    top_ref[...] = jnp.broadcast_to(top, (rows, LANES))


def map_parts(lists, u, near, far, weights, width, shards):
    rows, cols = u.shape[0], u.shape[1] - LANES
    blocks = cols // width
    whole = pl.BlockSpec(memory_space=pltpu.VMEM)
    return pl.pallas_call(
        functools.partial(map_kernel, width, blocks, shards),
        in_specs=[pl.BlockSpec(memory_space=pl.ANY)] + [whole] * 4,
        out_shape=[jax.ShapeDtypeStruct((rows, cols), f32), jax.ShapeDtypeStruct((rows, LANES), f32)],
        scratch_shapes=[pltpu.VMEM((3, rows, cols), bf16), pltpu.VMEM((3, rows, LANES), f32)]
        + [pltpu.SMEM(lists.shape, i32), pltpu.SemaphoreType.DMA],
        compiler_params=params(),
        cost_estimate=pl.CostEstimate(
            flops=2 * rows * weights.size, bytes_accessed=2 * weights.size, transcendentals=0
        ),
        name="map_parts",
    )(lists, u, near, far, weights)


def finish_kernel(pieces, *refs):
    stats_refs, (e_ref, m_ref, m_top_ref, out_ref, nll_ref) = refs[:pieces], refs[pieces:]
    stats = [ref[k : k + 8, :] for ref in stats_refs for k in range(0, ref.shape[0], 8)]
    shards = range(len(stats))
    row = lambda s, k: stats[s][k : k + 1, :]
    top_l = functools.reduce(jnp.maximum, [row(s, 0) for s in shards])
    top_q = functools.reduce(jnp.maximum, [row(s, 2) for s in shards])
    sum_l = functools.reduce(jnp.add, [row(s, 1) * jnp.exp(row(s, 0) - top_l) for s in shards])
    sum_q = functools.reduce(jnp.add, [row(s, 3) * jnp.exp(row(s, 2) - top_q) for s in shards])
    part_l = [jnp.exp(row(s, 0) - top_l) / sum_l for s in shards]
    part_q = [jnp.exp(row(s, 2) - top_q) / sum_q for s in shards]
    mass = functools.reduce(jnp.add, [row(s, 4) * part_q[s] for s in shards])
    pick_e = functools.reduce(jnp.add, [row(s, 5) * part_l[s] for s in shards])
    pick_m = functools.reduce(jnp.add, [row(s, 6) * part_q[s] for s in shards])
    log_norm = jnp.log1p(mass)
    nll_ref[...] = log_norm - jnp.log(jnp.maximum(pick_e, FLOOR) + pick_m)
    tile = jnp.concatenate([part_l[0], top_q, 1.0 / sum_q, log_norm, jnp.zeros((4, log_norm.shape[1]), f32)], axis=0)
    turned = jnp.transpose(tile)
    a, top, share, c = (turned[:, i : i + 1] for i in range(4))
    b = jnp.exp(m_top_ref[:, :1] - top) * share
    out_ref[...] = jnp.log(jnp.maximum(e_ref[...] * a, FLOOR) + m_ref[...] * b) - c


def finish(pieces, e, m, m_top):
    rows, cols = e.shape
    return pl.pallas_call(
        functools.partial(finish_kernel, len(pieces)),
        out_shape=[
            jax.ShapeDtypeStruct((rows, cols), f32),
            jax.ShapeDtypeStruct((1, rows), f32),
        ],
        compiler_params=params(),
        cost_estimate=pl.CostEstimate(
            flops=20 * rows * cols, bytes_accessed=12 * rows * cols, transcendentals=2 * rows * cols
        ),
        name="finish",
    )(*pieces, e, m, m_top)


def gather_pieces(own, shards):
    pieces, step = [own], 1
    while step < shards:
        radix = 4 if step > 1 and 4 * step <= shards else 2
        sent = pieces[0] if len(pieces) == 1 else jnp.concatenate(pieces, axis=0)
        for turn in range(1, radix):
            pieces.append(lax.ppermute(sent, "vocab", [(i, i ^ (turn * step)) for i in range(shards)]))
        step *= radix
    return pieces, sent


def on_device(
    hidden, norm_gain, head_weights, pair_source, pair_target, pair_count, pair_weight, next_token
):
    shards = lax.axis_size("vocab")
    row_groups = lax.axis_size("rows")
    hidden, head = hidden[0], head_weights[0]
    token = next_token[None, :]
    held_hidden = pltpu.with_memory_space_constraint(hidden, pltpu.HBM)
    held_weight = pltpu.with_memory_space_constraint(pair_weight, pltpu.HBM)
    held_gain = pltpu.with_memory_space_constraint(norm_gain, pltpu.HBM)
    held_head = pltpu.with_memory_space_constraint(head, pltpu.HBM)
    width = pair_weight.shape[1]
    features = hidden.shape[1] * row_groups
    lists = jnp.concatenate([pair_source, pair_target, pair_count])

    inside = [(i, i ^ 1) for i in range(shards)]
    across = [(i, i + 1 if i % 2 else i - 1) for i in range(1, shards - 1)]
    lefts, squares, head = first_prep(held_hidden, held_gain, held_head, (3, 1))
    (to_d,) = encode_parts(product(lefts[0], head), squares[:1])
    from_d = lax.ppermute(to_d, ("mp", "rows"), [(0, 3), (1, 2), (2, 1), (3, 0)])
    left_y, _ = lax.optimization_barrier((lefts[1], to_d))
    (to_y,) = encode_parts(product(left_y, head), squares[1:2])
    from_y = lax.ppermute(to_y, "rows", [(0, 1), (1, 0)])
    late_gain, _ = lax.optimization_barrier((norm_gain, to_y))
    left_x, squares_x = prep_rows(held_hidden, late_gain, 2)
    (to_x,) = encode_parts(product(left_x, head), [squares_x])
    from_x = lax.ppermute(to_x, "mp", [(0, 1), (1, 0)])
    early, _ = lax.optimization_barrier((lists, to_x))
    (to_near, columns, to_far), left_own, squares_own, head = side_parts(
        early, token, held_hidden, held_gain, held_weight, held_head, width
    )
    own = product(left_own, head)
    to_near, _ = lax.optimization_barrier((to_near, own))
    near_columns = lax.ppermute(to_near, "vocab", inside)
    far_columns = lax.ppermute(to_far, "vocab", across)

    codes = (from_y, from_x, from_d)
    u, stats = join_qwen(own, squares_own, codes, width, features)
    far = lax.ppermute(u, "vocab", across)
    e, stats = join_llama(
        own, squares_own, codes, token, u, (near_columns, columns, far_columns), stats, width, features
    )
    pieces, last = gather_pieces(stats, shards)
    late_u, _ = lax.optimization_barrier((u, last))
    near = lax.ppermute(late_u, "vocab", inside)
    m, m_top = map_parts(lists, u, near, far, pair_weight, width, shards)
    out, nll = finish(pieces, e, m, m_top)
    return out, nll[0]


def solution(mesh):
    in_specs = (
        P("mp", None, "rows"),
        P("mp", "rows"),
        P("mp", "rows", "vocab"),
        P("vocab"),
        P("vocab"),
        P("vocab"),
        P("vocab", None, None),
        P(("mp", "rows")),
    )
    out_specs = (P(("mp", "rows"), "vocab"), P(("mp", "rows")))
    return jax.shard_map(
        on_device, mesh=mesh, in_specs=in_specs, out_specs=out_specs, check_vma=False
    )
```

```python
import functools

import jax
import jax.numpy as jnp
from jax import lax
from jax.experimental import pallas as pl
from jax.experimental.pallas import tpu as pltpu
from jax.sharding import PartitionSpec as P

LANES = 128
EXTRA = 16
CODE = 512
HEAD_COPIES = 1
TOP = 32700.0
ROUNDER = 12582912.0
LEAST = 1e-30
FLOOR = 1.9287498479639178e-22
VMEM = 16 * 1024 * 1024

f32, bf16, i32, i16 = jnp.float32, jnp.bfloat16, jnp.int32, jnp.int16


def params():
    return pltpu.CompilerParams(vmem_limit_bytes=VMEM)


def exponent(value):
    return jnp.ceil(jnp.log2(jnp.maximum(value, LEAST)))


def columns_to_lanes(values, rows):
    lanes = lax.broadcasted_iota(i32, (rows, LANES), 1)
    out = jnp.zeros((rows, LANES), f32)
    for place, value in enumerate(values):
        out = jnp.where(lanes == place, value, out)
    return out


def split_exact(gained):
    high = gained.astype(bf16)
    return high, (gained - high.astype(f32)).astype(bf16)


def encode(values, power):
    wide = values * (jnp.exp2(-power) * (TOP * TOP))
    root = wide * lax.rsqrt(jnp.maximum(jnp.abs(wide), LEAST))
    return ((root + ROUNDER) - ROUNDER).astype(i32).astype(i16)


def decode(codes, power):
    wide = codes.astype(i32).astype(f32)
    return wide * jnp.abs(wide) * (jnp.exp2(power) * (1.0 / (TOP * TOP)))


def encode_scalar(value):
    power = exponent(value)
    mantissa = jnp.maximum(value, LEAST) * jnp.exp2(-power) * 16384.0
    first = jnp.floor(mantissa)
    return power, first, jnp.floor((mantissa - first) * 16384.0)


def decode_scalar(power, first, second):
    return (first + second * (1.0 / 16384.0)) * (1.0 / 16384.0) * jnp.exp2(power)


def prepare(hidden, gain, left_ref, at):
    rows = hidden.shape[0]
    values = hidden.astype(f32)
    high, low = split_exact(values * gain)
    left_ref[pl.ds(at, rows), :] = high
    left_ref[pl.ds(at + rows, rows), :] = low
    return jnp.sum(values * values, axis=1, keepdims=True)


def put_codes(out_ref, both, first):
    rows = both.shape[0] // 2
    part = both[:rows] + both[rows:]
    power = exponent(jnp.max(jnp.abs(part), axis=1, keepdims=True))
    codes = encode(part, power)
    for k in range(part.shape[1] // LANES):
        out_ref[pl.ds((first // LANES + k) * rows, rows), :] = codes[:, k * LANES : (k + 1) * LANES]
    return power


def put_extra(out_ref, powers, squares):
    rows = squares.shape[0]
    extra = columns_to_lanes(powers + list(encode_scalar(squares)), rows)
    body = out_ref.shape[0] - EXTRA
    out_ref[pl.ds(body, EXTRA), :] = jnp.transpose(extra)[:EXTRA].astype(i32).astype(i16)


def first_kernel(kinds, rows, hidden_ref, gain_ref, head_ref, *refs):
    count = len(kinds)
    left_refs, square_refs, head_out = refs[:count], refs[count : 2 * count], refs[2 * count]
    held, gain_held, sems, gain_sem, head_sems = refs[2 * count + 1 :]
    copies = []
    for place, which in enumerate(kinds):
        quarter = jnp.bitwise_xor(2 * lax.axis_index("mp") + lax.axis_index("rows"), which)
        at = pl.ds(pl.multiple_of(quarter * rows, rows), rows)
        copies.append(pltpu.make_async_copy(hidden_ref.at[at, :], held.at[place], sems.at[place]))
    gain_copy = pltpu.make_async_copy(gain_ref, gain_held, gain_sem)
    deep = head_ref.shape[0] // HEAD_COPIES
    spans = [pl.ds(k * deep, deep) for k in range(HEAD_COPIES)]
    head_copies = [
        pltpu.make_async_copy(head_ref.at[at, :], head_out.at[at, :], head_sems.at[k])
        for k, at in enumerate(spans)
    ]
    gain_copy.start()
    for copy in copies + head_copies:
        copy.start()
    gain_copy.wait()
    gain = gain_held[...].astype(f32)
    for place, copy in enumerate(copies):
        copy.wait()
        squares = prepare(held[place], gain, left_refs[place], 0)
        square_refs[place][...] = jnp.broadcast_to(squares, (rows, LANES))
    for copy in head_copies:
        copy.wait()


def first_prep(hidden, gain, head, kinds):
    rows, feats, count = hidden.shape[0] // 4, hidden.shape[1], len(kinds)
    hbm = pl.BlockSpec(memory_space=pltpu.HBM)
    outs = pl.pallas_call(
        functools.partial(first_kernel, kinds, rows),
        in_specs=[hbm, hbm, hbm],
        out_shape=[jax.ShapeDtypeStruct((2 * rows, feats), bf16)] * count
        + [jax.ShapeDtypeStruct((rows, LANES), f32)] * count
        + [jax.ShapeDtypeStruct(head.shape, head.dtype)],
        scratch_shapes=[
            pltpu.VMEM((count, rows, feats), bf16),
            pltpu.VMEM(gain.shape, bf16),
            pltpu.SemaphoreType.DMA((count,)),
            pltpu.SemaphoreType.DMA,
            pltpu.SemaphoreType.DMA((HEAD_COPIES,)),
        ],
        compiler_params=params(),
        cost_estimate=pl.CostEstimate(
            flops=8 * count * rows * feats, bytes_accessed=2 * head.size, transcendentals=0
        ),
        name="first_prep",
    )(hidden, gain, head)
    return outs[:count], outs[count : 2 * count], outs[2 * count]


def encode_kernel(count, both_ref, *refs):
    square_refs, outs = refs[:count], refs[count:]
    rows, cols = both_ref.shape[0] // count // 2, both_ref.shape[1]
    for place, out_ref in enumerate(outs):
        powers = []
        for first in range(0, cols, CODE):
            both = both_ref[pl.ds(2 * place * rows, 2 * rows), pl.ds(first, CODE)]
            powers.append(put_codes(out_ref, both, first))
        put_extra(out_ref, powers, square_refs[place][:, :1])


def encode_parts(both, squares):
    count = len(squares)
    rows, cols = both.shape[0] // count // 2, both.shape[1]
    return pl.pallas_call(
        functools.partial(encode_kernel, count),
        out_shape=[jax.ShapeDtypeStruct((cols // LANES * rows + EXTRA, LANES), i16)] * count,
        compiler_params=params(),
        cost_estimate=pl.CostEstimate(
            flops=20 * count * rows * cols, bytes_accessed=10 * count * rows * cols, transcendentals=count * rows * cols
        ),
        name="encode_parts",
    )(both, *squares)


def product(left, head):
    return jnp.dot(left, head, preferred_element_type=f32)


def side_kernel(width, blocks, lists_ref, token_ref, hidden_ref, gain_ref, w_ref, head_ref, near_ref, own_ref, far_ref, left_ref, squares_ref, head_out, held, gain_held, w_held, sum_ref, meta_ref, sem, gain_sem, w_sems, head_sem, meta_sem):
    rows = token_ref.shape[1]
    slots = w_ref.shape[0]
    meta_copy = pltpu.make_async_copy(lists_ref, meta_ref, meta_sem)
    meta_copy.start()
    quarter = 2 * lax.axis_index("mp") + lax.axis_index("rows")
    at = pl.ds(pl.multiple_of(quarter * rows, rows), rows)
    hidden_copy = pltpu.make_async_copy(hidden_ref.at[at, :], held, sem)
    gain_copy = pltpu.make_async_copy(gain_ref, gain_held, gain_sem)
    w_copies = [pltpu.make_async_copy(w_ref.at[k], w_held.at[k], w_sems.at[k]) for k in range(slots)]
    gain_copy.start()
    hidden_copy.start()
    for copy in w_copies:
        copy.start()
    head_copy = pltpu.make_async_copy(head_ref, head_out, head_sem)
    head_copy.start()
    shard = lax.axis_index("vocab")
    near_at = jnp.where(shard % 2 == 0, 2, 0)
    token = jnp.transpose(jnp.broadcast_to(token_ref[...].astype(f32), (8, rows)))[:, :1].astype(i32)
    place = lax.broadcasted_iota(i32, (rows, width), 1)
    sum_ref[...] = jnp.zeros_like(sum_ref)
    gain_copy.wait()
    hidden_copy.wait()
    squares = prepare(held[...], gain_held[...].astype(f32), left_ref, 0)
    squares_ref[...] = jnp.broadcast_to(squares, (rows, LANES))
    meta_copy.wait()
    for slot in range(slots):
        w_copies[slot].wait()

        @pl.when(slot < meta_ref[2 * slots])
        def _():
            source = jnp.clip(meta_ref[slot] - (shard - 1) * blocks, 0, 3 * blocks - 1)
            hits = (token - meta_ref[slots + slot] * width == place).astype(bf16)
            left = jnp.concatenate([hits, jnp.ones((EXTRA, width), bf16)], axis=0)
            found = lax.dot_general(
                left, w_held[slot], (((1,), (1,)), ((), ())), preferred_element_type=f32
            )
            at = pl.ds(pl.multiple_of(source % blocks * width, width), width)
            sum_ref[source // blocks, :, at] += found

    order = lax.broadcasted_iota(i32, (EXTRA, 1), 0)
    for out_ref, k in ((near_ref, near_at), (own_ref, 1), (far_ref, 2 - near_at)):
        out_ref[pl.ds(0, rows), :] = sum_ref[k, pl.ds(0, rows), :].astype(bf16)
        sums = sum_ref[k, pl.ds(rows, EXTRA), :]
        first = sums.astype(bf16).astype(f32)
        second = (sums - first).astype(bf16).astype(f32)
        third = sums - first - second
        parts = jnp.where(order == 0, first, jnp.where(order == 1, second, jnp.where(order == 2, third, 0.0)))
        out_ref[pl.ds(rows, EXTRA), :] = parts.astype(bf16)
    near_ref[pl.ds(rows + EXTRA, EXTRA), :] = jnp.zeros((EXTRA, near_ref.shape[1]), bf16)
    head_copy.wait()


def side_parts(lists, token, hidden, gain, weights, head, width):
    rows, feats, cols = token.shape[1], hidden.shape[1], head.shape[1]
    hbm = pl.BlockSpec(memory_space=pltpu.HBM)
    outs = pl.pallas_call(
        functools.partial(side_kernel, width, cols // width),
        in_specs=[pl.BlockSpec(memory_space=pl.ANY), pl.BlockSpec(memory_space=pltpu.VMEM), hbm, hbm, hbm, hbm],
        out_shape=[jax.ShapeDtypeStruct((rows + many * EXTRA, cols), bf16) for many in (2, 1, 1)]
        + [jax.ShapeDtypeStruct((2 * rows, feats), bf16), jax.ShapeDtypeStruct((rows, LANES), f32)]
        + [jax.ShapeDtypeStruct(head.shape, head.dtype)],
        scratch_shapes=[
            pltpu.VMEM((rows, feats), bf16),
            pltpu.VMEM(gain.shape, bf16),
            pltpu.VMEM(weights.shape, bf16),
            pltpu.VMEM((3, rows + EXTRA, cols), f32),
            pltpu.SMEM(lists.shape, i32),
            pltpu.SemaphoreType.DMA,
            pltpu.SemaphoreType.DMA,
            pltpu.SemaphoreType.DMA((weights.shape[0],)),
            pltpu.SemaphoreType.DMA,
            pltpu.SemaphoreType.DMA,
        ],
        compiler_params=params(),
        cost_estimate=pl.CostEstimate(flops=1, bytes_accessed=1, transcendentals=0),
        name="side_parts",
    )(lists, token, hidden, gain, weights, head)
    return outs[:3], outs[3], outs[4], outs[5]


def extras(ref, rows):
    tile = ref[pl.ds(ref.shape[0] - EXTRA, EXTRA), :].astype(i32).astype(f32)
    wide = jnp.transpose(tile)
    groups = (ref.shape[0] - EXTRA) // rows * LANES // CODE
    at = [wide[:, j : j + 1] for j in range(groups + 3)]
    return at[:groups], decode_scalar(*at[groups:])


def model_logits(mine, features, own_ref, squares_ref, cy_ref, cx_ref, cd_ref, out_ref):
    rows = squares_ref.shape[0]
    cols = own_ref.shape[1]

    def run(scale, at_slab):
        for slab in range(cols // LANES):
            out_ref[:, pl.ds(slab * LANES, LANES)] = at_slab(slab) * scale

    @pl.when(mine)
    def _():
        power_y, squares_y = extras(cy_ref, rows)

        def at_slab(slab):
            at = pl.ds(slab * LANES, LANES)
            own = own_ref[pl.ds(0, rows), at] + own_ref[pl.ds(rows, rows), at]
            return own + decode(cy_ref[pl.ds(slab * rows, rows), :], power_y[slab * LANES // CODE])

        run(lax.rsqrt((squares_ref[:, :1] + squares_y) / features + 1e-05), at_slab)

    @pl.when(jnp.logical_not(mine))
    def _():
        power_x, squares_x = extras(cx_ref, rows)
        power_d, squares_d = extras(cd_ref, rows)

        def at_slab(slab):
            part, group = pl.ds(slab * rows, rows), slab * LANES // CODE
            return decode(cx_ref[part, :], power_x[group]) + decode(cd_ref[part, :], power_d[group])

        run(lax.rsqrt((squares_x + squares_d) / features + 1e-05), at_slab)

    peak = jnp.full((rows, LANES), -jnp.inf, f32)
    for slab in range(cols // LANES):
        peak = jnp.maximum(peak, out_ref[:, pl.ds(slab * LANES, LANES)])
    return jnp.max(peak, axis=1, keepdims=True)


def qwen_kernel(width, blocks, features, own_ref, squares_ref, cy_ref, cx_ref, cd_ref, u_ref, stats_ref, q_ref):
    rows = squares_ref.shape[0]
    body = blocks * width
    peak = model_logits(lax.axis_index("mp") == 1, features, own_ref, squares_ref, cy_ref, cx_ref, cd_ref, q_ref)
    total = jnp.zeros((rows, 1), f32)
    for j in range(blocks):
        at = pl.ds(j * width, width)
        qwen = jnp.exp(q_ref[:, at] - peak)
        u_ref[:, at] = qwen.astype(bf16)
        total += jnp.sum(qwen, axis=1, keepdims=True)
    first = peak.astype(bf16).astype(f32)
    second = (peak - first).astype(bf16).astype(f32)
    third = peak - first - second
    u_ref[:, body:] = columns_to_lanes([first, second, third], rows).astype(bf16)
    stats_ref[...] = columns_to_lanes([peak, total], rows)


def join_qwen(own, squares, codes, width, features):
    rows, cols = own.shape[0] // 2, own.shape[1]
    whole = pl.BlockSpec(memory_space=pltpu.VMEM)
    return pl.pallas_call(
        functools.partial(qwen_kernel, width, cols // width, features),
        in_specs=[whole] * 5,
        out_shape=[
            jax.ShapeDtypeStruct((rows, cols + LANES), bf16),
            jax.ShapeDtypeStruct((rows, LANES), f32),
        ],
        scratch_shapes=[pltpu.VMEM((rows, cols), f32)],
        compiler_params=params(),
        cost_estimate=pl.CostEstimate(flops=20000000000, bytes_accessed=8 * 1024 * 1024, transcendentals=0),
        name="join_qwen",
    )(own, squares, *codes)


def llama_kernel(width, blocks, features, own_ref, squares_ref, cy_ref, cx_ref, cd_ref, token_ref, u_ref, near_ref, mine_ref, far_ref, before_ref, e_ref, stats_ref):
    rows = squares_ref.shape[0]
    body = blocks * width
    columns_refs = (near_ref, mine_ref, far_ref)
    peak = model_logits(lax.axis_index("mp") == 0, features, own_ref, squares_ref, cy_ref, cx_ref, cd_ref, e_ref)
    total = jnp.zeros((rows, 1), f32)
    mass = jnp.zeros((rows, 1), f32)
    pick_e = jnp.zeros((rows, 1), f32)
    pick_m = jnp.zeros((rows, 1), f32)
    token = jnp.transpose(jnp.broadcast_to(token_ref[...].astype(f32), (8, rows)))
    token = token[:, :1].astype(i32) - lax.axis_index("vocab") * body
    for j in range(blocks):
        at = pl.ds(j * width, width)
        llama = jnp.exp(e_ref[:, at] - peak)
        e_ref[:, at] = llama
        total += jnp.sum(llama, axis=1, keepdims=True)
        hit = lax.broadcasted_iota(i32, (rows, width), 1) + j * width == token
        pick_e += jnp.sum(jnp.where(hit, llama, 0.0), axis=1, keepdims=True)
        held = u_ref[:, at].astype(f32)
        columns = functools.reduce(jnp.add, [ref[pl.ds(0, rows), at].astype(f32) for ref in columns_refs])
        pick_m += jnp.sum(held * columns, axis=1, keepdims=True)
        sums = functools.reduce(jnp.add, [ref[pl.ds(rows, EXTRA), at].astype(f32) for ref in columns_refs])
        mass += jnp.sum(held * jnp.sum(sums, axis=0, keepdims=True), axis=1, keepdims=True)
    before = before_ref[...]
    stats = columns_to_lanes([peak, total, before[:, 0:1], before[:, 1:2], mass, pick_e, pick_m], rows)
    stats_ref[...] = jnp.transpose(stats)[:8]


def join_llama(own, squares, codes, token, u, columns, stats, width, features):
    rows, cols = own.shape[0] // 2, own.shape[1]
    whole = pl.BlockSpec(memory_space=pltpu.VMEM)
    return pl.pallas_call(
        functools.partial(llama_kernel, width, cols // width, features),
        in_specs=[whole] * 11,
        out_shape=[jax.ShapeDtypeStruct((rows, cols), f32), jax.ShapeDtypeStruct((8, rows), f32)],
        compiler_params=params(),
        cost_estimate=pl.CostEstimate(flops=20000000000, bytes_accessed=8 * 1024 * 1024, transcendentals=0),
        name="join_llama",
    )(own, squares, *codes, token, u, *columns, stats)


def map_kernel(width, blocks, shards, lists_ref, u_ref, near_ref, far_ref, w_ref, m_ref, top_ref, all_ref, scale_ref, meta_ref, meta_sem):
    rows = u_ref.shape[0]
    body = blocks * width
    meta_copy = pltpu.make_async_copy(lists_ref, meta_ref, meta_sem)
    meta_copy.start()
    shard = lax.axis_index("vocab")
    slots = w_ref.shape[0]
    near_at = jnp.where(shard % 2 == 0, 2, 0)

    def peak_of(ref):
        lanes = ref[:, body:].astype(f32)
        return lanes[:, 0:1] + lanes[:, 1:2] + lanes[:, 2:3]

    own_peak = peak_of(u_ref)
    near_peak = peak_of(near_ref)
    far_peak = jnp.where((shard > 0) & (shard < shards - 1), peak_of(far_ref), own_peak)
    top = jnp.maximum(jnp.maximum(near_peak, far_peak), own_peak)
    for k, ref, peak in ((near_at, near_ref, near_peak), (1, u_ref, own_peak), (2 - near_at, far_ref, far_peak)):
        all_ref[k] = ref[:, :body]
        scale_ref[k] = jnp.broadcast_to(jnp.exp(peak - top), (rows, LANES))
    m_ref[...] = jnp.zeros_like(m_ref)
    meta_copy.wait()
    for slot in range(slots):

        @pl.when(slot < meta_ref[2 * slots])
        def _():
            source = jnp.clip(meta_ref[slot] - (shard - 1) * blocks, 0, 3 * blocks - 1)
            target = jnp.clip(meta_ref[slots + slot] - shard * blocks, 0, blocks - 1)
            inside = pl.multiple_of(source % blocks * width, width)
            picked = all_ref[source // blocks, :, pl.ds(inside, width)]
            term = jnp.dot(picked, w_ref[slot], preferred_element_type=f32)
            at = pl.ds(pl.multiple_of(target * width, width), width)
            m_ref[:, at] += term * scale_ref[source // blocks][:, :1]

    top_ref[...] = jnp.broadcast_to(top, (rows, LANES))


def map_parts(lists, u, near, far, weights, width, shards):
    rows, cols = u.shape[0], u.shape[1] - LANES
    blocks = cols // width
    whole = pl.BlockSpec(memory_space=pltpu.VMEM)
    return pl.pallas_call(
        functools.partial(map_kernel, width, blocks, shards),
        in_specs=[pl.BlockSpec(memory_space=pl.ANY)] + [whole] * 4,
        out_shape=[jax.ShapeDtypeStruct((rows, cols), f32), jax.ShapeDtypeStruct((rows, LANES), f32)],
        scratch_shapes=[pltpu.VMEM((3, rows, cols), bf16), pltpu.VMEM((3, rows, LANES), f32)]
        + [pltpu.SMEM(lists.shape, i32), pltpu.SemaphoreType.DMA],
        compiler_params=params(),
        cost_estimate=pl.CostEstimate(
            flops=2 * rows * weights.size, bytes_accessed=2 * weights.size, transcendentals=0
        ),
        name="map_parts",
    )(lists, u, near, far, weights)


def finish_kernel(pieces, *refs):
    stats_refs, (e_ref, m_ref, m_top_ref, out_ref, nll_ref) = refs[:pieces], refs[pieces:]
    stats = [ref[k : k + 8, :] for ref in stats_refs for k in range(0, ref.shape[0], 8)]
    shards = range(len(stats))
    row = lambda s, k: stats[s][k : k + 1, :]
    top_l = functools.reduce(jnp.maximum, [row(s, 0) for s in shards])
    top_q = functools.reduce(jnp.maximum, [row(s, 2) for s in shards])
    sum_l = functools.reduce(jnp.add, [row(s, 1) * jnp.exp(row(s, 0) - top_l) for s in shards])
    sum_q = functools.reduce(jnp.add, [row(s, 3) * jnp.exp(row(s, 2) - top_q) for s in shards])
    part_l = [jnp.exp(row(s, 0) - top_l) / sum_l for s in shards]
    part_q = [jnp.exp(row(s, 2) - top_q) / sum_q for s in shards]
    mass = functools.reduce(jnp.add, [row(s, 4) * part_q[s] for s in shards])
    pick_e = functools.reduce(jnp.add, [row(s, 5) * part_l[s] for s in shards])
    pick_m = functools.reduce(jnp.add, [row(s, 6) * part_q[s] for s in shards])
    log_norm = jnp.log1p(mass)
    nll_ref[...] = log_norm - jnp.log(jnp.maximum(pick_e, FLOOR) + pick_m)
    tile = jnp.concatenate([part_l[0], top_q, 1.0 / sum_q, log_norm, jnp.zeros((4, log_norm.shape[1]), f32)], axis=0)
    turned = jnp.transpose(tile)
    a, top, share, c = (turned[:, i : i + 1] for i in range(4))
    b = jnp.exp(m_top_ref[:, :1] - top) * share
    out_ref[...] = jnp.log(jnp.maximum(e_ref[...] * a, FLOOR) + m_ref[...] * b) - c


def finish(pieces, e, m, m_top):
    rows, cols = e.shape
    return pl.pallas_call(
        functools.partial(finish_kernel, len(pieces)),
        out_shape=[
            jax.ShapeDtypeStruct((rows, cols), f32),
            jax.ShapeDtypeStruct((1, rows), f32),
        ],
        compiler_params=params(),
        cost_estimate=pl.CostEstimate(
            flops=20 * rows * cols, bytes_accessed=12 * rows * cols, transcendentals=2 * rows * cols
        ),
        name="finish",
    )(*pieces, e, m, m_top)


def gather_pieces(own, shards):
    pieces, step = [own], 1
    while step < shards:
        radix = 4 if step > 1 and 4 * step <= shards else 2
        sent = pieces[0] if len(pieces) == 1 else jnp.concatenate(pieces, axis=0)
        for turn in range(1, radix):
            pieces.append(lax.ppermute(sent, "vocab", [(i, i ^ (turn * step)) for i in range(shards)]))
        step *= radix
    return pieces, sent


def on_device(
    hidden, norm_gain, head_weights, pair_source, pair_target, pair_count, pair_weight, next_token
):
    shards = lax.axis_size("vocab")
    row_groups = lax.axis_size("rows")
    hidden, head = hidden[0], head_weights[0]
    token = next_token[None, :]
    held_hidden = pltpu.with_memory_space_constraint(hidden, pltpu.HBM)
    held_weight = pltpu.with_memory_space_constraint(pair_weight, pltpu.HBM)
    held_gain = pltpu.with_memory_space_constraint(norm_gain, pltpu.HBM)
    held_head = pltpu.with_memory_space_constraint(head, pltpu.HBM)
    width = pair_weight.shape[1]
    features = hidden.shape[1] * row_groups
    lists = jnp.concatenate([pair_source, pair_target, pair_count])

    inside = [(i, i ^ 1) for i in range(shards)]
    across = [(i, i + 1 if i % 2 else i - 1) for i in range(1, shards - 1)]
    lefts, squares, head = first_prep(held_hidden, held_gain, held_head, (3, 1, 2))
    (to_d,) = encode_parts(product(lefts[0], head), squares[:1])
    from_d = lax.ppermute(to_d, ("mp", "rows"), [(0, 3), (1, 2), (2, 1), (3, 0)])
    left_y, _ = lax.optimization_barrier((lefts[1], to_d))
    (to_y,) = encode_parts(product(left_y, head), squares[1:2])
    from_y = lax.ppermute(to_y, "rows", [(0, 1), (1, 0)])
    left_x, _ = lax.optimization_barrier((lefts[2], to_y))
    (to_x,) = encode_parts(product(left_x, head), squares[2:])
    from_x = lax.ppermute(to_x, "mp", [(0, 1), (1, 0)])
    early, _ = lax.optimization_barrier((lists, to_x))
    (to_near, columns, to_far), left_own, squares_own, head = side_parts(
        early, token, held_hidden, held_gain, held_weight, held_head, width
    )
    own = product(left_own, head)
    to_near, _ = lax.optimization_barrier((to_near, own))
    near_columns = lax.ppermute(to_near, "vocab", inside)
    far_columns = lax.ppermute(to_far, "vocab", across)

    codes = (from_y, from_x, from_d)
    u, stats = join_qwen(own, squares_own, codes, width, features)
    far = lax.ppermute(u, "vocab", across)
    e, stats = join_llama(
        own, squares_own, codes, token, u, (near_columns, columns, far_columns), stats, width, features
    )
    pieces, last = gather_pieces(stats, shards)
    late_u, _ = lax.optimization_barrier((u, last))
    near = lax.ppermute(late_u, "vocab", inside)
    m, m_top = map_parts(lists, u, near, far, pair_weight, width, shards)
    out, nll = finish(pieces, e, m, m_top)
    return out, nll[0]


def solution(mesh):
    in_specs = (
        P("mp", None, "rows"),
        P("mp", "rows"),
        P("mp", "rows", "vocab"),
        P("vocab"),
        P("vocab"),
        P("vocab"),
        P("vocab", None, None),
        P(("mp", "rows")),
    )
    out_specs = (P(("mp", "rows"), "vocab"), P(("mp", "rows")))
    return jax.shard_map(
        on_device, mesh=mesh, in_specs=in_specs, out_specs=out_specs, check_vma=False
    )
```

```python
import functools

import jax
import jax.numpy as jnp
from jax import lax
from jax.experimental import pallas as pl
from jax.experimental.pallas import tpu as pltpu
from jax.sharding import PartitionSpec as P

LANES = 128
EXTRA = 16
CODE = 512
HEAD_COPIES = 1
TOP = 32700.0
ROUNDER = 12582912.0
LEAST = 1e-30
FLOOR = 1.9287498479639178e-22
VMEM = 16 * 1024 * 1024

f32, bf16, i32, i16 = jnp.float32, jnp.bfloat16, jnp.int32, jnp.int16


def params():
    return pltpu.CompilerParams(vmem_limit_bytes=VMEM)


def exponent(value):
    return jnp.ceil(jnp.log2(jnp.maximum(value, LEAST)))


def columns_to_lanes(values, rows):
    lanes = lax.broadcasted_iota(i32, (rows, LANES), 1)
    out = jnp.zeros((rows, LANES), f32)
    for place, value in enumerate(values):
        out = jnp.where(lanes == place, value, out)
    return out


def split_exact(gained):
    high = gained.astype(bf16)
    return high, (gained - high.astype(f32)).astype(bf16)


def encode(values, power):
    wide = values * (jnp.exp2(-power) * (TOP * TOP))
    root = wide * lax.rsqrt(jnp.maximum(jnp.abs(wide), LEAST))
    return ((root + ROUNDER) - ROUNDER).astype(i32).astype(i16)


def decode(codes, power):
    wide = codes.astype(i32).astype(f32)
    return wide * jnp.abs(wide) * (jnp.exp2(power) * (1.0 / (TOP * TOP)))


def encode_scalar(value):
    power = exponent(value)
    mantissa = jnp.maximum(value, LEAST) * jnp.exp2(-power) * 16384.0
    first = jnp.floor(mantissa)
    return power, first, jnp.floor((mantissa - first) * 16384.0)


def decode_scalar(power, first, second):
    return (first + second * (1.0 / 16384.0)) * (1.0 / 16384.0) * jnp.exp2(power)


def prepare(hidden, gain, left_ref, at):
    rows = hidden.shape[0]
    values = hidden.astype(f32)
    high, low = split_exact(values * gain)
    left_ref[pl.ds(at, rows), :] = high
    left_ref[pl.ds(at + rows, rows), :] = low
    return jnp.sum(values * values, axis=1, keepdims=True)


def put_codes(out_ref, both, first):
    rows = both.shape[0] // 2
    part = both[:rows] + both[rows:]
    power = exponent(jnp.max(jnp.abs(part), axis=1, keepdims=True))
    codes = encode(part, power)
    for k in range(part.shape[1] // LANES):
        out_ref[pl.ds((first // LANES + k) * rows, rows), :] = codes[:, k * LANES : (k + 1) * LANES]
    return power


def put_extra(out_ref, powers, squares):
    rows = squares.shape[0]
    extra = columns_to_lanes(powers + list(encode_scalar(squares)), rows)
    body = out_ref.shape[0] - EXTRA
    out_ref[pl.ds(body, EXTRA), :] = jnp.transpose(extra)[:EXTRA].astype(i32).astype(i16)


def first_kernel(kinds, rows, hidden_ref, gain_ref, head_ref, *refs):
    count = len(kinds)
    left_refs, square_refs, head_out = refs[:count], refs[count : 2 * count], refs[2 * count]
    held, gain_held, sems, gain_sem, head_sems = refs[2 * count + 1 :]
    copies = []
    for place, which in enumerate(kinds):
        quarter = jnp.bitwise_xor(2 * lax.axis_index("mp") + lax.axis_index("rows"), which)
        at = pl.ds(pl.multiple_of(quarter * rows, rows), rows)
        copies.append(pltpu.make_async_copy(hidden_ref.at[at, :], held.at[place], sems.at[place]))
    gain_copy = pltpu.make_async_copy(gain_ref, gain_held, gain_sem)
    deep = head_ref.shape[0] // HEAD_COPIES
    spans = [pl.ds(k * deep, deep) for k in range(HEAD_COPIES)]
    head_copies = [
        pltpu.make_async_copy(head_ref.at[at, :], head_out.at[at, :], head_sems.at[k])
        for k, at in enumerate(spans)
    ]
    gain_copy.start()
    for copy in copies + head_copies:
        copy.start()
    gain_copy.wait()
    gain = gain_held[...].astype(f32)
    for place, copy in enumerate(copies):
        copy.wait()
        squares = prepare(held[place], gain, left_refs[place], 0)
        square_refs[place][...] = jnp.broadcast_to(squares, (rows, LANES))
    for copy in head_copies:
        copy.wait()


def first_prep(hidden, gain, head, kinds):
    rows, feats, count = hidden.shape[0] // 4, hidden.shape[1], len(kinds)
    hbm = pl.BlockSpec(memory_space=pltpu.HBM)
    outs = pl.pallas_call(
        functools.partial(first_kernel, kinds, rows),
        in_specs=[hbm, hbm, hbm],
        out_shape=[jax.ShapeDtypeStruct((2 * rows, feats), bf16)] * count
        + [jax.ShapeDtypeStruct((rows, LANES), f32)] * count
        + [jax.ShapeDtypeStruct(head.shape, head.dtype)],
        scratch_shapes=[
            pltpu.VMEM((count, rows, feats), bf16),
            pltpu.VMEM(gain.shape, bf16),
            pltpu.SemaphoreType.DMA((count,)),
            pltpu.SemaphoreType.DMA,
            pltpu.SemaphoreType.DMA((HEAD_COPIES,)),
        ],
        compiler_params=params(),
        cost_estimate=pl.CostEstimate(
            flops=8 * count * rows * feats, bytes_accessed=2 * head.size, transcendentals=0
        ),
        name="first_prep",
    )(hidden, gain, head)
    return outs[:count], outs[count : 2 * count], outs[2 * count]


def encode_kernel(count, both_ref, *refs):
    square_refs, outs = refs[:count], refs[count:]
    rows, cols = both_ref.shape[0] // count // 2, both_ref.shape[1]
    for place, out_ref in enumerate(outs):
        powers = []
        for first in range(0, cols, CODE):
            both = both_ref[pl.ds(2 * place * rows, 2 * rows), pl.ds(first, CODE)]
            powers.append(put_codes(out_ref, both, first))
        put_extra(out_ref, powers, square_refs[place][:, :1])


def encode_parts(both, squares):
    count = len(squares)
    rows, cols = both.shape[0] // count // 2, both.shape[1]
    return pl.pallas_call(
        functools.partial(encode_kernel, count),
        out_shape=[jax.ShapeDtypeStruct((cols // LANES * rows + EXTRA, LANES), i16)] * count,
        compiler_params=params(),
        cost_estimate=pl.CostEstimate(
            flops=20 * count * rows * cols, bytes_accessed=10 * count * rows * cols, transcendentals=count * rows * cols
        ),
        name="encode_parts",
    )(both, *squares)


def product(left, head):
    return jnp.dot(left, head, preferred_element_type=f32)


def side_kernel(width, blocks, lists_ref, token_ref, hidden_ref, gain_ref, w_ref, head_ref, near_ref, own_ref, far_ref, left_ref, squares_ref, head_out, held, gain_held, w_held, sum_ref, meta_ref, sem, gain_sem, w_sems, head_sem, meta_sem):
    rows = token_ref.shape[1]
    slots = w_ref.shape[0]
    meta_copy = pltpu.make_async_copy(lists_ref, meta_ref, meta_sem)
    meta_copy.start()
    quarter = 2 * lax.axis_index("mp") + lax.axis_index("rows")
    at = pl.ds(pl.multiple_of(quarter * rows, rows), rows)
    hidden_copy = pltpu.make_async_copy(hidden_ref.at[at, :], held, sem)
    gain_copy = pltpu.make_async_copy(gain_ref, gain_held, gain_sem)
    w_copies = [pltpu.make_async_copy(w_ref.at[k], w_held.at[k], w_sems.at[k]) for k in range(slots)]
    gain_copy.start()
    hidden_copy.start()
    for copy in w_copies:
        copy.start()
    head_copy = pltpu.make_async_copy(head_ref, head_out, head_sem)
    head_copy.start()
    shard = lax.axis_index("vocab")
    near_at = jnp.where(shard % 2 == 0, 2, 0)
    token = jnp.transpose(jnp.broadcast_to(token_ref[...].astype(f32), (8, rows)))[:, :1].astype(i32)
    place = lax.broadcasted_iota(i32, (rows, width), 1)
    sum_ref[...] = jnp.zeros_like(sum_ref)
    gain_copy.wait()
    hidden_copy.wait()
    squares = prepare(held[...], gain_held[...].astype(f32), left_ref, 0)
    squares_ref[...] = jnp.broadcast_to(squares, (rows, LANES))
    meta_copy.wait()
    for slot in range(slots):
        w_copies[slot].wait()

        @pl.when(slot < meta_ref[2 * slots])
        def _():
            source = jnp.clip(meta_ref[slot] - (shard - 1) * blocks, 0, 3 * blocks - 1)
            hits = (token - meta_ref[slots + slot] * width == place).astype(bf16)
            left = jnp.concatenate([hits, jnp.ones((EXTRA, width), bf16)], axis=0)
            found = lax.dot_general(
                left, w_held[slot], (((1,), (1,)), ((), ())), preferred_element_type=f32
            )
            at = pl.ds(pl.multiple_of(source % blocks * width, width), width)
            sum_ref[source // blocks, :, at] += found

    order = lax.broadcasted_iota(i32, (EXTRA, 1), 0)
    for out_ref, k in ((near_ref, near_at), (own_ref, 1), (far_ref, 2 - near_at)):
        out_ref[pl.ds(0, rows), :] = sum_ref[k, pl.ds(0, rows), :].astype(bf16)
        sums = sum_ref[k, pl.ds(rows, EXTRA), :]
        first = sums.astype(bf16).astype(f32)
        second = (sums - first).astype(bf16).astype(f32)
        third = sums - first - second
        parts = jnp.where(order == 0, first, jnp.where(order == 1, second, jnp.where(order == 2, third, 0.0)))
        out_ref[pl.ds(rows, EXTRA), :] = parts.astype(bf16)
    near_ref[pl.ds(rows + EXTRA, EXTRA), :] = jnp.zeros((EXTRA, near_ref.shape[1]), bf16)
    head_copy.wait()


def side_parts(lists, token, hidden, gain, weights, head, width):
    rows, feats, cols = token.shape[1], hidden.shape[1], head.shape[1]
    hbm = pl.BlockSpec(memory_space=pltpu.HBM)
    outs = pl.pallas_call(
        functools.partial(side_kernel, width, cols // width),
        in_specs=[pl.BlockSpec(memory_space=pl.ANY), pl.BlockSpec(memory_space=pltpu.VMEM), hbm, hbm, hbm, hbm],
        out_shape=[jax.ShapeDtypeStruct((rows + many * EXTRA, cols), bf16) for many in (2, 1, 1)]
        + [jax.ShapeDtypeStruct((2 * rows, feats), bf16), jax.ShapeDtypeStruct((rows, LANES), f32)]
        + [jax.ShapeDtypeStruct(head.shape, head.dtype)],
        scratch_shapes=[
            pltpu.VMEM((rows, feats), bf16),
            pltpu.VMEM(gain.shape, bf16),
            pltpu.VMEM(weights.shape, bf16),
            pltpu.VMEM((3, rows + EXTRA, cols), f32),
            pltpu.SMEM(lists.shape, i32),
            pltpu.SemaphoreType.DMA,
            pltpu.SemaphoreType.DMA,
            pltpu.SemaphoreType.DMA((weights.shape[0],)),
            pltpu.SemaphoreType.DMA,
            pltpu.SemaphoreType.DMA,
        ],
        compiler_params=params(),
        cost_estimate=pl.CostEstimate(flops=1, bytes_accessed=1, transcendentals=0),
        name="side_parts",
    )(lists, token, hidden, gain, weights, head)
    return outs[:3], outs[3], outs[4], outs[5]


def extras(ref, rows):
    tile = ref[pl.ds(ref.shape[0] - EXTRA, EXTRA), :].astype(i32).astype(f32)
    wide = jnp.transpose(tile)
    groups = (ref.shape[0] - EXTRA) // rows * LANES // CODE
    at = [wide[:, j : j + 1] for j in range(groups + 3)]
    return at[:groups], decode_scalar(*at[groups:])


def model_logits(mine, features, own_ref, squares_ref, cy_ref, cx_ref, cd_ref, out_ref):
    rows = squares_ref.shape[0]
    cols = own_ref.shape[1]

    def run(scale, at_slab):
        for slab in range(cols // LANES):
            out_ref[:, pl.ds(slab * LANES, LANES)] = at_slab(slab) * scale

    @pl.when(mine)
    def _():
        power_y, squares_y = extras(cy_ref, rows)

        def at_slab(slab):
            at = pl.ds(slab * LANES, LANES)
            own = own_ref[pl.ds(0, rows), at] + own_ref[pl.ds(rows, rows), at]
            return own + decode(cy_ref[pl.ds(slab * rows, rows), :], power_y[slab * LANES // CODE])

        run(lax.rsqrt((squares_ref[:, :1] + squares_y) / features + 1e-05), at_slab)

    @pl.when(jnp.logical_not(mine))
    def _():
        power_x, squares_x = extras(cx_ref, rows)
        power_d, squares_d = extras(cd_ref, rows)

        def at_slab(slab):
            part, group = pl.ds(slab * rows, rows), slab * LANES // CODE
            return decode(cx_ref[part, :], power_x[group]) + decode(cd_ref[part, :], power_d[group])

        run(lax.rsqrt((squares_x + squares_d) / features + 1e-05), at_slab)

    peak = jnp.full((rows, LANES), -jnp.inf, f32)
    for slab in range(cols // LANES):
        peak = jnp.maximum(peak, out_ref[:, pl.ds(slab * LANES, LANES)])
    return jnp.max(peak, axis=1, keepdims=True)


def qwen_kernel(width, blocks, features, own_ref, squares_ref, cy_ref, cx_ref, cd_ref, u_ref, stats_ref, q_ref):
    rows = squares_ref.shape[0]
    body = blocks * width
    peak = model_logits(lax.axis_index("mp") == 1, features, own_ref, squares_ref, cy_ref, cx_ref, cd_ref, q_ref)
    total = jnp.zeros((rows, 1), f32)
    for j in range(blocks):
        at = pl.ds(j * width, width)
        qwen = jnp.exp(q_ref[:, at] - peak)
        held = qwen.astype(bf16)
        for k in range(width // LANES):
            slab = j * (width // LANES) + k
            u_ref[pl.ds(slab * rows, rows), :] = held[:, k * LANES : (k + 1) * LANES]
        total += jnp.sum(qwen, axis=1, keepdims=True)
    first = peak.astype(bf16).astype(f32)
    second = (peak - first).astype(bf16).astype(f32)
    third = peak - first - second
    parts = jnp.transpose(columns_to_lanes([first, second, third], rows))[:EXTRA]
    u_ref[pl.ds(body // LANES * rows, EXTRA), :] = parts.astype(bf16)
    stats_ref[...] = columns_to_lanes([peak, total], rows)


def join_qwen(own, squares, codes, width, features):
    rows, cols = own.shape[0] // 2, own.shape[1]
    whole = pl.BlockSpec(memory_space=pltpu.VMEM)
    return pl.pallas_call(
        functools.partial(qwen_kernel, width, cols // width, features),
        in_specs=[whole] * 5,
        out_shape=[
            jax.ShapeDtypeStruct((cols // LANES * rows + EXTRA, LANES), bf16),
            jax.ShapeDtypeStruct((rows, LANES), f32),
        ],
        scratch_shapes=[pltpu.VMEM((rows, cols), f32)],
        compiler_params=params(),
        cost_estimate=pl.CostEstimate(flops=20000000000, bytes_accessed=8 * 1024 * 1024, transcendentals=0),
        name="join_qwen",
    )(own, squares, *codes)


def llama_kernel(width, blocks, features, own_ref, squares_ref, cy_ref, cx_ref, cd_ref, token_ref, u_ref, near_ref, mine_ref, far_ref, before_ref, e_ref, stats_ref):
    rows = squares_ref.shape[0]
    body = blocks * width
    columns_refs = (near_ref, mine_ref, far_ref)
    peak = model_logits(lax.axis_index("mp") == 0, features, own_ref, squares_ref, cy_ref, cx_ref, cd_ref, e_ref)
    total = jnp.zeros((rows, 1), f32)
    mass = jnp.zeros((rows, 1), f32)
    pick_e = jnp.zeros((rows, 1), f32)
    pick_m = jnp.zeros((rows, 1), f32)
    token = jnp.transpose(jnp.broadcast_to(token_ref[...].astype(f32), (8, rows)))
    token = token[:, :1].astype(i32) - lax.axis_index("vocab") * body
    for j in range(blocks):
        at = pl.ds(j * width, width)
        llama = jnp.exp(e_ref[:, at] - peak)
        e_ref[:, at] = llama
        total += jnp.sum(llama, axis=1, keepdims=True)
        hit = lax.broadcasted_iota(i32, (rows, width), 1) + j * width == token
        pick_e += jnp.sum(jnp.where(hit, llama, 0.0), axis=1, keepdims=True)
        slabs = range(j * (width // LANES), (j + 1) * (width // LANES))
        held = jnp.concatenate([u_ref[pl.ds(slab * rows, rows), :] for slab in slabs], axis=1).astype(f32)
        columns = functools.reduce(jnp.add, [ref[pl.ds(0, rows), at].astype(f32) for ref in columns_refs])
        pick_m += jnp.sum(held * columns, axis=1, keepdims=True)
        sums = functools.reduce(jnp.add, [ref[pl.ds(rows, EXTRA), at].astype(f32) for ref in columns_refs])
        mass += jnp.sum(held * jnp.sum(sums, axis=0, keepdims=True), axis=1, keepdims=True)
    before = before_ref[...]
    stats = columns_to_lanes([peak, total, before[:, 0:1], before[:, 1:2], mass, pick_e, pick_m], rows)
    stats_ref[...] = jnp.transpose(stats)[:8]


def join_llama(own, squares, codes, token, u, columns, stats, width, features):
    rows, cols = own.shape[0] // 2, own.shape[1]
    whole = pl.BlockSpec(memory_space=pltpu.VMEM)
    return pl.pallas_call(
        functools.partial(llama_kernel, width, cols // width, features),
        in_specs=[whole] * 11,
        out_shape=[jax.ShapeDtypeStruct((rows, cols), f32), jax.ShapeDtypeStruct((8, rows), f32)],
        compiler_params=params(),
        cost_estimate=pl.CostEstimate(flops=20000000000, bytes_accessed=8 * 1024 * 1024, transcendentals=0),
        name="join_llama",
    )(own, squares, *codes, token, u, *columns, stats)


def map_kernel(width, blocks, shards, lists_ref, u_ref, near_ref, far_ref, w_ref, m_ref, top_ref, all_ref, scale_ref, meta_ref, meta_sem):
    rows = m_ref.shape[0]
    body = blocks * width
    meta_copy = pltpu.make_async_copy(lists_ref, meta_ref, meta_sem)
    meta_copy.start()
    shard = lax.axis_index("vocab")
    slots = w_ref.shape[0]
    near_at = jnp.where(shard % 2 == 0, 2, 0)

    def peak_of(ref):
        lanes = jnp.transpose(ref[pl.ds(body // LANES * rows, EXTRA), :].astype(f32))
        return lanes[:, 0:1] + lanes[:, 1:2] + lanes[:, 2:3]

    own_peak = peak_of(u_ref)
    near_peak = peak_of(near_ref)
    far_peak = jnp.where((shard > 0) & (shard < shards - 1), peak_of(far_ref), own_peak)
    top = jnp.maximum(jnp.maximum(near_peak, far_peak), own_peak)
    for k, ref, peak in ((near_at, near_ref, near_peak), (1, u_ref, own_peak), (2 - near_at, far_ref, far_peak)):
        for slab in range(body // LANES):
            all_ref[k, :, pl.ds(slab * LANES, LANES)] = ref[pl.ds(slab * rows, rows), :]
        scale_ref[k] = jnp.broadcast_to(jnp.exp(peak - top), (rows, LANES))
    m_ref[...] = jnp.zeros_like(m_ref)
    meta_copy.wait()
    for slot in range(slots):

        @pl.when(slot < meta_ref[2 * slots])
        def _():
            source = jnp.clip(meta_ref[slot] - (shard - 1) * blocks, 0, 3 * blocks - 1)
            target = jnp.clip(meta_ref[slots + slot] - shard * blocks, 0, blocks - 1)
            inside = pl.multiple_of(source % blocks * width, width)
            picked = all_ref[source // blocks, :, pl.ds(inside, width)]
            term = jnp.dot(picked, w_ref[slot], preferred_element_type=f32)
            at = pl.ds(pl.multiple_of(target * width, width), width)
            m_ref[:, at] += term * scale_ref[source // blocks][:, :1]

    top_ref[...] = jnp.broadcast_to(top, (rows, LANES))


def map_parts(lists, u, near, far, weights, width, shards, rows):
    cols = (u.shape[0] - EXTRA) // rows * LANES
    blocks = cols // width
    whole = pl.BlockSpec(memory_space=pltpu.VMEM)
    return pl.pallas_call(
        functools.partial(map_kernel, width, blocks, shards),
        in_specs=[pl.BlockSpec(memory_space=pl.ANY)] + [whole] * 4,
        out_shape=[jax.ShapeDtypeStruct((rows, cols), f32), jax.ShapeDtypeStruct((rows, LANES), f32)],
        scratch_shapes=[pltpu.VMEM((3, rows, cols), bf16), pltpu.VMEM((3, rows, LANES), f32)]
        + [pltpu.SMEM(lists.shape, i32), pltpu.SemaphoreType.DMA],
        compiler_params=params(),
        cost_estimate=pl.CostEstimate(
            flops=2 * rows * weights.size, bytes_accessed=2 * weights.size, transcendentals=0
        ),
        name="map_parts",
    )(lists, u, near, far, weights)


def finish_kernel(pieces, *refs):
    stats_refs, (e_ref, m_ref, m_top_ref, out_ref, nll_ref) = refs[:pieces], refs[pieces:]
    stats = [ref[k : k + 8, :] for ref in stats_refs for k in range(0, ref.shape[0], 8)]
    shards = range(len(stats))
    row = lambda s, k: stats[s][k : k + 1, :]
    top_l = functools.reduce(jnp.maximum, [row(s, 0) for s in shards])
    top_q = functools.reduce(jnp.maximum, [row(s, 2) for s in shards])
    sum_l = functools.reduce(jnp.add, [row(s, 1) * jnp.exp(row(s, 0) - top_l) for s in shards])
    sum_q = functools.reduce(jnp.add, [row(s, 3) * jnp.exp(row(s, 2) - top_q) for s in shards])
    part_l = [jnp.exp(row(s, 0) - top_l) / sum_l for s in shards]
    part_q = [jnp.exp(row(s, 2) - top_q) / sum_q for s in shards]
    mass = functools.reduce(jnp.add, [row(s, 4) * part_q[s] for s in shards])
    pick_e = functools.reduce(jnp.add, [row(s, 5) * part_l[s] for s in shards])
    pick_m = functools.reduce(jnp.add, [row(s, 6) * part_q[s] for s in shards])
    log_norm = jnp.log1p(mass)
    nll_ref[...] = log_norm - jnp.log(jnp.maximum(pick_e, FLOOR) + pick_m)
    tile = jnp.concatenate([part_l[0], top_q, 1.0 / sum_q, log_norm, jnp.zeros((4, log_norm.shape[1]), f32)], axis=0)
    turned = jnp.transpose(tile)
    a, top, share, c = (turned[:, i : i + 1] for i in range(4))
    b = jnp.exp(m_top_ref[:, :1] - top) * share
    out_ref[...] = jnp.log(jnp.maximum(e_ref[...] * a, FLOOR) + m_ref[...] * b) - c


def finish(pieces, e, m, m_top):
    rows, cols = e.shape
    return pl.pallas_call(
        functools.partial(finish_kernel, len(pieces)),
        out_shape=[
            jax.ShapeDtypeStruct((rows, cols), f32),
            jax.ShapeDtypeStruct((1, rows), f32),
        ],
        compiler_params=params(),
        cost_estimate=pl.CostEstimate(
            flops=20 * rows * cols, bytes_accessed=12 * rows * cols, transcendentals=2 * rows * cols
        ),
        name="finish",
    )(*pieces, e, m, m_top)


def gather_pieces(own, shards):
    pieces, step = [own], 1
    while step < shards:
        radix = 4 if step > 1 and 4 * step <= shards else 2
        sent = pieces[0] if len(pieces) == 1 else jnp.concatenate(pieces, axis=0)
        for turn in range(1, radix):
            pieces.append(lax.ppermute(sent, "vocab", [(i, i ^ (turn * step)) for i in range(shards)]))
        step *= radix
    return pieces, sent


def on_device(
    hidden, norm_gain, head_weights, pair_source, pair_target, pair_count, pair_weight, next_token
):
    shards = lax.axis_size("vocab")
    row_groups = lax.axis_size("rows")
    hidden, head = hidden[0], head_weights[0]
    token = next_token[None, :]
    held_hidden = pltpu.with_memory_space_constraint(hidden, pltpu.HBM)
    held_weight = pltpu.with_memory_space_constraint(pair_weight, pltpu.HBM)
    held_gain = pltpu.with_memory_space_constraint(norm_gain, pltpu.HBM)
    held_head = pltpu.with_memory_space_constraint(head, pltpu.HBM)
    width = pair_weight.shape[1]
    features = hidden.shape[1] * row_groups
    lists = jnp.concatenate([pair_source, pair_target, pair_count])

    inside = [(i, i ^ 1) for i in range(shards)]
    across = [(i, i + 1 if i % 2 else i - 1) for i in range(1, shards - 1)]
    lefts, squares, head = first_prep(held_hidden, held_gain, held_head, (3, 1, 2))
    (to_d,) = encode_parts(product(lefts[0], head), squares[:1])
    from_d = lax.ppermute(to_d, ("mp", "rows"), [(0, 3), (1, 2), (2, 1), (3, 0)])
    left_y, _ = lax.optimization_barrier((lefts[1], to_d))
    (to_y,) = encode_parts(product(left_y, head), squares[1:2])
    from_y = lax.ppermute(to_y, "rows", [(0, 1), (1, 0)])
    left_x, _ = lax.optimization_barrier((lefts[2], to_y))
    (to_x,) = encode_parts(product(left_x, head), squares[2:])
    from_x = lax.ppermute(to_x, "mp", [(0, 1), (1, 0)])
    early, _ = lax.optimization_barrier((lists, to_x))
    (to_near, columns, to_far), left_own, squares_own, head = side_parts(
        early, token, held_hidden, held_gain, held_weight, held_head, width
    )
    own = product(left_own, head)
    to_near, _ = lax.optimization_barrier((to_near, own))
    near_columns = lax.ppermute(to_near, "vocab", inside)
    far_columns = lax.ppermute(to_far, "vocab", across)

    codes = (from_y, from_x, from_d)
    u, stats = join_qwen(own, squares_own, codes, width, features)
    far = lax.ppermute(u, "vocab", across)
    e, stats = join_llama(
        own, squares_own, codes, token, u, (near_columns, columns, far_columns), stats, width, features
    )
    pieces, last = gather_pieces(stats, shards)
    late_u, _ = lax.optimization_barrier((u, last))
    near = lax.ppermute(late_u, "vocab", inside)
    m, m_top = map_parts(lists, u, near, far, pair_weight, width, shards, e.shape[0])
    out, nll = finish(pieces, e, m, m_top)
    return out, nll[0]


def solution(mesh):
    in_specs = (
        P("mp", None, "rows"),
        P("mp", "rows"),
        P("mp", "rows", "vocab"),
        P("vocab"),
        P("vocab"),
        P("vocab"),
        P("vocab", None, None),
        P(("mp", "rows")),
    )
    out_specs = (P(("mp", "rows"), "vocab"), P(("mp", "rows")))
    return jax.shard_map(
        on_device, mesh=mesh, in_specs=in_specs, out_specs=out_specs, check_vma=False
    )
```

```python
import functools

import jax
import jax.numpy as jnp
from jax import lax
from jax.experimental import pallas as pl
from jax.experimental.pallas import tpu as pltpu
from jax.sharding import PartitionSpec as P

LANES = 128
EXTRA = 16
CODE = 512
HEAD_COPIES = 1
TOP = 32700.0
ROUNDER = 12582912.0
LEAST = 1e-30
FLOOR = 1.9287498479639178e-22
VMEM = 16 * 1024 * 1024

f32, bf16, i32, i16 = jnp.float32, jnp.bfloat16, jnp.int32, jnp.int16


def params():
    return pltpu.CompilerParams(vmem_limit_bytes=VMEM)


def exponent(value):
    return jnp.ceil(jnp.log2(jnp.maximum(value, LEAST)))


def columns_to_lanes(values, rows):
    lanes = lax.broadcasted_iota(i32, (rows, LANES), 1)
    out = jnp.zeros((rows, LANES), f32)
    for place, value in enumerate(values):
        out = jnp.where(lanes == place, value, out)
    return out


def split_exact(gained):
    high = gained.astype(bf16)
    return high, (gained - high.astype(f32)).astype(bf16)


def encode(values, power):
    wide = values * (jnp.exp2(-power) * (TOP * TOP))
    root = wide * lax.rsqrt(jnp.maximum(jnp.abs(wide), LEAST))
    return ((root + ROUNDER) - ROUNDER).astype(i32).astype(i16)


def decode(codes, power):
    wide = codes.astype(i32).astype(f32)
    return wide * jnp.abs(wide) * (jnp.exp2(power) * (1.0 / (TOP * TOP)))


def encode_scalar(value):
    power = exponent(value)
    mantissa = jnp.maximum(value, LEAST) * jnp.exp2(-power) * 16384.0
    first = jnp.floor(mantissa)
    return power, first, jnp.floor((mantissa - first) * 16384.0)


def decode_scalar(power, first, second):
    return (first + second * (1.0 / 16384.0)) * (1.0 / 16384.0) * jnp.exp2(power)


def prepare(hidden, gain, left_ref, at):
    rows = hidden.shape[0]
    values = hidden.astype(f32)
    high, low = split_exact(values * gain)
    left_ref[pl.ds(at, rows), :] = high
    left_ref[pl.ds(at + rows, rows), :] = low
    return jnp.sum(values * values, axis=1, keepdims=True)


def put_codes(out_ref, both, first):
    rows = both.shape[0] // 2
    part = both[:rows] + both[rows:]
    power = exponent(jnp.max(jnp.abs(part), axis=1, keepdims=True))
    codes = encode(part, power)
    for k in range(part.shape[1] // LANES):
        out_ref[pl.ds((first // LANES + k) * rows, rows), :] = codes[:, k * LANES : (k + 1) * LANES]
    return power


def put_extra(out_ref, powers, squares):
    rows = squares.shape[0]
    extra = columns_to_lanes(powers + list(encode_scalar(squares)), rows)
    body = out_ref.shape[0] - EXTRA
    out_ref[pl.ds(body, EXTRA), :] = jnp.transpose(extra)[:EXTRA].astype(i32).astype(i16)


def first_kernel(kinds, rows, hidden_ref, gain_ref, head_ref, *refs):
    count = len(kinds)
    left_refs, square_refs, head_out = refs[:count], refs[count : 2 * count], refs[2 * count]
    held, gain_held, sems, gain_sem, head_sems = refs[2 * count + 1 :]
    copies = []
    for place, which in enumerate(kinds):
        quarter = jnp.bitwise_xor(2 * lax.axis_index("mp") + lax.axis_index("rows"), which)
        at = pl.ds(pl.multiple_of(quarter * rows, rows), rows)
        copies.append(pltpu.make_async_copy(hidden_ref.at[at, :], held.at[place], sems.at[place]))
    gain_copy = pltpu.make_async_copy(gain_ref, gain_held, gain_sem)
    deep = head_ref.shape[0] // HEAD_COPIES
    spans = [pl.ds(k * deep, deep) for k in range(HEAD_COPIES)]
    head_copies = [
        pltpu.make_async_copy(head_ref.at[at, :], head_out.at[at, :], head_sems.at[k])
        for k, at in enumerate(spans)
    ]
    gain_copy.start()
    for copy in copies + head_copies:
        copy.start()
    gain_copy.wait()
    gain = gain_held[...].astype(f32)
    for place, copy in enumerate(copies):
        copy.wait()
        squares = prepare(held[place], gain, left_refs[place], 0)
        square_refs[place][...] = jnp.broadcast_to(squares, (rows, LANES))
    for copy in head_copies:
        copy.wait()


def first_prep(hidden, gain, head, kinds):
    rows, feats, count = hidden.shape[0] // 4, hidden.shape[1], len(kinds)
    hbm = pl.BlockSpec(memory_space=pltpu.HBM)
    outs = pl.pallas_call(
        functools.partial(first_kernel, kinds, rows),
        in_specs=[hbm, hbm, hbm],
        out_shape=[jax.ShapeDtypeStruct((2 * rows, feats), bf16)] * count
        + [jax.ShapeDtypeStruct((rows, LANES), f32)] * count
        + [jax.ShapeDtypeStruct(head.shape, head.dtype)],
        scratch_shapes=[
            pltpu.VMEM((count, rows, feats), bf16),
            pltpu.VMEM(gain.shape, bf16),
            pltpu.SemaphoreType.DMA((count,)),
            pltpu.SemaphoreType.DMA,
            pltpu.SemaphoreType.DMA((HEAD_COPIES,)),
        ],
        compiler_params=params(),
        cost_estimate=pl.CostEstimate(
            flops=8 * count * rows * feats, bytes_accessed=2 * head.size, transcendentals=0
        ),
        name="first_prep",
    )(hidden, gain, head)
    return outs[:count], outs[count : 2 * count], outs[2 * count]


def encode_kernel(count, both_ref, *refs):
    square_refs, outs = refs[:count], refs[count:]
    rows, cols = both_ref.shape[0] // count // 2, both_ref.shape[1]
    for place, out_ref in enumerate(outs):
        powers = []
        for first in range(0, cols, CODE):
            both = both_ref[pl.ds(2 * place * rows, 2 * rows), pl.ds(first, CODE)]
            powers.append(put_codes(out_ref, both, first))
        put_extra(out_ref, powers, square_refs[place][:, :1])


def encode_parts(both, squares):
    count = len(squares)
    rows, cols = both.shape[0] // count // 2, both.shape[1]
    return pl.pallas_call(
        functools.partial(encode_kernel, count),
        out_shape=[jax.ShapeDtypeStruct((cols // LANES * rows + EXTRA, LANES), i16)] * count,
        compiler_params=params(),
        cost_estimate=pl.CostEstimate(
            flops=20 * count * rows * cols, bytes_accessed=10 * count * rows * cols, transcendentals=count * rows * cols
        ),
        name="encode_parts",
    )(both, *squares)


def product(left, head):
    return jnp.dot(left, head, preferred_element_type=f32)


def side_kernel(width, blocks, lists_ref, token_ref, hidden_ref, gain_ref, w_ref, head_ref, near_ref, own_ref, far_ref, left_ref, squares_ref, head_out, held, gain_held, w_held, sum_ref, meta_ref, sem, gain_sem, w_sems, head_sem, meta_sem):
    rows = token_ref.shape[1]
    slots = w_ref.shape[0]
    meta_copy = pltpu.make_async_copy(lists_ref, meta_ref, meta_sem)
    meta_copy.start()
    quarter = 2 * lax.axis_index("mp") + lax.axis_index("rows")
    at = pl.ds(pl.multiple_of(quarter * rows, rows), rows)
    hidden_copy = pltpu.make_async_copy(hidden_ref.at[at, :], held, sem)
    gain_copy = pltpu.make_async_copy(gain_ref, gain_held, gain_sem)
    w_copies = [pltpu.make_async_copy(w_ref.at[k], w_held.at[k], w_sems.at[k]) for k in range(slots)]
    gain_copy.start()
    hidden_copy.start()
    for copy in w_copies:
        copy.start()
    head_copy = pltpu.make_async_copy(head_ref, head_out, head_sem)
    head_copy.start()
    shard = lax.axis_index("vocab")
    near_at = jnp.where(shard % 2 == 0, 2, 0)
    token = jnp.transpose(jnp.broadcast_to(token_ref[...].astype(f32), (8, rows)))[:, :1].astype(i32)
    place = lax.broadcasted_iota(i32, (rows, width), 1)
    sum_ref[...] = jnp.zeros_like(sum_ref)
    gain_copy.wait()
    hidden_copy.wait()
    squares = prepare(held[...], gain_held[...].astype(f32), left_ref, 0)
    squares_ref[...] = jnp.broadcast_to(squares, (rows, LANES))
    meta_copy.wait()
    for slot in range(slots):
        w_copies[slot].wait()

        @pl.when(slot < meta_ref[2 * slots])
        def _():
            source = jnp.clip(meta_ref[slot] - (shard - 1) * blocks, 0, 3 * blocks - 1)
            hits = (token - meta_ref[slots + slot] * width == place).astype(bf16)
            left = jnp.concatenate([hits, jnp.ones((EXTRA, width), bf16)], axis=0)
            found = lax.dot_general(
                left, w_held[slot], (((1,), (1,)), ((), ())), preferred_element_type=f32
            )
            at = pl.ds(pl.multiple_of(source % blocks * width, width), width)
            sum_ref[source // blocks, :, at] += found

    order = lax.broadcasted_iota(i32, (EXTRA, 1), 0)
    for out_ref, k in ((near_ref, near_at), (own_ref, 1), (far_ref, 2 - near_at)):
        out_ref[pl.ds(0, rows), :] = sum_ref[k, pl.ds(0, rows), :].astype(bf16)
        sums = sum_ref[k, pl.ds(rows, EXTRA), :]
        first = sums.astype(bf16).astype(f32)
        second = (sums - first).astype(bf16).astype(f32)
        third = sums - first - second
        parts = jnp.where(order == 0, first, jnp.where(order == 1, second, jnp.where(order == 2, third, 0.0)))
        out_ref[pl.ds(rows, EXTRA), :] = parts.astype(bf16)
    near_ref[pl.ds(rows + EXTRA, EXTRA), :] = jnp.zeros((EXTRA, near_ref.shape[1]), bf16)
    head_copy.wait()


def side_parts(lists, token, hidden, gain, weights, head, width):
    rows, feats, cols = token.shape[1], hidden.shape[1], head.shape[1]
    hbm = pl.BlockSpec(memory_space=pltpu.HBM)
    outs = pl.pallas_call(
        functools.partial(side_kernel, width, cols // width),
        in_specs=[pl.BlockSpec(memory_space=pl.ANY), pl.BlockSpec(memory_space=pltpu.VMEM), hbm, hbm, hbm, hbm],
        out_shape=[jax.ShapeDtypeStruct((rows + many * EXTRA, cols), bf16) for many in (2, 1, 1)]
        + [jax.ShapeDtypeStruct((2 * rows, feats), bf16), jax.ShapeDtypeStruct((rows, LANES), f32)]
        + [jax.ShapeDtypeStruct(head.shape, head.dtype)],
        scratch_shapes=[
            pltpu.VMEM((rows, feats), bf16),
            pltpu.VMEM(gain.shape, bf16),
            pltpu.VMEM(weights.shape, bf16),
            pltpu.VMEM((3, rows + EXTRA, cols), f32),
            pltpu.SMEM(lists.shape, i32),
            pltpu.SemaphoreType.DMA,
            pltpu.SemaphoreType.DMA,
            pltpu.SemaphoreType.DMA((weights.shape[0],)),
            pltpu.SemaphoreType.DMA,
            pltpu.SemaphoreType.DMA,
        ],
        compiler_params=params(),
        cost_estimate=pl.CostEstimate(flops=1, bytes_accessed=1, transcendentals=0),
        name="side_parts",
    )(lists, token, hidden, gain, weights, head)
    return outs[:3], outs[3], outs[4], outs[5]


def extras(ref, rows):
    tile = ref[pl.ds(ref.shape[0] - EXTRA, EXTRA), :].astype(i32).astype(f32)
    wide = jnp.transpose(tile)
    groups = (ref.shape[0] - EXTRA) // rows * LANES // CODE
    at = [wide[:, j : j + 1] for j in range(groups + 3)]
    return at[:groups], decode_scalar(*at[groups:])


def model_logits(mine, features, own_ref, squares_ref, cy_ref, cx_ref, cd_ref, out_ref):
    rows = squares_ref.shape[0]
    cols = own_ref.shape[1]

    def run(scale, at_slab):
        for slab in range(cols // LANES):
            out_ref[:, pl.ds(slab * LANES, LANES)] = at_slab(slab) * scale

    @pl.when(mine)
    def _():
        power_y, squares_y = extras(cy_ref, rows)

        def at_slab(slab):
            at = pl.ds(slab * LANES, LANES)
            own = own_ref[pl.ds(0, rows), at] + own_ref[pl.ds(rows, rows), at]
            return own + decode(cy_ref[pl.ds(slab * rows, rows), :], power_y[slab * LANES // CODE])

        run(lax.rsqrt((squares_ref[:, :1] + squares_y) / features + 1e-05), at_slab)

    @pl.when(jnp.logical_not(mine))
    def _():
        power_x, squares_x = extras(cx_ref, rows)
        power_d, squares_d = extras(cd_ref, rows)

        def at_slab(slab):
            part, group = pl.ds(slab * rows, rows), slab * LANES // CODE
            return decode(cx_ref[part, :], power_x[group]) + decode(cd_ref[part, :], power_d[group])

        run(lax.rsqrt((squares_x + squares_d) / features + 1e-05), at_slab)

    peak = jnp.full((rows, LANES), -jnp.inf, f32)
    for slab in range(cols // LANES):
        peak = jnp.maximum(peak, out_ref[:, pl.ds(slab * LANES, LANES)])
    return jnp.max(peak, axis=1, keepdims=True)


def qwen_kernel(width, blocks, features, own_ref, squares_ref, cy_ref, cx_ref, cd_ref, u_ref, stats_ref, q_ref):
    rows = squares_ref.shape[0]
    body = blocks * width
    peak = model_logits(lax.axis_index("mp") == 1, features, own_ref, squares_ref, cy_ref, cx_ref, cd_ref, q_ref)
    total = jnp.zeros((rows, 1), f32)
    for j in range(blocks):
        at = pl.ds(j * width, width)
        qwen = jnp.exp(q_ref[:, at] - peak)
        held = qwen.astype(bf16)
        for k in range(width // LANES):
            slab = j * (width // LANES) + k
            u_ref[pl.ds(slab * rows, rows), :] = held[:, k * LANES : (k + 1) * LANES]
        total += jnp.sum(qwen, axis=1, keepdims=True)
    first = peak.astype(bf16).astype(f32)
    second = (peak - first).astype(bf16).astype(f32)
    third = peak - first - second
    parts = jnp.transpose(columns_to_lanes([first, second, third], rows))[:EXTRA]
    u_ref[pl.ds(body // LANES * rows, EXTRA), :] = parts.astype(bf16)
    stats_ref[...] = columns_to_lanes([peak, total], rows)


def join_qwen(own, squares, codes, width, features):
    rows, cols = own.shape[0] // 2, own.shape[1]
    whole = pl.BlockSpec(memory_space=pltpu.VMEM)
    return pl.pallas_call(
        functools.partial(qwen_kernel, width, cols // width, features),
        in_specs=[whole] * 5,
        out_shape=[
            jax.ShapeDtypeStruct((cols // LANES * rows + EXTRA, LANES), bf16),
            jax.ShapeDtypeStruct((rows, LANES), f32),
        ],
        scratch_shapes=[pltpu.VMEM((rows, cols), f32)],
        compiler_params=params(),
        cost_estimate=pl.CostEstimate(flops=20000000000, bytes_accessed=8 * 1024 * 1024, transcendentals=0),
        name="join_qwen",
    )(own, squares, *codes)


def llama_kernel(width, blocks, features, own_ref, squares_ref, cy_ref, cx_ref, cd_ref, token_ref, u_ref, near_ref, mine_ref, far_ref, before_ref, e_ref, stats_ref):
    rows = squares_ref.shape[0]
    body = blocks * width
    columns_refs = (near_ref, mine_ref, far_ref)
    peak = model_logits(lax.axis_index("mp") == 0, features, own_ref, squares_ref, cy_ref, cx_ref, cd_ref, e_ref)
    total = jnp.zeros((rows, 1), f32)
    mass = jnp.zeros((rows, 1), f32)
    pick_e = jnp.zeros((rows, 1), f32)
    pick_m = jnp.zeros((rows, 1), f32)
    token = jnp.transpose(jnp.broadcast_to(token_ref[...].astype(f32), (8, rows)))
    token = token[:, :1].astype(i32) - lax.axis_index("vocab") * body
    for j in range(blocks):
        at = pl.ds(j * width, width)
        llama = jnp.exp(e_ref[:, at] - peak)
        e_ref[:, at] = llama
        total += jnp.sum(llama, axis=1, keepdims=True)
        hit = lax.broadcasted_iota(i32, (rows, width), 1) + j * width == token
        pick_e += jnp.sum(jnp.where(hit, llama, 0.0), axis=1, keepdims=True)
        slabs = range(j * (width // LANES), (j + 1) * (width // LANES))
        held = jnp.concatenate([u_ref[pl.ds(slab * rows, rows), :] for slab in slabs], axis=1).astype(f32)
        columns = functools.reduce(jnp.add, [ref[pl.ds(0, rows), at].astype(f32) for ref in columns_refs])
        pick_m += jnp.sum(held * columns, axis=1, keepdims=True)
        sums = functools.reduce(jnp.add, [ref[pl.ds(rows, EXTRA), at].astype(f32) for ref in columns_refs])
        mass += jnp.sum(held * jnp.sum(sums, axis=0, keepdims=True), axis=1, keepdims=True)
    before = before_ref[...]
    stats = columns_to_lanes([peak, total, before[:, 0:1], before[:, 1:2], mass, pick_e, pick_m], rows)
    stats_ref[...] = jnp.transpose(stats)[:8]


def join_llama(own, squares, codes, token, u, columns, stats, width, features):
    rows, cols = own.shape[0] // 2, own.shape[1]
    whole = pl.BlockSpec(memory_space=pltpu.VMEM)
    return pl.pallas_call(
        functools.partial(llama_kernel, width, cols // width, features),
        in_specs=[whole] * 11,
        out_shape=[jax.ShapeDtypeStruct((rows, cols), f32), jax.ShapeDtypeStruct((8, rows), f32)],
        compiler_params=params(),
        cost_estimate=pl.CostEstimate(flops=20000000000, bytes_accessed=8 * 1024 * 1024, transcendentals=0),
        name="join_llama",
    )(own, squares, *codes, token, u, *columns, stats)


def map_kernel(width, blocks, shards, lists_ref, u_ref, near_ref, far_ref, w_ref, m_ref, top_ref, all_ref, scale_ref, meta_ref, meta_sem):
    rows = m_ref.shape[0]
    body = blocks * width
    meta_copy = pltpu.make_async_copy(lists_ref, meta_ref, meta_sem)
    meta_copy.start()
    shard = lax.axis_index("vocab")
    slots = w_ref.shape[0]
    near_at = jnp.where(shard % 2 == 0, 2, 0)

    def peak_of(ref):
        lanes = jnp.transpose(ref[pl.ds(body // LANES * rows, EXTRA), :].astype(f32))
        return lanes[:, 0:1] + lanes[:, 1:2] + lanes[:, 2:3]

    own_peak = peak_of(u_ref)
    near_peak = peak_of(near_ref)
    far_peak = jnp.where((shard > 0) & (shard < shards - 1), peak_of(far_ref), own_peak)
    top = jnp.maximum(jnp.maximum(near_peak, far_peak), own_peak)
    for k, ref, peak in ((near_at, near_ref, near_peak), (1, u_ref, own_peak), (2 - near_at, far_ref, far_peak)):
        for slab in range(body // LANES):
            all_ref[k, :, pl.ds(slab * LANES, LANES)] = ref[pl.ds(slab * rows, rows), :]
        scale_ref[k] = jnp.broadcast_to(jnp.exp(peak - top), (rows, LANES))
    m_ref[...] = jnp.zeros_like(m_ref)
    meta_copy.wait()
    for slot in range(slots):

        @pl.when(slot < meta_ref[2 * slots])
        def _():
            source = jnp.clip(meta_ref[slot] - (shard - 1) * blocks, 0, 3 * blocks - 1)
            target = jnp.clip(meta_ref[slots + slot] - shard * blocks, 0, blocks - 1)
            inside = pl.multiple_of(source % blocks * width, width)
            picked = all_ref[source // blocks, :, pl.ds(inside, width)]
            term = jnp.dot(picked, w_ref[slot], preferred_element_type=f32)
            at = pl.ds(pl.multiple_of(target * width, width), width)
            m_ref[:, at] += term * scale_ref[source // blocks][:, :1]

    top_ref[...] = jnp.broadcast_to(top, (rows, LANES))


def map_parts(lists, u, near, far, weights, width, shards, rows):
    cols = (u.shape[0] - EXTRA) // rows * LANES
    blocks = cols // width
    whole = pl.BlockSpec(memory_space=pltpu.VMEM)
    return pl.pallas_call(
        functools.partial(map_kernel, width, blocks, shards),
        in_specs=[pl.BlockSpec(memory_space=pl.ANY)] + [whole] * 4,
        out_shape=[jax.ShapeDtypeStruct((rows, cols), f32), jax.ShapeDtypeStruct((rows, LANES), f32)],
        scratch_shapes=[pltpu.VMEM((3, rows, cols), bf16), pltpu.VMEM((3, rows, LANES), f32)]
        + [pltpu.SMEM(lists.shape, i32), pltpu.SemaphoreType.DMA],
        compiler_params=params(),
        cost_estimate=pl.CostEstimate(
            flops=2 * rows * weights.size, bytes_accessed=2 * weights.size, transcendentals=0
        ),
        name="map_parts",
    )(lists, u, near, far, weights)


def finish_kernel(pieces, *refs):
    stats_refs, (e_ref, m_ref, m_top_ref, out_ref, nll_ref) = refs[:pieces], refs[pieces:]
    stats = [ref[k : k + 8, :] for ref in stats_refs for k in range(0, ref.shape[0], 8)]
    shards = range(len(stats))
    row = lambda s, k: stats[s][k : k + 1, :]
    top_l = functools.reduce(jnp.maximum, [row(s, 0) for s in shards])
    top_q = functools.reduce(jnp.maximum, [row(s, 2) for s in shards])
    sum_l = functools.reduce(jnp.add, [row(s, 1) * jnp.exp(row(s, 0) - top_l) for s in shards])
    sum_q = functools.reduce(jnp.add, [row(s, 3) * jnp.exp(row(s, 2) - top_q) for s in shards])
    part_l = [jnp.exp(row(s, 0) - top_l) / sum_l for s in shards]
    part_q = [jnp.exp(row(s, 2) - top_q) / sum_q for s in shards]
    mass = functools.reduce(jnp.add, [row(s, 4) * part_q[s] for s in shards])
    pick_e = functools.reduce(jnp.add, [row(s, 5) * part_l[s] for s in shards])
    pick_m = functools.reduce(jnp.add, [row(s, 6) * part_q[s] for s in shards])
    log_norm = jnp.log1p(mass)
    nll_ref[...] = log_norm - jnp.log(jnp.maximum(pick_e, FLOOR) + pick_m)
    tile = jnp.concatenate([part_l[0], top_q, 1.0 / sum_q, log_norm, jnp.zeros((4, log_norm.shape[1]), f32)], axis=0)
    turned = jnp.transpose(tile)
    a, top, share, c = (turned[:, i : i + 1] for i in range(4))
    b = jnp.exp(m_top_ref[:, :1] - top) * share
    out_ref[...] = jnp.log(jnp.maximum(e_ref[...] * a, FLOOR) + m_ref[...] * b) - c


def finish(pieces, e, m, m_top):
    rows, cols = e.shape
    return pl.pallas_call(
        functools.partial(finish_kernel, len(pieces)),
        out_shape=[
            jax.ShapeDtypeStruct((rows, cols), f32),
            jax.ShapeDtypeStruct((1, rows), f32),
        ],
        compiler_params=params(),
        cost_estimate=pl.CostEstimate(
            flops=20 * rows * cols, bytes_accessed=12 * rows * cols, transcendentals=2 * rows * cols
        ),
        name="finish",
    )(*pieces, e, m, m_top)


def gather_pieces(own, shards):
    pieces, step = [own], 1
    while step < shards:
        radix = 4 if step > 1 and 4 * step <= shards else 2
        sent = pieces[0] if len(pieces) == 1 else jnp.concatenate(pieces, axis=0)
        for turn in (1, 3, 2)[: radix - 1] if radix == 4 else (1,):
            pieces.append(lax.ppermute(sent, "vocab", [(i, i ^ (turn * step)) for i in range(shards)]))
        step *= radix
    return pieces, sent


def on_device(
    hidden, norm_gain, head_weights, pair_source, pair_target, pair_count, pair_weight, next_token
):
    shards = lax.axis_size("vocab")
    row_groups = lax.axis_size("rows")
    hidden, head = hidden[0], head_weights[0]
    token = next_token[None, :]
    held_hidden = pltpu.with_memory_space_constraint(hidden, pltpu.HBM)
    held_weight = pltpu.with_memory_space_constraint(pair_weight, pltpu.HBM)
    held_gain = pltpu.with_memory_space_constraint(norm_gain, pltpu.HBM)
    held_head = pltpu.with_memory_space_constraint(head, pltpu.HBM)
    width = pair_weight.shape[1]
    features = hidden.shape[1] * row_groups
    lists = jnp.concatenate([pair_source, pair_target, pair_count])

    inside = [(i, i ^ 1) for i in range(shards)]
    across = [(i, i + 1 if i % 2 else i - 1) for i in range(1, shards - 1)]
    lefts, squares, head = first_prep(held_hidden, held_gain, held_head, (3, 1, 2))
    (to_d,) = encode_parts(product(lefts[0], head), squares[:1])
    from_d = lax.ppermute(to_d, ("mp", "rows"), [(0, 3), (1, 2), (2, 1), (3, 0)])
    left_y, _ = lax.optimization_barrier((lefts[1], to_d))
    (to_y,) = encode_parts(product(left_y, head), squares[1:2])
    from_y = lax.ppermute(to_y, "rows", [(0, 1), (1, 0)])
    left_x, _ = lax.optimization_barrier((lefts[2], to_y))
    (to_x,) = encode_parts(product(left_x, head), squares[2:])
    from_x = lax.ppermute(to_x, "mp", [(0, 1), (1, 0)])
    early, _ = lax.optimization_barrier((lists, to_x))
    (to_near, columns, to_far), left_own, squares_own, head = side_parts(
        early, token, held_hidden, held_gain, held_weight, held_head, width
    )
    own = product(left_own, head)
    to_near, _ = lax.optimization_barrier((to_near, own))
    near_columns = lax.ppermute(to_near, "vocab", inside)
    far_columns = lax.ppermute(to_far, "vocab", across)

    codes = (from_y, from_x, from_d)
    u, stats = join_qwen(own, squares_own, codes, width, features)
    far = lax.ppermute(u, "vocab", across)
    e, stats = join_llama(
        own, squares_own, codes, token, u, (near_columns, columns, far_columns), stats, width, features
    )
    pieces, last = gather_pieces(stats, shards)
    late_u, _ = lax.optimization_barrier((u, last))
    near = lax.ppermute(late_u, "vocab", inside)
    m, m_top = map_parts(lists, u, near, far, pair_weight, width, shards, e.shape[0])
    out, nll = finish(pieces, e, m, m_top)
    return out, nll[0]


def solution(mesh):
    in_specs = (
        P("mp", None, "rows"),
        P("mp", "rows"),
        P("mp", "rows", "vocab"),
        P("vocab"),
        P("vocab"),
        P("vocab"),
        P("vocab", None, None),
        P(("mp", "rows")),
    )
    out_specs = (P(("mp", "rows"), "vocab"), P(("mp", "rows")))
    return jax.shard_map(
        on_device, mesh=mesh, in_specs=in_specs, out_specs=out_specs, check_vma=False
    )
```

```python
import functools

import jax
import jax.numpy as jnp
from jax import lax
from jax.experimental import pallas as pl
from jax.experimental.pallas import tpu as pltpu
from jax.sharding import PartitionSpec as P

LANES = 128
EXTRA = 16
CODE = 512
HEAD_COPIES = 1
TOP = 32700.0
ROUNDER = 12582912.0
LEAST = 1e-30
FLOOR = 1.9287498479639178e-22
VMEM = 16 * 1024 * 1024

f32, bf16, i32, i16 = jnp.float32, jnp.bfloat16, jnp.int32, jnp.int16


def params():
    return pltpu.CompilerParams(vmem_limit_bytes=VMEM)


def exponent(value):
    return jnp.ceil(jnp.log2(jnp.maximum(value, LEAST)))


def columns_to_lanes(values, rows):
    lanes = lax.broadcasted_iota(i32, (rows, LANES), 1)
    out = jnp.zeros((rows, LANES), f32)
    for place, value in enumerate(values):
        out = jnp.where(lanes == place, value, out)
    return out


def split_exact(gained):
    high = gained.astype(bf16)
    return high, (gained - high.astype(f32)).astype(bf16)


def encode(values, power):
    wide = values * (jnp.exp2(-power) * (TOP * TOP))
    root = wide * lax.rsqrt(jnp.maximum(jnp.abs(wide), LEAST))
    return ((root + ROUNDER) - ROUNDER).astype(i32).astype(i16)


def decode(codes, power):
    wide = codes.astype(i32).astype(f32)
    return wide * jnp.abs(wide) * (jnp.exp2(power) * (1.0 / (TOP * TOP)))


def encode_scalar(value):
    power = exponent(value)
    mantissa = jnp.maximum(value, LEAST) * jnp.exp2(-power) * 16384.0
    first = jnp.floor(mantissa)
    return power, first, jnp.floor((mantissa - first) * 16384.0)


def decode_scalar(power, first, second):
    return (first + second * (1.0 / 16384.0)) * (1.0 / 16384.0) * jnp.exp2(power)


def prepare(hidden, gain, left_ref, at):
    rows = hidden.shape[0]
    values = hidden.astype(f32)
    high, low = split_exact(values * gain)
    left_ref[pl.ds(at, rows), :] = high
    left_ref[pl.ds(at + rows, rows), :] = low
    return jnp.sum(values * values, axis=1, keepdims=True)


def put_codes(out_ref, both, first):
    rows = both.shape[0] // 2
    part = both[:rows] + both[rows:]
    power = exponent(jnp.max(jnp.abs(part), axis=1, keepdims=True))
    codes = encode(part, power)
    for k in range(part.shape[1] // LANES):
        out_ref[pl.ds((first // LANES + k) * rows, rows), :] = codes[:, k * LANES : (k + 1) * LANES]
    return power


def put_extra(out_ref, powers, squares):
    rows = squares.shape[0]
    extra = columns_to_lanes(powers + list(encode_scalar(squares)), rows)
    body = out_ref.shape[0] - EXTRA
    out_ref[pl.ds(body, EXTRA), :] = jnp.transpose(extra)[:EXTRA].astype(i32).astype(i16)


def first_kernel(kinds, rows, hidden_ref, gain_ref, head_ref, *refs):
    count = len(kinds)
    left_refs, square_refs, head_out = refs[:count], refs[count : 2 * count], refs[2 * count]
    held, gain_held, sems, gain_sem, head_sems = refs[2 * count + 1 :]
    copies = []
    for place, which in enumerate(kinds):
        quarter = jnp.bitwise_xor(2 * lax.axis_index("mp") + lax.axis_index("rows"), which)
        at = pl.ds(pl.multiple_of(quarter * rows, rows), rows)
        copies.append(pltpu.make_async_copy(hidden_ref.at[at, :], held.at[place], sems.at[place]))
    gain_copy = pltpu.make_async_copy(gain_ref, gain_held, gain_sem)
    deep = head_ref.shape[0] // HEAD_COPIES
    spans = [pl.ds(k * deep, deep) for k in range(HEAD_COPIES)]
    head_copies = [
        pltpu.make_async_copy(head_ref.at[at, :], head_out.at[at, :], head_sems.at[k])
        for k, at in enumerate(spans)
    ]
    gain_copy.start()
    for copy in copies + head_copies:
        copy.start()
    gain_copy.wait()
    gain = gain_held[...].astype(f32)
    for place, copy in enumerate(copies):
        copy.wait()
        squares = prepare(held[place], gain, left_refs[place], 0)
        square_refs[place][...] = jnp.broadcast_to(squares, (rows, LANES))
    for copy in head_copies:
        copy.wait()


def first_prep(hidden, gain, head, kinds):
    rows, feats, count = hidden.shape[0] // 4, hidden.shape[1], len(kinds)
    hbm = pl.BlockSpec(memory_space=pltpu.HBM)
    outs = pl.pallas_call(
        functools.partial(first_kernel, kinds, rows),
        in_specs=[hbm, hbm, hbm],
        out_shape=[jax.ShapeDtypeStruct((2 * rows, feats), bf16)] * count
        + [jax.ShapeDtypeStruct((rows, LANES), f32)] * count
        + [jax.ShapeDtypeStruct(head.shape, head.dtype)],
        scratch_shapes=[
            pltpu.VMEM((count, rows, feats), bf16),
            pltpu.VMEM(gain.shape, bf16),
            pltpu.SemaphoreType.DMA((count,)),
            pltpu.SemaphoreType.DMA,
            pltpu.SemaphoreType.DMA((HEAD_COPIES,)),
        ],
        compiler_params=params(),
        cost_estimate=pl.CostEstimate(
            flops=8 * count * rows * feats, bytes_accessed=2 * head.size, transcendentals=0
        ),
        name="first_prep",
    )(hidden, gain, head)
    return outs[:count], outs[count : 2 * count], outs[2 * count]


def encode_kernel(count, both_ref, *refs):
    square_refs, outs = refs[:count], refs[count:]
    rows, cols = both_ref.shape[0] // count // 2, both_ref.shape[1]
    for place, out_ref in enumerate(outs):
        powers = []
        for first in range(0, cols, CODE):
            both = both_ref[pl.ds(2 * place * rows, 2 * rows), pl.ds(first, CODE)]
            powers.append(put_codes(out_ref, both, first))
        put_extra(out_ref, powers, square_refs[place][:, :1])


def encode_parts(both, squares):
    count = len(squares)
    rows, cols = both.shape[0] // count // 2, both.shape[1]
    return pl.pallas_call(
        functools.partial(encode_kernel, count),
        out_shape=[jax.ShapeDtypeStruct((cols // LANES * rows + EXTRA, LANES), i16)] * count,
        compiler_params=params(),
        cost_estimate=pl.CostEstimate(
            flops=20 * count * rows * cols, bytes_accessed=10 * count * rows * cols, transcendentals=count * rows * cols
        ),
        name="encode_parts",
    )(both, *squares)


def product(left, head):
    return jnp.dot(left, head, preferred_element_type=f32)


def side_kernel(width, blocks, lists_ref, token_ref, hidden_ref, gain_ref, w_ref, head_ref, near_ref, own_ref, far_ref, left_ref, squares_ref, head_out, held, gain_held, w_held, sum_ref, meta_ref, sem, gain_sem, w_sems, head_sem, meta_sem):
    rows = token_ref.shape[1]
    slots = w_ref.shape[0]
    meta_copy = pltpu.make_async_copy(lists_ref, meta_ref, meta_sem)
    meta_copy.start()
    quarter = 2 * lax.axis_index("mp") + lax.axis_index("rows")
    at = pl.ds(pl.multiple_of(quarter * rows, rows), rows)
    hidden_copy = pltpu.make_async_copy(hidden_ref.at[at, :], held, sem)
    gain_copy = pltpu.make_async_copy(gain_ref, gain_held, gain_sem)
    w_copies = [pltpu.make_async_copy(w_ref.at[k], w_held.at[k], w_sems.at[k]) for k in range(slots)]
    gain_copy.start()
    hidden_copy.start()
    for copy in w_copies:
        copy.start()
    head_copy = pltpu.make_async_copy(head_ref, head_out, head_sem)
    head_copy.start()
    shard = lax.axis_index("vocab")
    near_at = jnp.where(shard % 2 == 0, 2, 0)
    token = jnp.transpose(jnp.broadcast_to(token_ref[...].astype(f32), (8, rows)))[:, :1].astype(i32)
    place = lax.broadcasted_iota(i32, (rows, width), 1)
    sum_ref[...] = jnp.zeros_like(sum_ref)
    gain_copy.wait()
    hidden_copy.wait()
    squares = prepare(held[...], gain_held[...].astype(f32), left_ref, 0)
    squares_ref[...] = jnp.broadcast_to(squares, (rows, LANES))
    meta_copy.wait()
    for slot in range(slots):
        w_copies[slot].wait()

        @pl.when(slot < meta_ref[2 * slots])
        def _():
            source = jnp.clip(meta_ref[slot] - (shard - 1) * blocks, 0, 3 * blocks - 1)
            hits = (token - meta_ref[slots + slot] * width == place).astype(bf16)
            left = jnp.concatenate([hits, jnp.ones((EXTRA, width), bf16)], axis=0)
            found = lax.dot_general(
                left, w_held[slot], (((1,), (1,)), ((), ())), preferred_element_type=f32
            )
            at = pl.ds(pl.multiple_of(source % blocks * width, width), width)
            sum_ref[source // blocks, :, at] += found

    order = lax.broadcasted_iota(i32, (EXTRA, 1), 0)
    for out_ref, k in ((near_ref, near_at), (own_ref, 1), (far_ref, 2 - near_at)):
        out_ref[pl.ds(0, rows), :] = sum_ref[k, pl.ds(0, rows), :].astype(bf16)
        sums = sum_ref[k, pl.ds(rows, EXTRA), :]
        first = sums.astype(bf16).astype(f32)
        second = (sums - first).astype(bf16).astype(f32)
        third = sums - first - second
        parts = jnp.where(order == 0, first, jnp.where(order == 1, second, jnp.where(order == 2, third, 0.0)))
        out_ref[pl.ds(rows, EXTRA), :] = parts.astype(bf16)
    near_ref[pl.ds(rows + EXTRA, EXTRA), :] = jnp.zeros((EXTRA, near_ref.shape[1]), bf16)
    head_copy.wait()


def side_parts(lists, token, hidden, gain, weights, head, width):
    rows, feats, cols = token.shape[1], hidden.shape[1], head.shape[1]
    hbm = pl.BlockSpec(memory_space=pltpu.HBM)
    outs = pl.pallas_call(
        functools.partial(side_kernel, width, cols // width),
        in_specs=[pl.BlockSpec(memory_space=pl.ANY), pl.BlockSpec(memory_space=pltpu.VMEM), hbm, hbm, hbm, hbm],
        out_shape=[jax.ShapeDtypeStruct((rows + many * EXTRA, cols), bf16) for many in (2, 1, 1)]
        + [jax.ShapeDtypeStruct((2 * rows, feats), bf16), jax.ShapeDtypeStruct((rows, LANES), f32)]
        + [jax.ShapeDtypeStruct(head.shape, head.dtype)],
        scratch_shapes=[
            pltpu.VMEM((rows, feats), bf16),
            pltpu.VMEM(gain.shape, bf16),
            pltpu.VMEM(weights.shape, bf16),
            pltpu.VMEM((3, rows + EXTRA, cols), f32),
            pltpu.SMEM(lists.shape, i32),
            pltpu.SemaphoreType.DMA,
            pltpu.SemaphoreType.DMA,
            pltpu.SemaphoreType.DMA((weights.shape[0],)),
            pltpu.SemaphoreType.DMA,
            pltpu.SemaphoreType.DMA,
        ],
        compiler_params=params(),
        cost_estimate=pl.CostEstimate(flops=1, bytes_accessed=1, transcendentals=0),
        name="side_parts",
    )(lists, token, hidden, gain, weights, head)
    return outs[:3], outs[3], outs[4], outs[5]


def extras(ref, rows):
    tile = ref[pl.ds(ref.shape[0] - EXTRA, EXTRA), :].astype(i32).astype(f32)
    wide = jnp.transpose(tile)
    groups = (ref.shape[0] - EXTRA) // rows * LANES // CODE
    at = [wide[:, j : j + 1] for j in range(groups + 3)]
    return at[:groups], decode_scalar(*at[groups:])


def model_logits(mine, features, own_ref, squares_ref, cy_ref, cx_ref, cd_ref, out_ref, peak_ref=None):
    rows = squares_ref.shape[0]
    cols = own_ref.shape[1]

    def run(scale, at_slab):
        peak = jnp.full((rows, LANES), -jnp.inf, f32)
        for slab in range(cols // LANES):
            logits = at_slab(slab) * scale
            out_ref[:, pl.ds(slab * LANES, LANES)] = logits
            peak = jnp.maximum(peak, logits)
        if peak_ref is not None:
            peak_ref[...] = peak

    @pl.when(mine)
    def _():
        power_y, squares_y = extras(cy_ref, rows)

        def at_slab(slab):
            at = pl.ds(slab * LANES, LANES)
            own = own_ref[pl.ds(0, rows), at] + own_ref[pl.ds(rows, rows), at]
            return own + decode(cy_ref[pl.ds(slab * rows, rows), :], power_y[slab * LANES // CODE])

        run(lax.rsqrt((squares_ref[:, :1] + squares_y) / features + 1e-05), at_slab)

    @pl.when(jnp.logical_not(mine))
    def _():
        power_x, squares_x = extras(cx_ref, rows)
        power_d, squares_d = extras(cd_ref, rows)

        def at_slab(slab):
            part, group = pl.ds(slab * rows, rows), slab * LANES // CODE
            return decode(cx_ref[part, :], power_x[group]) + decode(cd_ref[part, :], power_d[group])

        run(lax.rsqrt((squares_x + squares_d) / features + 1e-05), at_slab)

    if peak_ref is not None:
        return jnp.max(peak_ref[...], axis=1, keepdims=True)
    peak = jnp.full((rows, LANES), -jnp.inf, f32)
    for slab in range(cols // LANES):
        peak = jnp.maximum(peak, out_ref[:, pl.ds(slab * LANES, LANES)])
    return jnp.max(peak, axis=1, keepdims=True)


def qwen_kernel(width, blocks, features, own_ref, squares_ref, cy_ref, cx_ref, cd_ref, u_ref, stats_ref, q_ref, peak_ref):
    rows = squares_ref.shape[0]
    body = blocks * width
    peak = model_logits(lax.axis_index("mp") == 1, features, own_ref, squares_ref, cy_ref, cx_ref, cd_ref, q_ref, peak_ref)
    total = jnp.zeros((rows, 1), f32)
    for j in range(blocks):
        at = pl.ds(j * width, width)
        qwen = jnp.exp(q_ref[:, at] - peak)
        held = qwen.astype(bf16)
        for k in range(width // LANES):
            slab = j * (width // LANES) + k
            u_ref[pl.ds(slab * rows, rows), :] = held[:, k * LANES : (k + 1) * LANES]
        total += jnp.sum(qwen, axis=1, keepdims=True)
    first = peak.astype(bf16).astype(f32)
    second = (peak - first).astype(bf16).astype(f32)
    third = peak - first - second
    parts = jnp.transpose(columns_to_lanes([first, second, third], rows))[:EXTRA]
    u_ref[pl.ds(body // LANES * rows, EXTRA), :] = parts.astype(bf16)
    stats_ref[...] = columns_to_lanes([peak, total], rows)


def join_qwen(own, squares, codes, width, features):
    rows, cols = own.shape[0] // 2, own.shape[1]
    whole = pl.BlockSpec(memory_space=pltpu.VMEM)
    return pl.pallas_call(
        functools.partial(qwen_kernel, width, cols // width, features),
        in_specs=[whole] * 5,
        out_shape=[
            jax.ShapeDtypeStruct((cols // LANES * rows + EXTRA, LANES), bf16),
            jax.ShapeDtypeStruct((rows, LANES), f32),
        ],
        scratch_shapes=[pltpu.VMEM((rows, cols), f32), pltpu.VMEM((rows, LANES), f32)],
        compiler_params=params(),
        cost_estimate=pl.CostEstimate(flops=20000000000, bytes_accessed=8 * 1024 * 1024, transcendentals=0),
        name="join_qwen",
    )(own, squares, *codes)


def llama_kernel(width, blocks, features, own_ref, squares_ref, cy_ref, cx_ref, cd_ref, token_ref, u_ref, near_ref, mine_ref, far_ref, before_ref, e_ref, stats_ref):
    rows = squares_ref.shape[0]
    body = blocks * width
    columns_refs = (near_ref, mine_ref, far_ref)
    peak = model_logits(lax.axis_index("mp") == 0, features, own_ref, squares_ref, cy_ref, cx_ref, cd_ref, e_ref)
    total = jnp.zeros((rows, 1), f32)
    mass = jnp.zeros((rows, 1), f32)
    pick_e = jnp.zeros((rows, 1), f32)
    pick_m = jnp.zeros((rows, 1), f32)
    token = jnp.transpose(jnp.broadcast_to(token_ref[...].astype(f32), (8, rows)))
    token = token[:, :1].astype(i32) - lax.axis_index("vocab") * body
    for j in range(blocks):
        at = pl.ds(j * width, width)
        llama = jnp.exp(e_ref[:, at] - peak)
        e_ref[:, at] = llama
        total += jnp.sum(llama, axis=1, keepdims=True)
        hit = lax.broadcasted_iota(i32, (rows, width), 1) + j * width == token
        pick_e += jnp.sum(jnp.where(hit, llama, 0.0), axis=1, keepdims=True)
        slabs = range(j * (width // LANES), (j + 1) * (width // LANES))
        held = jnp.concatenate([u_ref[pl.ds(slab * rows, rows), :] for slab in slabs], axis=1).astype(f32)
        columns = functools.reduce(jnp.add, [ref[pl.ds(0, rows), at].astype(f32) for ref in columns_refs])
        pick_m += jnp.sum(held * columns, axis=1, keepdims=True)
        sums = functools.reduce(jnp.add, [ref[pl.ds(rows, EXTRA), at].astype(f32) for ref in columns_refs])
        mass += jnp.sum(held * jnp.sum(sums, axis=0, keepdims=True), axis=1, keepdims=True)
    before = before_ref[...]
    stats = columns_to_lanes([peak, total, before[:, 0:1], before[:, 1:2], mass, pick_e, pick_m], rows)
    stats_ref[...] = jnp.transpose(stats)[:8]


def join_llama(own, squares, codes, token, u, columns, stats, width, features):
    rows, cols = own.shape[0] // 2, own.shape[1]
    whole = pl.BlockSpec(memory_space=pltpu.VMEM)
    return pl.pallas_call(
        functools.partial(llama_kernel, width, cols // width, features),
        in_specs=[whole] * 11,
        out_shape=[jax.ShapeDtypeStruct((rows, cols), f32), jax.ShapeDtypeStruct((8, rows), f32)],
        compiler_params=params(),
        cost_estimate=pl.CostEstimate(flops=20000000000, bytes_accessed=8 * 1024 * 1024, transcendentals=0),
        name="join_llama",
    )(own, squares, *codes, token, u, *columns, stats)


def map_kernel(width, blocks, shards, lists_ref, u_ref, near_ref, far_ref, w_ref, m_ref, top_ref, all_ref, scale_ref, meta_ref, meta_sem):
    rows = m_ref.shape[0]
    body = blocks * width
    meta_copy = pltpu.make_async_copy(lists_ref, meta_ref, meta_sem)
    meta_copy.start()
    shard = lax.axis_index("vocab")
    slots = w_ref.shape[0]
    near_at = jnp.where(shard % 2 == 0, 2, 0)

    def peak_of(ref):
        lanes = jnp.transpose(ref[pl.ds(body // LANES * rows, EXTRA), :].astype(f32))
        return lanes[:, 0:1] + lanes[:, 1:2] + lanes[:, 2:3]

    own_peak = peak_of(u_ref)
    near_peak = peak_of(near_ref)
    far_peak = jnp.where((shard > 0) & (shard < shards - 1), peak_of(far_ref), own_peak)
    top = jnp.maximum(jnp.maximum(near_peak, far_peak), own_peak)
    for k, ref, peak in ((near_at, near_ref, near_peak), (1, u_ref, own_peak), (2 - near_at, far_ref, far_peak)):
        for slab in range(body // LANES):
            all_ref[k, :, pl.ds(slab * LANES, LANES)] = ref[pl.ds(slab * rows, rows), :]
        scale_ref[k] = jnp.broadcast_to(jnp.exp(peak - top), (rows, LANES))
    m_ref[...] = jnp.zeros_like(m_ref)
    meta_copy.wait()
    for slot in range(slots):

        @pl.when(slot < meta_ref[2 * slots])
        def _():
            source = jnp.clip(meta_ref[slot] - (shard - 1) * blocks, 0, 3 * blocks - 1)
            target = jnp.clip(meta_ref[slots + slot] - shard * blocks, 0, blocks - 1)
            inside = pl.multiple_of(source % blocks * width, width)
            picked = all_ref[source // blocks, :, pl.ds(inside, width)]
            term = jnp.dot(picked, w_ref[slot], preferred_element_type=f32)
            at = pl.ds(pl.multiple_of(target * width, width), width)
            m_ref[:, at] += term * scale_ref[source // blocks][:, :1]

    top_ref[...] = jnp.broadcast_to(top, (rows, LANES))


def map_parts(lists, u, near, far, weights, width, shards, rows):
    cols = (u.shape[0] - EXTRA) // rows * LANES
    blocks = cols // width
    whole = pl.BlockSpec(memory_space=pltpu.VMEM)
    return pl.pallas_call(
        functools.partial(map_kernel, width, blocks, shards),
        in_specs=[pl.BlockSpec(memory_space=pl.ANY)] + [whole] * 4,
        out_shape=[jax.ShapeDtypeStruct((rows, cols), f32), jax.ShapeDtypeStruct((rows, LANES), f32)],
        scratch_shapes=[pltpu.VMEM((3, rows, cols), bf16), pltpu.VMEM((3, rows, LANES), f32)]
        + [pltpu.SMEM(lists.shape, i32), pltpu.SemaphoreType.DMA],
        compiler_params=params(),
        cost_estimate=pl.CostEstimate(
            flops=2 * rows * weights.size, bytes_accessed=2 * weights.size, transcendentals=0
        ),
        name="map_parts",
    )(lists, u, near, far, weights)


def finish_kernel(pieces, *refs):
    stats_refs, (e_ref, m_ref, m_top_ref, out_ref, nll_ref) = refs[:pieces], refs[pieces:]
    stats = [ref[k : k + 8, :] for ref in stats_refs for k in range(0, ref.shape[0], 8)]
    shards = range(len(stats))
    row = lambda s, k: stats[s][k : k + 1, :]
    top_l = functools.reduce(jnp.maximum, [row(s, 0) for s in shards])
    top_q = functools.reduce(jnp.maximum, [row(s, 2) for s in shards])
    sum_l = functools.reduce(jnp.add, [row(s, 1) * jnp.exp(row(s, 0) - top_l) for s in shards])
    sum_q = functools.reduce(jnp.add, [row(s, 3) * jnp.exp(row(s, 2) - top_q) for s in shards])
    part_l = [jnp.exp(row(s, 0) - top_l) / sum_l for s in shards]
    part_q = [jnp.exp(row(s, 2) - top_q) / sum_q for s in shards]
    mass = functools.reduce(jnp.add, [row(s, 4) * part_q[s] for s in shards])
    pick_e = functools.reduce(jnp.add, [row(s, 5) * part_l[s] for s in shards])
    pick_m = functools.reduce(jnp.add, [row(s, 6) * part_q[s] for s in shards])
    log_norm = jnp.log1p(mass)
    nll_ref[...] = log_norm - jnp.log(jnp.maximum(pick_e, FLOOR) + pick_m)
    tile = jnp.concatenate([part_l[0], top_q, 1.0 / sum_q, log_norm, jnp.zeros((4, log_norm.shape[1]), f32)], axis=0)
    turned = jnp.transpose(tile)
    a, top, share, c = (turned[:, i : i + 1] for i in range(4))
    b = jnp.exp(m_top_ref[:, :1] - top) * share
    out_ref[...] = jnp.log(jnp.maximum(e_ref[...] * a, FLOOR) + m_ref[...] * b) - c


def finish(pieces, e, m, m_top):
    rows, cols = e.shape
    return pl.pallas_call(
        functools.partial(finish_kernel, len(pieces)),
        out_shape=[
            jax.ShapeDtypeStruct((rows, cols), f32),
            jax.ShapeDtypeStruct((1, rows), f32),
        ],
        compiler_params=params(),
        cost_estimate=pl.CostEstimate(
            flops=20 * rows * cols, bytes_accessed=12 * rows * cols, transcendentals=2 * rows * cols
        ),
        name="finish",
    )(*pieces, e, m, m_top)


def gather_pieces(own, shards):
    pieces, step = [own], 1
    while step < shards:
        radix = 4 if step > 1 and 4 * step <= shards else 2
        sent = pieces[0] if len(pieces) == 1 else jnp.concatenate(pieces, axis=0)
        for turn in range(1, radix):
            pieces.append(lax.ppermute(sent, "vocab", [(i, i ^ (turn * step)) for i in range(shards)]))
        step *= radix
    return pieces, sent


def on_device(
    hidden, norm_gain, head_weights, pair_source, pair_target, pair_count, pair_weight, next_token
):
    shards = lax.axis_size("vocab")
    row_groups = lax.axis_size("rows")
    hidden, head = hidden[0], head_weights[0]
    token = next_token[None, :]
    held_hidden = pltpu.with_memory_space_constraint(hidden, pltpu.HBM)
    held_weight = pltpu.with_memory_space_constraint(pair_weight, pltpu.HBM)
    held_gain = pltpu.with_memory_space_constraint(norm_gain, pltpu.HBM)
    held_head = pltpu.with_memory_space_constraint(head, pltpu.HBM)
    width = pair_weight.shape[1]
    features = hidden.shape[1] * row_groups
    lists = jnp.concatenate([pair_source, pair_target, pair_count])

    inside = [(i, i ^ 1) for i in range(shards)]
    across = [(i, i + 1 if i % 2 else i - 1) for i in range(1, shards - 1)]
    lefts, squares, head = first_prep(held_hidden, held_gain, held_head, (3, 1, 2))
    (to_d,) = encode_parts(product(lefts[0], head), squares[:1])
    from_d = lax.ppermute(to_d, ("mp", "rows"), [(0, 3), (1, 2), (2, 1), (3, 0)])
    left_y, _ = lax.optimization_barrier((lefts[1], to_d))
    (to_y,) = encode_parts(product(left_y, head), squares[1:2])
    from_y = lax.ppermute(to_y, "rows", [(0, 1), (1, 0)])
    left_x, _ = lax.optimization_barrier((lefts[2], to_y))
    (to_x,) = encode_parts(product(left_x, head), squares[2:])
    from_x = lax.ppermute(to_x, "mp", [(0, 1), (1, 0)])
    early, _ = lax.optimization_barrier((lists, to_x))
    (to_near, columns, to_far), left_own, squares_own, head = side_parts(
        early, token, held_hidden, held_gain, held_weight, held_head, width
    )
    own = product(left_own, head)
    to_near, _ = lax.optimization_barrier((to_near, own))
    near_columns = lax.ppermute(to_near, "vocab", inside)
    far_columns = lax.ppermute(to_far, "vocab", across)

    codes = (from_y, from_x, from_d)
    u, stats = join_qwen(own, squares_own, codes, width, features)
    far = lax.ppermute(u, "vocab", across)
    e, stats = join_llama(
        own, squares_own, codes, token, u, (near_columns, columns, far_columns), stats, width, features
    )
    pieces, last = gather_pieces(stats, shards)
    late_u, _ = lax.optimization_barrier((u, last))
    near = lax.ppermute(late_u, "vocab", inside)
    m, m_top = map_parts(lists, u, near, far, pair_weight, width, shards, e.shape[0])
    out, nll = finish(pieces, e, m, m_top)
    return out, nll[0]


def solution(mesh):
    in_specs = (
        P("mp", None, "rows"),
        P("mp", "rows"),
        P("mp", "rows", "vocab"),
        P("vocab"),
        P("vocab"),
        P("vocab"),
        P("vocab", None, None),
        P(("mp", "rows")),
    )
    out_specs = (P(("mp", "rows"), "vocab"), P(("mp", "rows")))
    return jax.shard_map(
        on_device, mesh=mesh, in_specs=in_specs, out_specs=out_specs, check_vma=False
    )
```
